32 devices in a mesh: dp: 8 (over y, x, core), head: 4 (over z).
Axes of the slice: x: 2, y: 2, z: 4, core: 2. Of those that a mesh axis runs over, the one named last changes fastest.
Arguments:
- image_tokens: bfloat16 [96, 196, 768], P(('dp', 'head')), may hold values from -6 to 6
- cotangent: bfloat16 [96, 196, 768], P(('dp', 'head')), may hold values from -6 to 6
- weights: float32 [24, 768, 768], P('head', 'dp'), may hold values from -4 to 4
- weights_ema: float32 [24, 768, 768], P('head', 'dp'), may hold values from -0.21875 to 0.21875
- left_stats: float32 [24, 768, 768], P('head', 'dp'), may hold values from -28901376 to 28901376
- right_stats: float32 [24, 768, 768], P('head', 'dp'), may hold values from -28901376 to 28901376
- left_root: float32 [24, 768, 768], P('head', 'dp'), may hold values from -1 to 8
- right_root: float32 [24, 768, 768], P('head', 'dp'), may hold values from -1 to 8
- vectors: float32 [2, 4736], replicated, may hold values from -2 to 3
- vec_first: float32 [2, 4736], replicated, may hold values from -18816 to 18816
- vec_second: float32 [2, 4736], replicated, may hold values from 0 to 18816
Outputs:
- block_out: bfloat16 [96, 196, 768], P(('dp', 'head'))
- input_grad: float32 [96, 196, 768], P(('dp', 'head'))
- weight_grad: float32 [24, 768, 768], P('head', 'dp')
- left_new: float32 [24, 768, 768], P('head', 'dp')
- right_new: float32 [24, 768, 768], P('head', 'dp')
- weight_new: float32 [24, 768, 768], P('head', 'dp')
- ema_new: float32 [24, 768, 768], P('head', 'dp')
- vec_first_new: float32 [2, 4736], replicated
- vec_second_new: float32 [2, 4736], replicated
- vec_new: float32 [2, 4736], replicated
The draws below stay inside these ranges and needn't reach their ends.
All inputs are finite; a program needn't handle non-finite values.
Results may differ from the reference program's by a relative error of at most 0.014.
Values may be sent and summed in bfloat16 or wider, within the bound.
No kernel may reach another device: no remote copies, remote signals or barrier semaphores. Data moves between devices by JAX's collectives and lax.ppermute only.
A program may use at most 384 MiB of HBM per device.

```python
import jax
import jax.numpy as jnp
from jax import lax

D = 768
HEADS = 12
HEAD_DIM = 64
FF = 3072
SEQ = 196
IMAGES_DP = 12
LAYERS = 2
STEP = 10
IMAGES = 96
BLOCKS = 24
VEC = 4736


def bounded(key, shape):
    return jax.random.truncated_normal(key, -4.0, 4.0, shape, jnp.float32)


def symmetric(key, shape):
    first = bounded(key, shape)
    return (first + jnp.swapaxes(first, 1, 2)) * 0.7071


def dominant(key, size_scale, off_scale):
    diagonal = jax.random.uniform(jax.random.fold_in(key, 1), (BLOCKS, D), jnp.float32, 1.0, 4.0)
    off_part = symmetric(jax.random.fold_in(key, 2), (BLOCKS, D, D)) * off_scale
    identity = jnp.eye(D, dtype=jnp.float32)
    return size_scale * (off_part + identity[None] * diagonal[:, :, None])


def grad_size():
    column = jnp.arange(VEC)
    in_bias = (column >= D + 2 * HEAD_DIM) & (column < D + 2 * HEAD_DIM + FF)
    return jnp.where(in_bias, 0.5, 1.0) * float(IMAGES * SEQ) ** 0.5


def draw_weights(key, part):
    key = jax.random.fold_in(key, 11)
    per_layer = 4 + 2 * (FF // D)
    slot = jnp.arange(BLOCKS) % per_layer
    factor = jnp.where(slot < 3 + FF // D, D ** (-0.5), FF ** (-0.5))
    factor = jnp.where(slot == 3 + FF // D, 4.0 * D ** (-0.5), factor)
    return bounded(key, (BLOCKS, D, D)) * factor[:, None, None]


def draw_left_stats(key, part):
    key = jax.random.fold_in(key, 13)
    return dominant(key, 0.3 * D * IMAGES * SEQ, 0.5 * D ** (-0.5))


def draw_right_stats(key, part):
    key = jax.random.fold_in(key, 17)
    return dominant(key, 0.3 * D * IMAGES * SEQ, 0.5 * D ** (-0.5))


def draw_left_root(key, part):
    key = jax.random.fold_in(key, 19)
    return dominant(key, (0.1 * IMAGES * SEQ) ** (-0.25), 0.7 * D ** (-0.5))


def draw_right_root(key, part):
    key = jax.random.fold_in(key, 23)
    return dominant(key, (0.1 * IMAGES * SEQ) ** (-0.25), 0.7 * D ** (-0.5))


def draw_vectors(key, part):
    key = jax.random.fold_in(key, 29)
    noise = bounded(key, (LAYERS, VEC))
    column = jnp.arange(VEC)
    is_gain = column < D + 2 * HEAD_DIM
    return jnp.where(is_gain[None], jnp.exp(0.2 * noise), 0.3 * noise)


def draw_vec_first(key, part):
    key = jax.random.fold_in(key, 31)
    return bounded(key, (LAYERS, VEC)) * 0.11 * grad_size()[None]


def draw_vec_second(key, part):
    key = jax.random.fold_in(key, 37)
    factor = jax.random.uniform(key, (LAYERS, VEC), jnp.float32, 1.0, 4.0)
    sizes = grad_size()
    return factor * 0.0526 * (sizes * sizes)[None]


def steps_of(stream_key, extent, shards, low, largest):
    loudness, own = 1.0, jax.random.fold_in(stream_key, 6)
    for axis_at, blocks in shards:
        steps = jnp.exp(jax.random.uniform(jax.random.fold_in(own, axis_at), (blocks,), jnp.float32, low / len(shards), largest / len(shards)))
        loudness = loudness * jnp.repeat(steps, extent[axis_at] // blocks).reshape([-1 if axis == axis_at else 1 for axis in range(len(extent))])
    return loudness


def scatter_about(rng, shape, scale, bound, split=(), kind=jnp.bfloat16):
    drawn = scale * jax.random.normal(rng, shape, jnp.float32)
    if split:
        drawn = drawn * steps_of(rng, shape, split, -0.22, 0.18)
    return jnp.clip(drawn, -bound, bound).astype(kind)


def setup_inputs(seed: int = 0) -> dict:
    key_list = jax.random.split(jax.random.key(seed), 12)
    return {
        "image_tokens": scatter_about(key_list[0], (IMAGES, SEQ, D), 1.0, 6.0, ((0, 32),)),
        "cotangent": scatter_about(key_list[1], (IMAGES, SEQ, D), 1.0, 6.0, ((0, 32),)),
        "weights": draw_weights(jax.random.fold_in(key_list[11], 71), 0),
        "weights_ema": scatter_about(key_list[3], (BLOCKS, D, D), D ** -0.5, 0.21875, ((0, 4), (1, 8)), jnp.float32),
        "left_stats": draw_left_stats(jax.random.fold_in(key_list[11], 71), 0),
        "right_stats": draw_right_stats(jax.random.fold_in(key_list[11], 71), 0),
        "left_root": draw_left_root(jax.random.fold_in(key_list[11], 71), 0),
        "right_root": draw_right_root(jax.random.fold_in(key_list[11], 71), 0),
        "vectors": draw_vectors(jax.random.fold_in(key_list[11], 71), 0),
        "vec_first": draw_vec_first(jax.random.fold_in(key_list[11], 71), 0),
        "vec_second": draw_vec_second(jax.random.fold_in(key_list[11], 71), 0),
    }


@jax.custom_vjp
def low(v):
    return lax.optimization_barrier(v.astype(jnp.bfloat16)).astype(jnp.float32)

@jax.custom_vjp
def low_back(v):
    return v

def low_keep(v):
    return (low(v), None)

def low_pass(kept, grad):
    return (grad,)

def back_keep(v):
    return (v, None)

def back_low(kept, grad):
    return (low(grad),)
low.defvjp(low_keep, low_pass)
low_back.defvjp(back_keep, back_low)
PRECISE = lax.Precision.HIGHEST
EPS_NORM = 1e-06
BETA_ONE = 0.9
BETA_TWO = 0.95
ADAM_EPS = 1e-08
RATE_VEC = 0.3
RATE_MAT = 0.003
DECAY_MAT = 0.1
STAT_DECAY = 0.5
EMA_DECAY = 0.8

def layer_norm(values, gain_vec):
    average = lax.optimization_barrier(jnp.mean(values, axis=-1, keepdims=True))
    centred = values - average
    spread = lax.optimization_barrier(jnp.mean(centred * centred, axis=-1, keepdims=True))
    return centred * lax.rsqrt(spread + EPS_NORM) * gain_vec

def gelu_exact(values):
    return jax.nn.gelu(values, approximate=False)

def split_vector(row_vec):
    ln_gain = row_vec[:D]
    q_gain = row_vec[D:D + HEAD_DIM]
    k_gain = row_vec[D + HEAD_DIM:D + 2 * HEAD_DIM]
    mlp_bias = row_vec[D + 2 * HEAD_DIM:D + 2 * HEAD_DIM + FF]
    out_bias = row_vec[D + 2 * HEAD_DIM + FF:]
    return (ln_gain, q_gain, k_gain, mlp_bias, out_bias)

def forward(tokens, blocks, vectors):
    image_count = tokens.shape[0]
    mlp_ratio = FF // D
    per_layer = 4 + 2 * mlp_ratio
    in_count = 3 + mlp_ratio
    score_scale = HEAD_DIM ** (-0.5)
    stream = tokens
    for depth in range(LAYERS):
        in_blocks = blocks[depth * per_layer:depth * per_layer + in_count]
        out_blocks = blocks[depth * per_layer + in_count:(depth + 1) * per_layer]
        ln_gain, q_gain, k_gain, mlp_bias, out_bias = split_vector(vectors[depth])
        normed = low(layer_norm(stream, ln_gain))
        mixed_all = jnp.einsum('isk,bkn->isbn', normed, in_blocks, precision=PRECISE)
        queries = low_back(mixed_all[:, :, 0]).reshape(image_count, SEQ, HEADS, HEAD_DIM)
        key_vecs = low_back(mixed_all[:, :, 1]).reshape(image_count, SEQ, HEADS, HEAD_DIM)
        queries = low_back(low(layer_norm(queries, q_gain)))
        key_vecs = low_back(low(layer_norm(key_vecs, k_gain)))
        value_vecs = low_back(low(mixed_all[:, :, 2])).reshape(image_count, SEQ, HEADS, HEAD_DIM)
        pre_act = low_back(mixed_all[:, :, 3:].reshape(image_count, SEQ, FF) + mlp_bias)
        hidden = low(gelu_exact(pre_act))
        scores = low_back(jnp.einsum('ishd,ijhd->ihsj', queries, key_vecs, precision=PRECISE) * score_scale)
        soft_probs = low(jax.nn.softmax(scores, axis=-1))
        attended = jnp.einsum('ihsj,ijhd->ishd', soft_probs, value_vecs, precision=PRECISE).reshape(image_count, SEQ, D)
        attended = low_back(low(attended))
        joined = jnp.concatenate([attended[:, :, None], hidden.reshape(image_count, SEQ, mlp_ratio, D)], axis=2)
        branch = jnp.einsum('isbk,bkn->isn', joined, out_blocks, precision=PRECISE) + out_bias
        stream = stream + low_back(branch)
    return stream

def reference(image_tokens, cotangent, weights, weights_ema, left_stats, right_stats, left_root, right_root, vectors, vec_first, vec_second):
    rounded = low(weights)
    groups = IMAGES // IMAGES_DP
    tokens = image_tokens.astype(jnp.float32).reshape(groups, IMAGES_DP, SEQ, D)
    grads_in = cotangent.astype(jnp.float32).reshape(groups, IMAGES_DP, SEQ, D)

    def one_group(carry, pair):
        block_sum, vector_sum = carry
        group_tokens, group_cot = pair
        result, pull = jax.vjp(forward, group_tokens, rounded, vectors)
        token_grad, block_grad, vector_grad = pull(group_cot)
        return ((block_sum + block_grad, vector_sum + vector_grad), (result.astype(jnp.bfloat16), token_grad))
    start = (jnp.zeros_like(weights), jnp.zeros_like(vectors))
    (weight_grad, vector_grad), (outputs, token_grads) = lax.scan(one_group, start, (tokens, grads_in))
    gram_left = jnp.einsum('bik,bjk->bij', weight_grad, weight_grad, precision=PRECISE)
    gram_right = jnp.einsum('bki,bkj->bij', weight_grad, weight_grad, precision=PRECISE)
    left_new = STAT_DECAY * left_stats + (1.0 - STAT_DECAY) * gram_left
    right_new = STAT_DECAY * right_stats + (1.0 - STAT_DECAY) * gram_right
    lifted = jnp.einsum('bik,bkj->bij', left_root, weight_grad, precision=PRECISE)
    precond = jnp.einsum('bik,bkj->bij', lifted, right_root, precision=PRECISE)
    weight_new = weights * (1.0 - RATE_MAT * DECAY_MAT) - RATE_MAT * precond
    ema_new = EMA_DECAY * weights_ema + (1.0 - EMA_DECAY) * weight_new
    first_new = BETA_ONE * vec_first + (1.0 - BETA_ONE) * vector_grad
    second_new = BETA_TWO * vec_second + (1.0 - BETA_TWO) * vector_grad * vector_grad
    first_hat = first_new / (1.0 - BETA_ONE ** STEP)
    second_hat = second_new / (1.0 - BETA_TWO ** STEP)
    vec_new = vectors - RATE_VEC * first_hat / (jnp.sqrt(second_hat) + ADAM_EPS)
    return (outputs.reshape(IMAGES, SEQ, D), token_grads.reshape(IMAGES, SEQ, D), weight_grad, left_new, right_new, weight_new, ema_new, first_new, second_new, vec_new)
```

```python
import functools
import math

import jax
import jax.numpy as jnp
from jax import lax
from jax.experimental import pallas as pl
from jax.experimental.pallas import tpu as pltpu
from jax.sharding import PartitionSpec as P

D = 768
HEADS = 12
HEAD_DIM = 64
FF = 3072
SEQ = 196
PAD = 208
LAYERS = 2
STEP = 10
RATIO = FF // D
IN_COUNT = 3 + RATIO
OUT_COUNT = 1 + RATIO
PER_LAYER = IN_COUNT + OUT_COUNT
PAIR = 2 * HEAD_DIM
TILE = 256

EPS_NORM = 1e-06
BETA_ONE = 0.9
BETA_TWO = 0.95
ADAM_EPS = 1e-08
RATE_VEC = 0.3
RATE_MAT = 0.003
DECAY_MAT = 0.1
STAT_DECAY = 0.5
EMA_DECAY = 0.8
SCALE = HEAD_DIM ** (-0.5)
EXP2_SCALE = SCALE * math.log2(math.e)

BF = jnp.bfloat16
F32 = jnp.float32
NN = (((1,), (0,)), ((), ()))
NT = (((1,), (1,)), ((), ()))
TN = (((0,), (0,)), ((), ()))


def dot(a, b, dims=NN):
    return lax.dot_general(a, b, dims, preferred_element_type=F32)


def call(kernel, grid, operands, in_specs, outs, out_specs, scratch, flops, name):
    moved = sum(o.size * o.dtype.itemsize for o in operands) + sum(
        math.prod(o.shape) * o.dtype.itemsize for o in outs
    )
    return pl.pallas_call(
        kernel,
        grid=grid,
        in_specs=in_specs,
        out_specs=out_specs,
        out_shape=outs,
        scratch_shapes=scratch,
        compiler_params=pltpu.CompilerParams(vmem_limit_bytes=56 * 1024 * 1024),
        cost_estimate=pl.CostEstimate(flops=flops, bytes_accessed=moved, transcendentals=0),
        name=name,
    )(*operands)


def whole(shape):
    return pl.BlockSpec(shape, lambda *ids: (0,) * len(shape))


def sds(shape, dtype):
    return jax.ShapeDtypeStruct(shape, dtype)


def block_total(units):
    return sum(count for _, _, count in units)


def piece_operands(units):
    arrays, specs, start = [], [], 0
    for pieces, first, count in units:
        for piece in pieces:
            arrays.append(piece)
            specs.append(
                pl.BlockSpec(
                    (1,) + piece.shape[1:],
                    functools.partial(
                        lambda at, first, count, j: (first + jnp.clip(j - at, 0, count - 1), 0, 0),
                        start,
                        first,
                        count,
                    ),
                )
            )
        start += count
    return arrays, specs


def read_block(j, units, refs, held, offsets):
    if len(units) == 1 and len(units[0][0]) == 1:
        return refs[0][0]
    start, at = 0, 0
    for pieces, _, count in units:
        mine = refs[at : at + len(pieces)]

        @pl.when((j >= start) & (j < start + count))
        def _(mine=mine):
            rows_at = offsets(len(mine))
            for ref, row in zip(mine, rows_at):
                rows = ref.shape[1]
                held[pl.ds(pl.multiple_of(row, 16), rows), :] = ref[0]

        start += count
        at += len(pieces)
    return held[...]


def piece_rows(count):
    if count == 1:
        return [0]
    me = lax.axis_index("dp")
    rows = D // count
    core, x, y = lax.rem(me, 2), lax.rem(me // 2, 2), me // 4
    return [
        ((y + dy - 2 * y * dy) * 4 + (x + dx - 2 * x * dx) * 2 + (core + dc - 2 * core * dc)) * rows
        for dy in (0, 1)
        for dx in (0, 1)
        for dc in (0, 1)
    ]


def row_parts(values):
    average = jnp.mean(values, axis=-1, keepdims=True)
    centred = values - average
    inverse = lax.rsqrt(jnp.mean(centred * centred, axis=-1, keepdims=True) + EPS_NORM)
    return centred * inverse, inverse


def head_mixer():
    row = lax.broadcasted_iota(jnp.int32, (TILE, TILE), 0) // HEAD_DIM
    column = lax.broadcasted_iota(jnp.int32, (TILE, TILE), 1) // HEAD_DIM
    return jnp.where(row == column, 1.0 / HEAD_DIM, 0.0).astype(BF)


def head_mean(values, mixer):
    high = values.astype(BF)
    low = (values - high.astype(F32)).astype(BF)
    return jnp.concatenate(
        [
            dot(high[:, at : at + TILE], mixer) + dot(low[:, at : at + TILE], mixer)
            for at in range(0, D, TILE)
        ],
        axis=1,
    )


def gelu_parts(z):
    decay = jnp.exp(-0.5 * z * z)
    t = 1.0 / (1.0 + 0.3275911 * math.sqrt(0.5) * jnp.abs(z))
    poly = t * (
        0.254829592
        + t * (-0.284496736 + t * (1.421413741 + t * (-1.453152027 + t * 1.061405429)))
    )
    tail = 0.5 * poly * decay
    share = jnp.where(z >= 0, 1.0 - tail, tail)
    return z * share, share + z * decay * (1.0 / math.sqrt(2.0 * math.pi))


def row_steps(total, size, body):
    def step(i, carry):
        body(pl.ds(pl.multiple_of(i * size, size), size))
        return carry

    lax.fori_loop(0, total // size, step, 0)


def mlp_in(stream, gain, bias, units):
    tokens = stream.shape[0]
    weights, w_specs = piece_operands(units)

    def kernel(x_ref, g_ref, b_ref, *refs):
        w_refs, (h_ref, a_ref, s_ref, held, wide) = refs[: len(weights)], refs[len(weights) :]
        j = pl.program_id(0)

        @pl.when(j == 0)
        def _():
            def body(rows):
                unit, _ = row_parts(x_ref[rows, :].astype(F32))
                h_ref[rows, :] = (unit * g_ref[...]).astype(BF)

            row_steps(tokens, 48, body)

        wide[...] = dot(h_ref[...], read_block(j, units, w_refs, held, piece_rows))

        def body(rows):
            act, slope = gelu_parts(wide[rows, :] + b_ref[...])
            a_ref[rows, :] = act.astype(BF)
            s_ref[rows, :] = slope.astype(BF)

        row_steps(tokens, 16, body)

    return call(
        kernel,
        (RATIO,),
        [stream, gain, bias] + weights,
        [whole((tokens, D)), whole((1, D)), pl.BlockSpec((1, D), lambda j: (0, j))] + w_specs,
        [sds((tokens, D), BF), sds((tokens, FF), BF), sds((tokens, FF), BF)],
        [whole((tokens, D))] + [pl.BlockSpec((tokens, D), lambda j: (0, j))] * 2,
        [pltpu.VMEM((D, D), BF), pltpu.VMEM((tokens, D), F32)],
        2 * tokens * D * FF,
        "mlp_in",
    )


def half_masks(rows):
    low = lax.broadcasted_iota(jnp.int32, (rows, PAIR), 1) < HEAD_DIM
    return low


def split_pair(values, low):
    zero = jnp.zeros_like(values)
    return jnp.where(low, values, zero), jnp.where(low, zero, values)


def attend(normed, q_gain, k_gain, units):
    tokens = normed.shape[0]
    images = tokens // PAD
    weights, w_specs = piece_operands(units)

    def kernel(h_ref, gq_ref, gk_ref, *refs):
        w_refs = refs[: len(weights)]
        q_ref, k_ref, v_ref, qu_ref, qi_ref, ku_ref, ki_ref, o_ref, held, wide = refs[len(weights) :]
        j = pl.program_id(0)
        wide[...] = dot(h_ref[...], read_block(j, units, w_refs, held, piece_rows))

        def normalise(g_ref, n_ref, u_ref, i_ref):
            mixer = head_mixer()

            def body(rows):
                raw = wide[rows, :]
                centred = raw - head_mean(raw, mixer)
                inverse = lax.rsqrt(head_mean(centred * centred, mixer) + EPS_NORM)
                unit = centred * inverse
                n_ref[rows, :] = (unit * g_ref[...]).astype(BF)
                u_ref[rows, :] = unit.astype(BF)
                i_ref[rows, :] = inverse

            row_steps(tokens, 208, body)

        @pl.when(j == 0)
        def _():
            normalise(gq_ref, q_ref, qu_ref, qi_ref)

        @pl.when(j == 1)
        def _():
            normalise(gk_ref, k_ref, ku_ref, ki_ref)

        @pl.when(j == 2)
        def _():
            v_ref[...] = wide[...].astype(BF)
            low = half_masks(PAD)
            valid = lax.broadcasted_iota(jnp.int32, (PAD, PAD), 1) < SEQ

            def body(pair, carry):
                lanes = pl.ds(pl.multiple_of(pair * PAIR, PAIR), PAIR)
                for image in range(images):
                    rows = pl.ds(image * PAD, PAD)
                    keys, values = k_ref[rows, lanes], v_ref[rows, lanes]
                    sides = []
                    for query in split_pair(q_ref[rows, lanes], low):
                        raised = jnp.exp2(dot(query, keys, NT) * EXP2_SCALE)
                        raised = jnp.where(valid, raised, 0.0)
                        total = jnp.sum(raised, axis=1, keepdims=True)
                        sides.append(dot(raised.astype(BF), values) * (1.0 / total))
                    o_ref[rows, lanes] = jnp.where(low, sides[0], sides[1]).astype(BF)
                return carry

            lax.fori_loop(0, HEADS // 2, body, 0)

    flat = sds((tokens, D), BF)
    flat32 = sds((tokens, D), F32)
    return call(
        kernel,
        (3,),
        [normed, q_gain, k_gain] + weights,
        [whole((tokens, D)), whole((1, D)), whole((1, D))] + w_specs,
        [flat, flat, flat, flat, flat32, flat, flat32, flat],
        [whole((tokens, D))] * 8,
        [pltpu.VMEM((D, D), BF), pltpu.VMEM((tokens, D), F32)],
        2 * tokens * D * 3 * D + 4 * tokens * PAD * D,
        "attend",
    )


def project(stream, attended, hidden, bias, units, last):
    tokens = stream.shape[0]
    weights, w_specs = piece_operands(units)

    def kernel(x_ref, o_ref, a_ref, b_ref, *refs):
        w_refs, (y_ref, total, held) = refs[: len(weights)], refs[len(weights) :]
        j = pl.program_id(0)
        block = read_block(j, units, w_refs, held, piece_rows)

        @pl.when(j == 0)
        def _():
            total[...] = x_ref[...].astype(F32) + b_ref[...] + dot(o_ref[...], block)

        @pl.when(j > 0)
        def _():
            total[...] += dot(a_ref[...], block)

        @pl.when(j == OUT_COUNT - 1)
        def _():
            y_ref[...] = total[...].astype(y_ref.dtype)

    return call(
        kernel,
        (OUT_COUNT,),
        [stream, attended, hidden, bias] + weights,
        [
            whole((tokens, D)),
            whole((tokens, D)),
            pl.BlockSpec((tokens, D), lambda j: (0, jnp.maximum(j - 1, 0))),
            whole((1, D)),
        ]
        + w_specs,
        [sds((tokens, D), BF if last else F32)],
        [whole((tokens, D))],
        [pltpu.VMEM((tokens, D), F32), pltpu.VMEM((D, D), BF)],
        2 * tokens * D * OUT_COUNT * D,
        "project",
    )[0]


def mlp_back(grad, slope, units):
    tokens = grad.shape[0]
    weights, w_specs = piece_operands(units)

    def kernel(g_ref, s_ref, *refs):
        w_refs = refs[: len(weights)]
        dy_ref, do_ref, du_ref, dbo_ref, dbu_ref, held = refs[len(weights) :]
        j = pl.program_id(0)

        @pl.when(j == 0)
        def _():
            dy = g_ref[...].astype(BF)
            dy_ref[...] = dy
            dbo_ref[...] = jnp.sum(dy.astype(F32), axis=0, keepdims=True)

        wide = dot(dy_ref[...], read_block(j, units, w_refs, held, piece_rows), NT)

        @pl.when(j == 0)
        def _():
            do_ref[...] = wide.astype(BF)

        @pl.when(j > 0)
        def _():
            du = (wide * s_ref[...].astype(F32)).astype(BF)
            du_ref[...] = du
            dbu_ref[...] = jnp.sum(du.astype(F32), axis=0, keepdims=True)

    shifted = pl.BlockSpec((tokens, D), lambda j: (0, jnp.maximum(j - 1, 0)))
    return call(
        kernel,
        (OUT_COUNT,),
        [grad, slope] + weights,
        [whole((tokens, D)), shifted] + w_specs,
        [
            sds((tokens, D), BF),
            sds((tokens, D), BF),
            sds((tokens, FF), BF),
            sds((1, D), F32),
            sds((1, FF), F32),
        ],
        [
            whole((tokens, D)),
            whole((tokens, D)),
            shifted,
            whole((1, D)),
            pl.BlockSpec((1, D), lambda j: (0, jnp.maximum(j - 1, 0))),
        ],
        [pltpu.VMEM((D, D), BF)],
        2 * tokens * D * OUT_COUNT * D,
        "mlp_back",
    )


def attend_back(grad_o, queries, keys, values, q_unit, q_inverse, k_unit, k_inverse, q_gain, k_gain):
    tokens = grad_o.shape[0]
    images = tokens // PAD

    def kernel(
        do_ref, q_ref, k_ref, v_ref, qu_ref, qi_ref, ku_ref, ki_ref, gq_ref, gk_ref,
        dz_ref, dgq_ref, dgk_ref, dq_held, dk_held,
    ):
        low = half_masks(PAD)
        valid = lax.broadcasted_iota(jnp.int32, (PAD, PAD), 0) < SEQ

        def body(pair, carry):
            lanes = pl.ds(pl.multiple_of(pair * PAIR, PAIR), PAIR)
            for image in range(images):
                rows = pl.ds(image * PAD, PAD)
                key, value = k_ref[rows, lanes], v_ref[rows, lanes]
                sides = []
                for query, grad in zip(
                    split_pair(q_ref[rows, lanes], low), split_pair(do_ref[rows, lanes], low)
                ):
                    raised = jnp.exp2(dot(key, query, NT) * EXP2_SCALE)
                    raised = jnp.where(valid, raised, 0.0)
                    probs = raised * (1.0 / jnp.sum(raised, axis=0, keepdims=True))
                    grad_probs = dot(value, grad, NT)
                    mixed = probs * grad_probs
                    row_dot = jnp.sum(mixed, axis=0, keepdims=True)
                    scores = (mixed - probs * row_dot).astype(BF)
                    sides.append(
                        (
                            dot(scores, key, TN),
                            dot(scores, query),
                            dot(probs.astype(BF), grad),
                        )
                    )
                dq_held[rows, lanes] = (jnp.where(low, sides[0][0], sides[1][0]) * SCALE).astype(BF)
                dk_held[rows, lanes] = ((sides[0][1] + sides[1][1]) * SCALE).astype(BF)
                dz_ref[rows, pl.ds(pl.multiple_of(2 * D + pair * PAIR, PAIR), PAIR)] = (
                    sides[0][2] + sides[1][2]
                ).astype(BF)
            return carry

        lax.fori_loop(0, HEADS // 2, body, 0)
        mixer = head_mixer()
        for held, u_ref, i_ref, g_ref, dg_ref, at in (
            (dq_held, qu_ref, qi_ref, gq_ref, dgq_ref, 0),
            (dk_held, ku_ref, ki_ref, gk_ref, dgk_ref, D),
        ):
            dg_ref[...] = jnp.zeros_like(dg_ref)

            def body(rows):
                grad, unit = held[rows, :].astype(F32), u_ref[rows, :].astype(F32)
                dg_ref[...] += jnp.sum(grad * unit, axis=0, keepdims=True)
                hat = grad * g_ref[...]
                out = i_ref[rows, :] * (
                    hat - head_mean(hat, mixer) - unit * head_mean(hat * unit, mixer)
                )
                dz_ref[rows, pl.ds(at, D)] = out.astype(BF)

            row_steps(tokens, 208, body)

    return call(
        kernel,
        (1,),
        [grad_o, queries, keys, values, q_unit, q_inverse, k_unit, k_inverse, q_gain, k_gain],
        [whole((tokens, D))] * 8 + [whole((1, D))] * 2,
        [sds((tokens, 3 * D), BF), sds((1, D), F32), sds((1, D), F32)],
        [whole((tokens, 3 * D)), whole((1, D)), whole((1, D))],
        [pltpu.VMEM((tokens, D), BF), pltpu.VMEM((tokens, D), BF)],
        10 * tokens * PAD * D,
        "attend_back",
    )


def weight_grads(left, right, count, name):
    tokens = left.shape[0]

    def kernel(l_ref, r_ref, out_ref):
        out_ref[0] = dot(l_ref[...], r_ref[...], TN).astype(BF)

    def spec(array):
        wide = array.shape[1] > D
        return pl.BlockSpec((tokens, D), (lambda j: (0, j)) if wide else (lambda j: (0, 0)))

    return call(
        kernel,
        (count,),
        [left, right],
        [spec(left), spec(right)],
        [sds((count, D, D), BF)],
        [pl.BlockSpec((1, D, D), lambda j: (j, 0, 0))],
        [],
        2 * tokens * D * count * D,
        name,
    )[0]


def stream_back(grad, stream, gain, grad_u, grad_qkv, units):
    tokens = grad.shape[0]
    weights, w_specs = piece_operands(units)

    def kernel(g_ref, x_ref, c_ref, du_ref, dz_ref, *refs):
        w_refs, (out_ref, dg_ref, total, held) = refs[: len(weights)], refs[len(weights) :]
        j = pl.program_id(0)
        block = read_block(j, units, w_refs, held, piece_rows)

        @pl.when(j == 0)
        def _():
            total[...] = dot(du_ref[...], block, NT)

        @pl.when((j > 0) & (j < RATIO))
        def _():
            total[...] += dot(du_ref[...], block, NT)

        @pl.when(j >= RATIO)
        def _():
            total[...] += dot(dz_ref[...], block, NT)

        @pl.when(j == IN_COUNT - 1)
        def _():
            dg_ref[...] = jnp.zeros_like(dg_ref)

            def body(rows):
                unit, inverse = row_parts(x_ref[rows, :].astype(F32))
                grad_h = total[rows, :]
                dg_ref[...] += jnp.sum(grad_h * unit, axis=0, keepdims=True)
                hat = grad_h * c_ref[...]
                out_ref[rows, :] = g_ref[rows, :].astype(F32) + inverse * (
                    hat
                    - jnp.mean(hat, axis=-1, keepdims=True)
                    - unit * jnp.mean(hat * unit, axis=-1, keepdims=True)
                )

            row_steps(tokens, 48, body)

    return call(
        kernel,
        (IN_COUNT,),
        [grad, stream, gain, grad_u, grad_qkv] + weights,
        [
            whole((tokens, D)),
            whole((tokens, D)),
            whole((1, D)),
            pl.BlockSpec((tokens, D), lambda j: (0, jnp.minimum(j, RATIO - 1))),
            pl.BlockSpec((tokens, D), lambda j: (0, jnp.maximum(j - RATIO, 0))),
        ]
        + w_specs,
        [sds((tokens, D), F32), sds((1, D), F32)],
        [whole((tokens, D)), whole((1, D))],
        [pltpu.VMEM((tokens, D), F32), pltpu.VMEM((D, D), BF)],
        2 * tokens * D * IN_COUNT * D,
        "stream_back",
    )


def shampoo(grad, full, right_full, left_root, left_stats, right_stats, weights, ema):
    count, rows, _ = grad.shape

    def kernel(g_ref, f_ref, r_ref, lr_ref, ls_ref, rs_ref, w_ref, e_ref, lo_ref, ro_ref, wo_ref, eo_ref):
        at = lax.axis_index("dp") * rows
        block = f_ref[0]
        gram = dot(g_ref[0].astype(BF), block, NT)
        lo_ref[0] = STAT_DECAY * ls_ref[0] + (1.0 - STAT_DECAY) * gram
        pick = (
            lax.broadcasted_iota(jnp.int32, (rows, D), 1)
            == lax.broadcasted_iota(jnp.int32, (rows, D), 0) + at
        )
        columns = dot(jnp.where(pick, 1.0, 0.0).astype(BF), block, NT).astype(BF)
        ro_ref[0] = STAT_DECAY * rs_ref[0] + (1.0 - STAT_DECAY) * dot(columns, block)
        lifted = dot(lr_ref[0].astype(BF), block).astype(BF)
        precond = dot(lifted, r_ref[0])
        renewed = w_ref[0] * (1.0 - RATE_MAT * DECAY_MAT) - RATE_MAT * precond
        wo_ref[0] = renewed
        eo_ref[0] = EMA_DECAY * e_ref[0] + (1.0 - EMA_DECAY) * renewed

    own = pl.BlockSpec((1, rows, D), lambda j: (j, 0, 0))
    square = pl.BlockSpec((1, D, D), lambda j: (j, 0, 0))
    return call(
        kernel,
        (count,),
        [grad, full, right_full, left_root, left_stats, right_stats, weights, ema],
        [own, square, square] + [own] * 5,
        [sds((count, rows, D), F32)] * 4,
        [own] * 4,
        [],
        10 * rows * D * count * D,
        "shampoo",
    )


def split_vector(row_vec):
    ends = (D, D + HEAD_DIM, D + 2 * HEAD_DIM, D + 2 * HEAD_DIM + FF)
    ln_gain, q_gain, k_gain, mlp_bias, out_bias = jnp.split(row_vec, ends)
    return (
        ln_gain[None],
        jnp.tile(q_gain, HEADS)[None],
        jnp.tile(k_gain, HEADS)[None],
        mlp_bias[None],
        out_bias[None],
    )


def pad_tokens(array):
    return jnp.pad(array, ((0, 0), (0, PAD - SEQ), (0, 0))).reshape(-1, D)


def cut_tokens(array):
    return array.reshape(-1, PAD, D)[:, :SEQ]


def on_device(
    image_tokens,
    cotangent,
    weights,
    weights_ema,
    left_stats,
    right_stats,
    left_root,
    right_root,
    vectors,
    vec_first,
    vec_second,
):
    rounded = weights.astype(BF)
    block_rows = lax.all_gather(rounded, "head", axis=0, tiled=True)
    full_blocks = lax.all_gather(block_rows, "dp", axis=1, tiled=True)
    right_full = lax.all_gather(right_root.astype(BF), "dp", axis=1, tiled=True)

    def group(depth, first, count):
        return [([full_blocks], depth * PER_LAYER + first, count)]

    stream = pad_tokens(image_tokens)
    saved = []
    for depth in range(LAYERS):
        ln_gain, q_gain, k_gain, mlp_bias, out_bias = split_vector(vectors[depth])
        normed, hidden, slope = mlp_in(stream, ln_gain, mlp_bias, group(depth, 3, RATIO))
        queries, keys, values, q_unit, q_inv, k_unit, k_inv, attended = attend(
            normed, q_gain, k_gain, group(depth, 0, 3)
        )
        saved.append(
            (stream, normed, hidden, slope, queries, keys, values, q_unit, q_inv, k_unit, k_inv, attended)
        )
        stream = project(
            stream, attended, hidden, out_bias, group(depth, IN_COUNT, OUT_COUNT), depth == LAYERS - 1
        )
    block_out = cut_tokens(stream)
    grad = pad_tokens(cotangent)
    weight_parts = [None] * LAYERS
    vector_parts = [None] * LAYERS
    for depth in reversed(range(LAYERS)):
        ln_gain, q_gain, k_gain, _, _ = split_vector(vectors[depth])
        stream, normed, hidden, slope, queries, keys, values, q_unit, q_inv, k_unit, k_inv, attended = saved[depth]
        dy, do, du, dbo, dbu = mlp_back(grad, slope, group(depth, IN_COUNT, OUT_COUNT))
        dqkv, dgq, dgk = attend_back(
            do, queries, keys, values, q_unit, q_inv, k_unit, k_inv, q_gain, k_gain
        )
        weight_parts[depth] = [
            weight_grads(normed, dqkv, 3, "grad_qkv"),
            weight_grads(normed, du, RATIO, "grad_u"),
            weight_grads(attended, dy, 1, "grad_o"),
            weight_grads(hidden, dy, RATIO, "grad_a"),
        ]
        grad, dg = stream_back(
            grad, stream, ln_gain, du, dqkv, group(depth, 3, RATIO) + group(depth, 0, 3)
        )
        vector_parts[depth] = jnp.concatenate(
            [
                dg[0],
                dgq.reshape(HEADS, HEAD_DIM).sum(0),
                dgk.reshape(HEADS, HEAD_DIM).sum(0),
                dbu[0],
                dbo[0],
            ]
        )
    grad_stream = cut_tokens(grad)
    partial_grad = jnp.concatenate([part for parts in weight_parts for part in parts], axis=0)
    rows_part = lax.psum_scatter(partial_grad, "dp", scatter_dimension=1, tiled=True)
    own_grad = lax.psum_scatter(rows_part, "head", scatter_dimension=0, tiled=True)
    weight_grad = own_grad.astype(F32)
    grad_full = lax.all_gather(own_grad, "dp", axis=1, tiled=True)
    vector_grad = lax.psum(jnp.stack(vector_parts), ("dp", "head"))
    left_new, right_new, weight_new, ema_new = shampoo(
        weight_grad, grad_full, right_full, left_root, left_stats, right_stats, weights, weights_ema
    )
    first_new = BETA_ONE * vec_first + (1.0 - BETA_ONE) * vector_grad
    second_new = BETA_TWO * vec_second + (1.0 - BETA_TWO) * vector_grad * vector_grad
    first_hat = first_new / (1.0 - BETA_ONE**STEP)
    second_hat = second_new / (1.0 - BETA_TWO**STEP)
    vec_new = vectors - RATE_VEC * first_hat / (jnp.sqrt(second_hat) + ADAM_EPS)
    return (
        block_out,
        grad_stream,
        weight_grad,
        left_new,
        right_new,
        weight_new,
        ema_new,
        first_new,
        second_new,
        vec_new,
    )


def solution(mesh):
    tokens, blocks = P(("dp", "head"), None, None), P("head", "dp", None)
    return jax.shard_map(
        on_device,
        mesh=mesh,
        in_specs=(tokens, tokens) + (blocks,) * 6 + (P(),) * 3,
        out_specs=(tokens, tokens) + (blocks,) * 5 + (P(),) * 3,
        check_vma=False,
    )
```

```python
import functools
import math

import jax
import jax.numpy as jnp
from jax import lax
from jax.experimental import pallas as pl
from jax.experimental.pallas import tpu as pltpu
from jax.sharding import PartitionSpec as P

D = 768
HEADS = 12
HEAD_DIM = 64
FF = 3072
SEQ = 196
PAD = 208
LAYERS = 2
STEP = 10
RATIO = FF // D
IN_COUNT = 3 + RATIO
OUT_COUNT = 1 + RATIO
PER_LAYER = IN_COUNT + OUT_COUNT
PAIR = 2 * HEAD_DIM
TILE = 256

EPS_NORM = 1e-06
BETA_ONE = 0.9
BETA_TWO = 0.95
ADAM_EPS = 1e-08
RATE_VEC = 0.3
RATE_MAT = 0.003
DECAY_MAT = 0.1
STAT_DECAY = 0.5
EMA_DECAY = 0.8
SCALE = HEAD_DIM ** (-0.5)
EXP2_SCALE = SCALE * math.log2(math.e)

BF = jnp.bfloat16
F32 = jnp.float32
NN = (((1,), (0,)), ((), ()))
NT = (((1,), (1,)), ((), ()))
TN = (((0,), (0,)), ((), ()))


def dot(a, b, dims=NN):
    return lax.dot_general(a, b, dims, preferred_element_type=F32)


def call(kernel, grid, operands, in_specs, outs, out_specs, scratch, flops, name, aliases=None):
    moved = sum(o.size * o.dtype.itemsize for o in operands) + sum(
        math.prod(o.shape) * o.dtype.itemsize for o in outs
    )
    return pl.pallas_call(
        kernel,
        grid=grid,
        in_specs=in_specs,
        out_specs=out_specs,
        out_shape=outs,
        scratch_shapes=scratch,
        compiler_params=pltpu.CompilerParams(vmem_limit_bytes=56 * 1024 * 1024),
        cost_estimate=pl.CostEstimate(flops=flops, bytes_accessed=moved, transcendentals=0),
        input_output_aliases=aliases or {},
        name=name,
    )(*operands)


def whole(shape):
    return pl.BlockSpec(shape, lambda *ids: (0,) * len(shape))


def sds(shape, dtype):
    return jax.ShapeDtypeStruct(shape, dtype)


CHIPS = ((0, 0), (0, 1), (1, 0), (1, 1))


class Blocks:
    def __init__(self, steps):
        self.steps = steps
        self.arrays = []
        for places in steps:
            for _, pieces in places:
                for array, _ in pieces:
                    if not any(array is other for other in self.arrays):
                        self.arrays.append(array)
        self.count = len(steps[0][0][1])
        self.specs = [pl.BlockSpec(memory_space=pl.ANY)] * len(self.arrays)
        self.scratch = [pltpu.VMEM((2, D, D), BF), pltpu.SemaphoreType.DMA((2, self.count))]

    def bind(self, refs, held, sems):
        self.refs, self.held, self.sems = refs, held, sems

    def copies(self, pieces, slot):
        made = []
        for at, (array, block) in enumerate(pieces):
            ref = next(ref for ref, other in zip(self.refs, self.arrays) if other is array)
            target = self.held.at[slot]
            if self.count > 1:
                rows = array.shape[-2]
                row = piece_row(*CHIPS[at % 4], at // 4, rows)
                target = self.held.at[slot, pl.ds(pl.multiple_of(row, 16), rows)]
            made.append(pltpu.make_async_copy(ref.at[block], target, self.sems.at[slot, at]))
        return made

    def start(self, j, wanted):
        head = lax.axis_index("head")
        for step, places in enumerate(self.steps):
            for owners, pieces in places:
                here = wanted == step
                if owners is not None:
                    here = here & functools.reduce(lambda a, b: a | b, [head == owner for owner in owners])

                @pl.when(here)
                def _(step=step, pieces=pieces):
                    for copy in self.copies(pieces, step % 2):
                        copy.start()

    def step(self, j):
        @pl.when(j == 0)
        def _():
            self.start(j, j)

        @pl.when(j + 1 < len(self.steps))
        def _():
            self.start(j, j + 1)

        slot = lax.rem(j, 2)
        for copy in self.copies(self.steps[0][0][1], slot):
            copy.wait()
        return self.held[slot]


def piece_row(dy, dx, dc, rows):
    me = lax.axis_index("dp")
    core, x, y = lax.rem(me, 2), lax.rem(me // 2, 2), me // 4
    y, x, core = (1 - v if d else v for v, d in ((y, dy), (x, dx), (core, dc)))
    return (y * 4 + x * 2 + core) * rows


def row_parts(values):
    average = jnp.mean(values, axis=-1, keepdims=True)
    centred = values - average
    inverse = lax.rsqrt(jnp.mean(centred * centred, axis=-1, keepdims=True) + EPS_NORM)
    return centred * inverse, inverse


def head_mixer():
    row = lax.broadcasted_iota(jnp.int32, (TILE, TILE), 0) // HEAD_DIM
    column = lax.broadcasted_iota(jnp.int32, (TILE, TILE), 1) // HEAD_DIM
    return jnp.where(row == column, 1.0 / HEAD_DIM, 0.0).astype(BF)


def head_mean(values, mixer):
    high = values.astype(BF)
    low = (values - high.astype(F32)).astype(BF)
    return jnp.concatenate(
        [
            dot(high[:, at : at + TILE], mixer) + dot(low[:, at : at + TILE], mixer)
            for at in range(0, D, TILE)
        ],
        axis=1,
    )


def gelu_parts(z):
    decay = jnp.exp(-0.5 * z * z)
    t = 1.0 / (1.0 + 0.3275911 * math.sqrt(0.5) * jnp.abs(z))
    poly = t * (
        0.254829592
        + t * (-0.284496736 + t * (1.421413741 + t * (-1.453152027 + t * 1.061405429)))
    )
    tail = 0.5 * poly * decay
    share = jnp.where(z >= 0, 1.0 - tail, tail)
    return z * share, share + z * decay * (1.0 / math.sqrt(2.0 * math.pi))


def row_steps(total, size, body):
    def step(i, carry):
        body(pl.ds(pl.multiple_of(i * size, size), size))
        return carry

    lax.fori_loop(0, total // size, step, 0)


def mlp_in(normed, bias, blocks):
    tokens = normed.shape[0]

    def kernel(h_ref, b_ref, *refs):
        w_refs, (a_ref, s_ref, wide, *fetch) = refs[: len(blocks.arrays)], refs[len(blocks.arrays) :]
        blocks.bind(w_refs, *fetch)
        j = pl.program_id(0)
        wide[...] = dot(h_ref[...], blocks.step(j))

        def body(rows):
            act, slope = gelu_parts(wide[rows, :] + b_ref[...])
            a_ref[rows, :] = act.astype(BF)
            s_ref[rows, :] = slope.astype(BF)

        row_steps(tokens, 16, body)

    return call(
        kernel,
        (RATIO,),
        [normed, bias] + blocks.arrays,
        [whole((tokens, D)), pl.BlockSpec((1, D), lambda j: (0, j))] + blocks.specs,
        [sds((tokens, FF), BF), sds((tokens, FF), BF)],
        [pl.BlockSpec((tokens, D), lambda j: (0, j))] * 2,
        [pltpu.VMEM((tokens, D), F32)] + blocks.scratch,
        2 * tokens * D * FF,
        "mlp_in",
    )


def half_masks(rows):
    low = lax.broadcasted_iota(jnp.int32, (rows, PAIR), 1) < HEAD_DIM
    return low


def split_pair(values, low):
    zero = jnp.zeros_like(values)
    return jnp.where(low, values, zero), jnp.where(low, zero, values)


def attend(stream, ln_gain, q_gain, k_gain, blocks):
    tokens = stream.shape[0]
    images = tokens // PAD

    def kernel(x_ref, g_ref, gq_ref, gk_ref, *refs):
        w_refs, refs = refs[: len(blocks.arrays)], refs[len(blocks.arrays) :]
        h_ref, q_ref, k_ref, v_ref, qu_ref, qi_ref, ku_ref, ki_ref, o_ref, wide, *fetch = refs
        blocks.bind(w_refs, *fetch)
        j = pl.program_id(0)

        @pl.when(j == 0)
        def _():
            def body(rows):
                unit, _ = row_parts(x_ref[rows, :].astype(F32))
                h_ref[rows, :] = (unit * g_ref[...]).astype(BF)

            row_steps(tokens, 48, body)

        wide[...] = dot(h_ref[...], blocks.step(j))

        def normalise(g_ref, n_ref, u_ref, i_ref):
            mixer = head_mixer()

            def body(rows):
                raw = wide[rows, :]
                centred = raw - head_mean(raw, mixer)
                inverse = lax.rsqrt(head_mean(centred * centred, mixer) + EPS_NORM)
                unit = centred * inverse
                n_ref[rows, :] = (unit * g_ref[...]).astype(BF)
                u_ref[rows, :] = unit.astype(BF)
                i_ref[rows, :] = inverse

            row_steps(tokens, 208, body)

        @pl.when(j == 0)
        def _():
            normalise(gq_ref, q_ref, qu_ref, qi_ref)

        @pl.when(j == 1)
        def _():
            normalise(gk_ref, k_ref, ku_ref, ki_ref)

        @pl.when(j == 2)
        def _():
            v_ref[...] = wide[...].astype(BF)
            low = half_masks(PAD)
            valid = lax.broadcasted_iota(jnp.int32, (PAD, PAD), 1) < SEQ

            def body(pair, carry):
                lanes = pl.ds(pl.multiple_of(pair * PAIR, PAIR), PAIR)
                for image in range(images):
                    rows = pl.ds(image * PAD, PAD)
                    keys, values = k_ref[rows, lanes], v_ref[rows, lanes]
                    sides = []
                    for query in split_pair(q_ref[rows, lanes], low):
                        raised = jnp.exp2(dot(query, keys, NT) * EXP2_SCALE)
                        raised = jnp.where(valid, raised, 0.0)
                        total = jnp.sum(raised, axis=1, keepdims=True)
                        sides.append(dot(raised.astype(BF), values) * (1.0 / total))
                    o_ref[rows, lanes] = jnp.where(low, sides[0], sides[1]).astype(BF)
                return carry

            lax.fori_loop(0, HEADS // 2, body, 0)

    flat = sds((tokens, D), BF)
    flat32 = sds((tokens, D), F32)
    return call(
        kernel,
        (3,),
        [stream, ln_gain, q_gain, k_gain] + blocks.arrays,
        [whole((tokens, D))] + [whole((1, D))] * 3 + blocks.specs,
        [flat, flat, flat, flat, flat, flat32, flat, flat32, flat],
        [whole((tokens, D))] * 9,
        [pltpu.VMEM((tokens, D), F32)] + blocks.scratch,
        2 * tokens * D * 3 * D + 4 * tokens * PAD * D,
        "attend",
    )


def project(stream, attended, hidden, bias, blocks, last):
    tokens = stream.shape[0]

    def kernel(x_ref, o_ref, a_ref, b_ref, *refs):
        w_refs, (y_ref, total, *fetch) = refs[: len(blocks.arrays)], refs[len(blocks.arrays) :]
        blocks.bind(w_refs, *fetch)
        j = pl.program_id(0)
        block = blocks.step(j)

        @pl.when(j == 0)
        def _():
            total[...] = x_ref[...].astype(F32) + b_ref[...] + dot(o_ref[...], block)

        @pl.when(j > 0)
        def _():
            total[...] += dot(a_ref[...], block)

        @pl.when(j == OUT_COUNT - 1)
        def _():
            y_ref[...] = total[...].astype(y_ref.dtype)

    return call(
        kernel,
        (OUT_COUNT,),
        [stream, attended, hidden, bias] + blocks.arrays,
        [
            whole((tokens, D)),
            whole((tokens, D)),
            pl.BlockSpec((tokens, D), lambda j: (0, jnp.maximum(j - 1, 0))),
            whole((1, D)),
        ]
        + blocks.specs,
        [sds((tokens, D), BF if last else F32)],
        [whole((tokens, D))],
        [pltpu.VMEM((tokens, D), F32)] + blocks.scratch,
        2 * tokens * D * OUT_COUNT * D,
        "project",
    )[0]


def mlp_back(grad, slope, blocks):
    tokens = grad.shape[0]

    def kernel(g_ref, s_ref, *refs):
        w_refs, refs = refs[: len(blocks.arrays)], refs[len(blocks.arrays) :]
        dy_ref, do_ref, du_ref, dbo_ref, dbu_ref, *fetch = refs
        blocks.bind(w_refs, *fetch)
        j = pl.program_id(0)

        @pl.when(j == 0)
        def _():
            dy = g_ref[...].astype(BF)
            dy_ref[...] = dy
            dbo_ref[...] = jnp.sum(dy.astype(F32), axis=0, keepdims=True)

        wide = dot(dy_ref[...], blocks.step(j), NT)

        @pl.when(j == 0)
        def _():
            do_ref[...] = wide.astype(BF)

        @pl.when(j > 0)
        def _():
            du = (wide * s_ref[...].astype(F32)).astype(BF)
            du_ref[...] = du
            dbu_ref[...] = jnp.sum(du.astype(F32), axis=0, keepdims=True)

    shifted = pl.BlockSpec((tokens, D), lambda j: (0, jnp.maximum(j - 1, 0)))
    return call(
        kernel,
        (OUT_COUNT,),
        [grad, slope] + blocks.arrays,
        [whole((tokens, D)), shifted] + blocks.specs,
        [
            sds((tokens, D), BF),
            sds((tokens, D), BF),
            sds((tokens, FF), BF),
            sds((1, D), F32),
            sds((1, FF), F32),
        ],
        [
            whole((tokens, D)),
            whole((tokens, D)),
            shifted,
            whole((1, D)),
            pl.BlockSpec((1, D), lambda j: (0, jnp.maximum(j - 1, 0))),
        ],
        blocks.scratch,
        2 * tokens * D * OUT_COUNT * D,
        "mlp_back",
    )


def attend_back(grad_o, queries, keys, values, q_unit, q_inverse, k_unit, k_inverse, q_gain, k_gain):
    tokens = grad_o.shape[0]
    images = tokens // PAD

    def kernel(
        do_ref, q_ref, k_ref, v_ref, qu_ref, qi_ref, ku_ref, ki_ref, gq_ref, gk_ref,
        dz_ref, dgq_ref, dgk_ref, dq_held, dk_held,
    ):
        low = half_masks(PAD)
        valid = lax.broadcasted_iota(jnp.int32, (PAD, PAD), 0) < SEQ

        def body(pair, carry):
            lanes = pl.ds(pl.multiple_of(pair * PAIR, PAIR), PAIR)
            for image in range(images):
                rows = pl.ds(image * PAD, PAD)
                key, value = k_ref[rows, lanes], v_ref[rows, lanes]
                sides = []
                for query, grad in zip(
                    split_pair(q_ref[rows, lanes], low), split_pair(do_ref[rows, lanes], low)
                ):
                    raised = jnp.exp2(dot(key, query, NT) * EXP2_SCALE)
                    raised = jnp.where(valid, raised, 0.0)
                    probs = raised * (1.0 / jnp.sum(raised, axis=0, keepdims=True))
                    grad_probs = dot(value, grad, NT)
                    mixed = probs * grad_probs
                    row_dot = jnp.sum(mixed, axis=0, keepdims=True)
                    scores = (mixed - probs * row_dot).astype(BF)
                    sides.append(
                        (
                            dot(scores, key, TN),
                            dot(scores, query),
                            dot(probs.astype(BF), grad),
                        )
                    )
                dq_held[rows, lanes] = (jnp.where(low, sides[0][0], sides[1][0]) * SCALE).astype(BF)
                dk_held[rows, lanes] = ((sides[0][1] + sides[1][1]) * SCALE).astype(BF)
                dz_ref[rows, pl.ds(pl.multiple_of(2 * D + pair * PAIR, PAIR), PAIR)] = (
                    sides[0][2] + sides[1][2]
                ).astype(BF)
            return carry

        lax.fori_loop(0, HEADS // 2, body, 0)
        mixer = head_mixer()
        for held, u_ref, i_ref, g_ref, dg_ref, at in (
            (dq_held, qu_ref, qi_ref, gq_ref, dgq_ref, 0),
            (dk_held, ku_ref, ki_ref, gk_ref, dgk_ref, D),
        ):
            dg_ref[...] = jnp.zeros_like(dg_ref)

            def body(rows):
                grad, unit = held[rows, :].astype(F32), u_ref[rows, :].astype(F32)
                dg_ref[...] += jnp.sum(grad * unit, axis=0, keepdims=True)
                hat = grad * g_ref[...]
                out = i_ref[rows, :] * (
                    hat - head_mean(hat, mixer) - unit * head_mean(hat * unit, mixer)
                )
                dz_ref[rows, pl.ds(at, D)] = out.astype(BF)

            row_steps(tokens, 208, body)

    return call(
        kernel,
        (1,),
        [grad_o, queries, keys, values, q_unit, q_inverse, k_unit, k_inverse, q_gain, k_gain],
        [whole((tokens, D))] * 8 + [whole((1, D))] * 2,
        [sds((tokens, 3 * D), BF), sds((1, D), F32), sds((1, D), F32)],
        [whole((tokens, 3 * D)), whole((1, D)), whole((1, D))],
        [pltpu.VMEM((tokens, D), BF), pltpu.VMEM((tokens, D), BF)],
        10 * tokens * PAD * D,
        "attend_back",
    )


def weight_grads(segments, cut, name):
    tokens = segments[0][0].shape[0]
    total = sum(count for _, _, count in segments)
    operands, specs, start = [], [], 0
    for left, right, count in segments:
        for side in (left, right):
            index = functools.partial(
                lambda at, last, j: (0, jnp.clip(j - at, 0, last)), start, side.shape[1] // D - 1
            )
            operands.append(side)
            specs.append(pl.BlockSpec((tokens, D), index))
        start += count

    def kernel(*refs):
        ins, outs = refs[: len(operands)], refs[len(operands) :]
        j = pl.program_id(0)
        start = 0
        for at, (_, _, count) in enumerate(segments):

            def body(at=at):
                value = dot(ins[2 * at][...], ins[2 * at + 1][...], TN)
                if cut:
                    outs[-1][...] = value
                else:
                    outs[0][0] = value.astype(BF)

            if count == total:
                body()
            else:
                pl.when((j >= start) & (j < start + count))(body)
            start += count
        if cut:
            held, rows = outs[-1], D // 8
            for chip, (dy, dx) in enumerate(CHIPS):
                for core in (0, 1):
                    row = pl.multiple_of(piece_row(dy, dx, core, rows), 16)
                    part = held[pl.ds(row, rows), :].astype(BF)
                    if core == 0:
                        outs[chip][0] = part
                    else:
                        outs[4][chip, 0] = part

    if cut:
        shapes = [sds((total, D // 8, D), BF)] * 4 + [sds((4, total, D // 8, D), BF)]
        out_specs = [pl.BlockSpec((1, D // 8, D), lambda j: (j, 0, 0))] * 4
        out_specs += [pl.BlockSpec((4, 1, D // 8, D), lambda j: (0, j, 0, 0))]
    else:
        shapes = [sds((total, D, D), BF)]
        out_specs = [pl.BlockSpec((1, D, D), lambda j: (j, 0, 0))]
    return call(
        kernel,
        (total,),
        operands,
        specs,
        shapes,
        out_specs,
        [pltpu.VMEM((D, D), F32)] if cut else [],
        2 * tokens * D * total * D,
        name,
    )


def stream_back(grad, stream, gain, grad_u, grad_qkv, blocks):
    tokens = grad.shape[0]

    def kernel(g_ref, x_ref, c_ref, du_ref, dz_ref, *refs):
        w_refs, (out_ref, dg_ref, total, *fetch) = refs[: len(blocks.arrays)], refs[len(blocks.arrays) :]
        blocks.bind(w_refs, *fetch)
        j = pl.program_id(0)
        block = blocks.step(j)

        @pl.when(j == 0)
        def _():
            total[...] = dot(du_ref[...], block, NT)

        @pl.when((j > 0) & (j < RATIO))
        def _():
            total[...] += dot(du_ref[...], block, NT)

        @pl.when(j >= RATIO)
        def _():
            total[...] += dot(dz_ref[...], block, NT)

        @pl.when(j == IN_COUNT - 1)
        def _():
            dg_ref[...] = jnp.zeros_like(dg_ref)

            def body(rows):
                unit, inverse = row_parts(x_ref[rows, :].astype(F32))
                grad_h = total[rows, :]
                dg_ref[...] += jnp.sum(grad_h * unit, axis=0, keepdims=True)
                hat = grad_h * c_ref[...]
                out_ref[rows, :] = g_ref[rows, :].astype(F32) + inverse * (
                    hat
                    - jnp.mean(hat, axis=-1, keepdims=True)
                    - unit * jnp.mean(hat * unit, axis=-1, keepdims=True)
                )

            row_steps(tokens, 48, body)

    return call(
        kernel,
        (IN_COUNT,),
        [grad, stream, gain, grad_u, grad_qkv] + blocks.arrays,
        [
            whole((tokens, D)),
            whole((tokens, D)),
            whole((1, D)),
            pl.BlockSpec((tokens, D), lambda j: (0, jnp.minimum(j, RATIO - 1))),
            pl.BlockSpec((tokens, D), lambda j: (0, jnp.maximum(j - RATIO, 0))),
        ]
        + blocks.specs,
        [sds((tokens, D), F32), sds((1, D), F32)],
        [whole((tokens, D)), whole((1, D))],
        [pltpu.VMEM((tokens, D), F32)] + blocks.scratch,
        2 * tokens * D * IN_COUNT * D,
        "stream_back",
    )


def shampoo(grad, full, right, left_root, left_stats, right_stats, weights, ema, first, earlier):
    count, rows, _ = grad.shape

    def kernel(g_ref, lr_ref, ls_ref, rs_ref, w_ref, e_ref, *refs):
        f_refs, refs = refs[: len(full.arrays)], refs[len(full.arrays) :]
        r_refs, refs = refs[: len(right.arrays)], refs[len(right.arrays) + len(earlier) :]
        go_ref, lo_ref, ro_ref, wo_ref, eo_ref, f_held, f_sems, r_held, r_sems = refs
        full.bind(f_refs, f_held, f_sems)
        right.bind(r_refs, r_held, r_sems)
        j = pl.program_id(0)
        at = lax.axis_index("dp") * rows
        block = full.step(j)
        right_block = right.step(j)
        go_ref[0] = g_ref[0]
        gram = dot(g_ref[0].astype(BF), block, NT)
        lo_ref[0] = STAT_DECAY * ls_ref[0] + (1.0 - STAT_DECAY) * gram
        pick = (
            lax.broadcasted_iota(jnp.int32, (rows, D), 1)
            == lax.broadcasted_iota(jnp.int32, (rows, D), 0) + at
        )
        columns = dot(jnp.where(pick, 1.0, 0.0).astype(BF), block, NT).astype(BF)
        ro_ref[0] = STAT_DECAY * rs_ref[0] + (1.0 - STAT_DECAY) * dot(columns, block)
        lifted = dot(lr_ref[0].astype(BF), block).astype(BF)
        precond = dot(lifted, right_block)
        renewed = w_ref[0] * (1.0 - RATE_MAT * DECAY_MAT) - RATE_MAT * precond
        wo_ref[0] = renewed
        eo_ref[0] = EMA_DECAY * e_ref[0] + (1.0 - EMA_DECAY) * renewed

    part = pl.BlockSpec((1, rows, D), lambda j: (j, 0, 0))
    own = pl.BlockSpec((1, rows, D), lambda j: (first + j, 0, 0))
    inputs = [grad, left_root, left_stats, right_stats, weights, ema] + full.arrays + right.arrays
    return call(
        kernel,
        (count,),
        inputs + list(earlier),
        [part] + [own] * 5 + full.specs + right.specs + [pl.BlockSpec(memory_space=pl.ANY)] * len(earlier),
        [sds(weights.shape, F32)] * 5,
        [own] * 5,
        full.scratch + right.scratch,
        10 * rows * D * count * D,
        "shampoo",
        {len(inputs) + at: at for at in range(len(earlier))},
    )


def split_vector(row_vec):
    ends = (D, D + HEAD_DIM, D + 2 * HEAD_DIM, D + 2 * HEAD_DIM + FF)
    ln_gain, q_gain, k_gain, mlp_bias, out_bias = jnp.split(row_vec, ends)
    return (
        ln_gain[None],
        jnp.tile(q_gain, HEADS)[None],
        jnp.tile(k_gain, HEADS)[None],
        mlp_bias[None],
        out_bias[None],
    )


def pad_tokens(array):
    return jnp.pad(array, ((0, 0), (0, PAD - SEQ), (0, 0))).reshape(-1, D)


def cut_tokens(array):
    return array.reshape(-1, PAD, D)[:, :SEQ]


QKV, MLP, OUT = 0, 3, IN_COUNT
SIZES = {QKV: 3, MLP: RATIO, OUT: OUT_COUNT}


class Collectives:
    cut = False

    def __init__(self, weights, right_root):
        rows = lax.all_gather(weights.astype(BF), "head", axis=0, tiled=True)
        self.blocks = lax.all_gather(rows, "dp", axis=1, tiled=True)
        self.right = lax.all_gather(right_root.astype(BF), "dp", axis=1, tiled=True)
        self.count = weights.shape[0]
        self.parts = {}

    def group(self, *runs):
        return Blocks(
            [
                [(None, [(self.blocks, depth * PER_LAYER + first + at)])]
                for depth, first, count in runs
                for at in range(count)
            ]
        )

    def next(self, array):
        return array

    def done(self, name, array):
        pass

    def add_grads(self, depth, first, pieces):
        self.parts[depth, first] = pieces[0]

    def finish(self, renew):
        partial = jnp.concatenate([self.parts[key] for key in sorted(self.parts)], axis=0)
        rows = lax.psum_scatter(partial, "dp", scatter_dimension=1, tiled=True)
        own = lax.psum_scatter(rows, "head", scatter_dimension=0, tiled=True)
        full = lax.all_gather(own, "dp", axis=1, tiled=True)
        full, right = (
            Blocks([[(None, [(array, at)])] for at in range(self.count)]) for array in (full, self.right)
        )
        return renew(own.astype(F32), full, right, 0, ())

    def vector_sum(self, vectors):
        return lax.psum(vectors, ("dp", "head"))


DP, LINE = 8, 4
HALF = 3
STEPS = {"core": 1, "x": 2, "y": 4}
ROUNDS = ((2, 0, 0, 0), (1, 2, 1, 1), (3, 3, 3, 2))


def swap(array, axis):
    return lax.ppermute(array, "dp", [(i, i ^ STEPS[axis]) for i in range(DP)])


def hop(array, *pairs):
    return lax.ppermute(array, "head", pairs)


def after(array, *earlier):
    return lax.optimization_barrier((array,) + earlier)[0] if earlier else array


class PlaneGather:
    def __init__(self, own, half):
        self.own, self.half = own, half

    def first(self, *earlier):
        own = self.own = after(self.own, *earlier)
        self.x, self.y = swap(own, "x"), swap(own, "y")
        return [own]

    def second(self, *earlier):
        x, y = after(self.x[: self.half], *earlier), after(self.y[self.half :], *earlier)
        self.far = [swap(x, "y"), swap(y, "x")]
        return [x, y]

    def cores(self, *earlier):
        self.chips = [after(chip, *earlier) for chip in [self.own, self.x, self.y] + self.far]
        self.others = [swap(chip, "core") for chip in self.chips]
        return self.chips

    def pieces(self, at):
        made = []
        for chips in (self.chips, self.others):
            made += [(chip, at) for chip in chips[:3]]
            made.append((chips[3], at) if at < self.half else (chips[4], at - self.half))
        return made


class Permutes:
    cut = True

    def __init__(self, weights, right_root):
        self.parts = {}
        self.last, self.pins, self.chains = (), [], []
        self.right_root = right_root.astype(BF)
        own = weights.astype(BF)
        head = lax.axis_index("head")
        plan = self.plan = [PlaneGather(own[:HALF], 1), PlaneGather(own[HALF:], 2)]
        halves = [lax.all_gather(part.own, "head") for part in plan]
        for at in (0, 1, 2):
            owner = functools.reduce(
                lambda value, z: jnp.where(head == z, ROUNDS[at][z], value), range(1, LINE), ROUNDS[at][0]
            )
            for side in (0, 1):
                plan.append(
                    PlaneGather(lax.dynamic_index_in_dim(halves[side], owner, 0, keepdims=False), 1 + side)
                )
        plan[0].first()
        plan[1].first()
        plan[0].second()
        plan[1].second()
        plan[2].first(*plan[1].far)
        plan[0].cores(*plan[1].far)
        plan[1].cores(*plan[1].far)
        plan[4].first(plan[2].x)
        plan[2].second()
        plan[2].cores()
        self.pins += plan[4].second(*plan[2].far)

    def done(self, name, array):
        plan = self.plan
        self.last, self.pins = (array,), []
        if name == "attend0":
            plan[4].cores(array)
            plan[3].first(array)
            plan[5].first(array)
            plan[3].second(array)
            plan[3].cores(array)
            self.pins += plan[5].second(*plan[3].far)
            self.pins += plan[6].first(*plan[3].far)
        if name == "mlp0":
            plan[5].cores(array)
            self.pins += plan[6].second(array)
            self.pins += plan[7].first(array)
        if name == "project0":
            plan[6].cores(array)
            self.pins += plan[7].second(array)
        if name == "attend1":
            plan[7].cores(array)
        if name == "project1":
            self.right = lax.all_gather(after(self.right_root, array), "dp", axis=1, tiled=True)
        self.chains = [chain for chain in self.chains if next(chain, None)]

    def next(self, array):
        return after(array, *self.last, *self.pins)

    def tied(self, array):
        return after(array, *self.last)

    def send(self, array, axis):
        self.pins.append(array)
        return swap(array, axis)

    def place(self, owner, side, head):
        if head == owner:
            return side
        return next(2 + 2 * at + side for at in (0, 1, 2) if ROUNDS[at][head] == owner)

    def group(self, *runs):
        steps = []
        for depth, first, count in runs:
            for block in range(first, first + count):
                owner, at = 2 * depth + block // (2 * HALF), block % (2 * HALF)
                side, at = at // HALF, at % HALF
                places = [self.place(owner, side, head) for head in range(LINE)]
                steps.append(
                    [
                        (
                            [head for head in range(LINE) if places[head] == place],
                            self.plan[place].pieces(at),
                        )
                        for place in sorted(set(places))
                    ]
                )
        return Blocks(steps)

    def add_grads(self, depth, first, pieces):
        chain = self.reduce(depth, first, pieces[:4], pieces[4])
        next(chain)
        self.chains.append(chain)

    def reduce(self, depth, first, mine, theirs):
        count = mine[0].shape[0]
        half = count // 2
        core = self.send(theirs, "core")
        yield True
        far = (self.tied(mine[3]).astype(F32) + core[3].astype(F32)).astype(BF)
        far_x, far_y = self.send(far[:half], "x"), self.send(far[half:], "y")
        yield True
        low = jnp.pad(far_x.astype(F32), ((0, count - half), (0, 0), (0, 0)))
        high = jnp.pad(far_y.astype(F32), ((half, 0), (0, 0), (0, 0)))
        to_x = (self.tied(mine[1]).astype(F32) + core[1].astype(F32) + high).astype(BF)
        to_y = (self.tied(mine[2]).astype(F32) + core[2].astype(F32) + low).astype(BF)
        x, y = self.send(to_x, "x"), self.send(to_y, "y")
        yield True
        total = self.tied(mine[0]).astype(F32) + core[0].astype(F32) + x.astype(F32) + y.astype(F32)
        total = total.astype(BF)
        split = min(max(2 * HALF - first, 0), count)
        runs = [(side, low, high) for side, low, high in ((0, 0, split), (1, split, count)) if low < high]
        totals = [total[low:high] for _, low, high in runs]
        self.pins += totals
        outer, inner, far_in, far_out = (0, 1, 2, 3) if depth == 0 else (3, 2, 1, 0)
        ones = []
        for (side, _, _), part in zip(runs, totals):
            owner = 2 * depth + side
            ones.append(hop(part, (far_out, far_in), (outer if owner == inner else inner, owner)))
        yield True
        for (side, low, high), part, one in zip(runs, totals, ones):
            joined = (self.tied(part).astype(F32) + one.astype(F32)).astype(BF)
            self.pins.append(joined)
            owner = 2 * depth + side
            last = hop(joined, (far_in, owner))
            for at in range(low, high):
                self.parts[depth, first + at] = (joined, last, at - low)
        yield True

    def own_blocks(self, low, high):
        head = lax.axis_index("head")
        own = None
        for owner in range(LINE):
            runs = []
            for at in range(low, high):
                joined, last, block = self.parts[owner // 2, 2 * HALF * (owner % 2) + at]
                if runs and runs[-1][0] is joined:
                    runs[-1][3] = block + 1
                else:
                    runs.append([joined, last, block, block + 1])
            sums = [a[start:stop].astype(F32) + b[start:stop].astype(F32) for a, b, start, stop in runs]
            value = sums[0] if len(sums) == 1 else jnp.concatenate(sums, axis=0)
            own = value if own is None else jnp.where(head == owner, value, own)
        return own

    def finish(self, renew):
        self.last = ()
        while len(self.chains) > 1:
            self.chains = [chain for chain in self.chains if next(chain, None)]
        results = ()
        for low, high in ((HALF, 2 * HALF), (0, HALF)):
            if low == 0:
                while self.chains:
                    self.chains = [chain for chain in self.chains if next(chain, None)]
            own = self.own_blocks(low, high)
            full = PlaneGather(own.astype(BF), 1 + (low == 0))
            full.first()
            full.second()
            full.cores()
            results = renew(
                own,
                Blocks([[(None, full.pieces(at))] for at in range(HALF)]),
                Blocks([[(None, [(self.right, low + at)])] for at in range(HALF)]),
                low,
                results,
            )
        return results

    def vector_sum(self, vectors):
        for axis in ("core", "x", "y"):
            vectors = vectors + swap(vectors, axis)
        for step in (1, 2):
            vectors = vectors + hop(vectors, *((i, i ^ step) for i in range(LINE)))
        return vectors


def on_device(
    image_tokens,
    cotangent,
    weights,
    weights_ema,
    left_stats,
    right_stats,
    left_root,
    right_root,
    vectors,
    vec_first,
    vec_second,
):
    fits = lax.axis_size("dp") == DP and lax.axis_size("head") == LINE
    links = (Permutes if fits else Collectives)(weights, right_root)
    stream = pad_tokens(image_tokens)
    grad = pad_tokens(cotangent)
    saved = []
    top = LAYERS - 1
    for depth in range(LAYERS):
        ln_gain, q_gain, k_gain, mlp_bias, out_bias = split_vector(vectors[depth])
        normed, queries, keys, values, q_unit, q_inv, k_unit, k_inv, attended = attend(
            links.next(stream), ln_gain, q_gain, k_gain, links.group((depth, QKV, 3))
        )
        links.done(f"attend{depth}", attended)
        hidden, slope = mlp_in(links.next(normed), mlp_bias, links.group((depth, MLP, RATIO)))
        links.done(f"mlp{depth}", hidden)
        saved.append(
            (stream, normed, hidden, slope, queries, keys, values, q_unit, q_inv, k_unit, k_inv, attended)
        )
        if depth == top:
            pieces = weight_grads(
                [(links.next(attended), grad, 1), (hidden, grad, RATIO)], links.cut, "grad_out"
            )
            links.done("grad_out", pieces[0])
            links.add_grads(depth, OUT, pieces)
        stream = project(
            links.next(stream), attended, hidden, out_bias, links.group((depth, OUT, OUT_COUNT)), depth == top
        )
        links.done(f"project{depth}", stream)
    block_out = cut_tokens(stream)
    vector_parts = [None] * LAYERS
    for depth in reversed(range(LAYERS)):
        ln_gain, q_gain, k_gain, _, _ = split_vector(vectors[depth])
        stream, normed, hidden, slope, queries, keys, values, q_unit, q_inv, k_unit, k_inv, attended = saved[depth]
        dy, do, du, dbo, dbu = mlp_back(links.next(grad), slope, links.group((depth, OUT, OUT_COUNT)))
        links.done("mlp_back", dy)
        segments = [(links.next(normed), du, RATIO)]
        if depth < top:
            segments += [(attended, dy, 1), (hidden, dy, RATIO)]
        pieces = weight_grads(segments, links.cut, "grad_mlp")
        links.done("grad_mlp", pieces[0])
        links.add_grads(depth, MLP, pieces)
        dqkv, dgq, dgk = attend_back(
            links.next(do), queries, keys, values, q_unit, q_inv, k_unit, k_inv, q_gain, k_gain
        )
        links.done("attend_back", dqkv)
        pieces = weight_grads([(links.next(normed), dqkv, 3)], links.cut, "grad_qkv")
        links.done("grad_qkv", pieces[0])
        links.add_grads(depth, QKV, pieces)
        grad, dg = stream_back(
            links.next(grad), stream, ln_gain, du, dqkv, links.group((depth, MLP, RATIO), (depth, QKV, 3))
        )
        links.done("stream_back", grad)
        vector_parts[depth] = jnp.concatenate(
            [
                dg[0],
                dgq.reshape(HEADS, HEAD_DIM).sum(0),
                dgk.reshape(HEADS, HEAD_DIM).sum(0),
                dbu[0],
                dbo[0],
            ]
        )
    grad_stream = cut_tokens(grad)
    vector_grad = links.vector_sum(jnp.stack(vector_parts))

    def renew(own, full, right, first, earlier):
        return shampoo(
            own, full, right, left_root, left_stats, right_stats, weights, weights_ema, first, earlier
        )

    weight_grad, left_new, right_new, weight_new, ema_new = links.finish(renew)
    first_new = BETA_ONE * vec_first + (1.0 - BETA_ONE) * vector_grad
    second_new = BETA_TWO * vec_second + (1.0 - BETA_TWO) * vector_grad * vector_grad
    first_hat = first_new / (1.0 - BETA_ONE**STEP)
    second_hat = second_new / (1.0 - BETA_TWO**STEP)
    vec_new = vectors - RATE_VEC * first_hat / (jnp.sqrt(second_hat) + ADAM_EPS)
    return (
        block_out,
        grad_stream,
        weight_grad,
        left_new,
        right_new,
        weight_new,
        ema_new,
        first_new,
        second_new,
        vec_new,
    )


def solution(mesh):
    tokens, blocks = P(("dp", "head"), None, None), P("head", "dp", None)
    return jax.shard_map(
        on_device,
        mesh=mesh,
        in_specs=(tokens, tokens) + (blocks,) * 6 + (P(),) * 3,
        out_specs=(tokens, tokens) + (blocks,) * 5 + (P(),) * 3,
        check_vma=False,
    )
```

```python
import functools
import math

import jax
import jax.numpy as jnp
from jax import lax
from jax.experimental import pallas as pl
from jax.experimental.pallas import tpu as pltpu
from jax.sharding import PartitionSpec as P

D = 768
HEADS = 12
HEAD_DIM = 64
FF = 3072
SEQ = 196
PAD = 208
LAYERS = 2
STEP = 10
RATIO = FF // D
IN_COUNT = 3 + RATIO
OUT_COUNT = 1 + RATIO
PER_LAYER = IN_COUNT + OUT_COUNT
PAIR = 2 * HEAD_DIM
TILE = 256

EPS_NORM = 1e-06
BETA_ONE = 0.9
BETA_TWO = 0.95
ADAM_EPS = 1e-08
RATE_VEC = 0.3
RATE_MAT = 0.003
DECAY_MAT = 0.1
STAT_DECAY = 0.5
EMA_DECAY = 0.8
SCALE = HEAD_DIM ** (-0.5)
EXP2_SCALE = SCALE * math.log2(math.e)

BF = jnp.bfloat16
F32 = jnp.float32
NN = (((1,), (0,)), ((), ()))
NT = (((1,), (1,)), ((), ()))
TN = (((0,), (0,)), ((), ()))


def dot(a, b, dims=NN):
    return lax.dot_general(a, b, dims, preferred_element_type=F32)


def call(kernel, grid, operands, in_specs, outs, out_specs, scratch, about_us, name, aliases=None):
    moved = sum(o.size * o.dtype.itemsize for o in operands) + sum(
        math.prod(o.shape) * o.dtype.itemsize for o in outs
    )
    return pl.pallas_call(
        kernel,
        grid=grid,
        in_specs=in_specs,
        out_specs=out_specs,
        out_shape=outs,
        scratch_shapes=scratch,
        compiler_params=pltpu.CompilerParams(vmem_limit_bytes=24 * 1024 * 1024),
        cost_estimate=pl.CostEstimate(flops=int(about_us * 1.1e9), bytes_accessed=moved, transcendentals=0),
        input_output_aliases=aliases or {},
        name=name,
    )(*operands)


def whole(shape):
    return pl.BlockSpec(shape, lambda *ids: (0,) * len(shape))


def sds(shape, dtype):
    return jax.ShapeDtypeStruct(shape, dtype)


WAYS = (0, 1, 2, 3)


class Blocks:
    def __init__(self, steps):
        self.steps = steps
        self.arrays = []
        for places in steps:
            for _, pieces in places:
                for array, _ in pieces:
                    if not any(array is other for other in self.arrays):
                        self.arrays.append(array)
        self.count = len(steps[0][0][1])
        self.specs = [pl.BlockSpec(memory_space=pltpu.HBM)] * len(self.arrays)
        self.scratch = [pltpu.VMEM((2, D, D), BF), pltpu.SemaphoreType.DMA((2, self.count))]

    def bind(self, refs, held, sems):
        self.refs, self.held, self.sems = refs, held, sems

    def copies(self, pieces, slot):
        made = []
        for at, (array, block) in enumerate(pieces):
            ref = next(ref for ref, other in zip(self.refs, self.arrays) if other is array)
            target = self.held.at[slot]
            if self.count > 1:
                rows = array.shape[-2]
                row = piece_row(at % 4, at // 4, rows)
                target = self.held.at[slot, pl.ds(pl.multiple_of(row, 16), rows)]
            made.append(pltpu.make_async_copy(ref.at[block], target, self.sems.at[slot, at]))
        return made

    def start(self, j, wanted):
        head = lax.axis_index("head")
        for step, places in enumerate(self.steps):
            for owners, pieces in places:
                here = wanted == step
                if owners is not None:
                    here = here & functools.reduce(lambda a, b: a | b, [head == owner for owner in owners])

                @pl.when(here)
                def _(step=step, pieces=pieces):
                    for copy in self.copies(pieces, step % 2):
                        copy.start()

    def step(self, j):
        @pl.when(j == 0)
        def _():
            self.start(j, j)

        @pl.when(j + 1 < len(self.steps))
        def _():
            self.start(j, j + 1)

        slot = lax.rem(j, 2)
        for copy in self.copies(self.steps[0][0][1], slot):
            copy.wait()
        return self.held.at[slot]


def piece_row(way, dc, rows):
    me = lax.axis_index("dp")
    core, x, y = lax.rem(me, 2), lax.rem(me // 2, 2), me // 4
    core = 1 - core if dc else core
    dx, dy = ((0, 0), (1 - core, core), (core, 1 - core), (1, 1))[way]
    return ((y + dy - 2 * y * dy) * 4 + (x + dx - 2 * x * dx) * 2 + core) * rows


def row_parts(values):
    average = jnp.mean(values, axis=-1, keepdims=True)
    centred = values - average
    inverse = lax.rsqrt(jnp.mean(centred * centred, axis=-1, keepdims=True) + EPS_NORM)
    return centred * inverse, inverse


def head_mixer():
    row = lax.broadcasted_iota(jnp.int32, (TILE, TILE), 0) // HEAD_DIM
    column = lax.broadcasted_iota(jnp.int32, (TILE, TILE), 1) // HEAD_DIM
    return jnp.where(row == column, 1.0 / HEAD_DIM, 0.0).astype(BF)


def head_mean(values, mixer):
    high = values.astype(BF)
    low = (values - high.astype(F32)).astype(BF)
    return dot(high, mixer) + dot(low, mixer)


def gelu_parts(z):
    decay = jnp.exp2(z * z * (-0.5 * math.log2(math.e)))
    t = 1.0 / (1.0 + (0.3275911 * math.sqrt(0.5)) * jnp.abs(z))
    poly = 0.5 * 1.061405429
    for factor in (-1.453152027, 1.421413741, -0.284496736, 0.254829592):
        poly = poly * t + 0.5 * factor
    tail = poly * t * decay
    share = jnp.where(z >= 0, 1.0 - tail, tail)
    return z * share, share + z * decay * (1.0 / math.sqrt(2.0 * math.pi))


def tiles(rows, columns):
    return [(slice(r, r + PAD), slice(c, c + TILE)) for r in range(0, rows, PAD) for c in range(0, columns, TILE)]


def mlp_in(normed, bias, blocks):
    tokens = normed.shape[0]

    def kernel(h_ref, b_ref, *refs):
        w_refs, (a_ref, s_ref, *fetch) = refs[: len(blocks.arrays)], refs[len(blocks.arrays) :]
        blocks.bind(w_refs, *fetch)
        block = blocks.step(pl.program_id(0))
        spots = tiles(tokens, D)
        wide = [dot(h_ref[rows, :], block[:, columns]) for rows, columns in spots]
        for (rows, columns), z in zip(spots, wide):
            act, slope = gelu_parts(z + b_ref[:, columns])
            a_ref[rows, columns] = act.astype(BF)
            s_ref[rows, columns] = slope.astype(BF)

    return call(
        kernel,
        (RATIO,),
        [normed, bias] + blocks.arrays,
        [whole((tokens, D)), pl.BlockSpec((1, D), lambda j: (0, j))] + blocks.specs,
        [sds((tokens, FF), BF), sds((tokens, FF), BF)],
        [pl.BlockSpec((tokens, D), lambda j: (0, j))] * 2,
        blocks.scratch,
        11.0,
        "mlp_in",
    )


def half_masks(rows):
    low = lax.broadcasted_iota(jnp.int32, (rows, PAIR), 1) < HEAD_DIM
    return low


def split_pair(values, low):
    zero = jnp.zeros_like(values)
    return jnp.where(low, values, zero), jnp.where(low, zero, values)


def split_rows(values, top):
    zero = jnp.zeros_like(values)
    return jnp.where(top, values, zero), jnp.where(top, zero, values)


def qkv_in(stream, ln_gain, gains, blocks):
    tokens = stream.shape[0]

    def kernel(x_ref, g_ref, c_ref, *refs):
        w_refs, (h_ref, n_ref, u_ref, i_ref, *fetch) = refs[: len(blocks.arrays)], refs[len(blocks.arrays) :]
        blocks.bind(w_refs, *fetch)
        j = pl.program_id(0)

        @pl.when(j == 0)
        def _():
            for row in range(0, tokens, PAD):
                rows = slice(row, row + PAD)
                unit, _ = row_parts(x_ref[rows, :].astype(F32))
                h_ref[rows, :] = (unit * g_ref[...]).astype(BF)

        block = blocks.step(j)

        @pl.when(j < 2)
        def _():
            mixer = head_mixer()
            spots = tiles(tokens, D)
            raws = [dot(h_ref[rows, :], block[:, columns]) for rows, columns in spots]
            centred = [raw - head_mean(raw, mixer) for raw in raws]
            spreads = [head_mean(part * part, mixer) for part in centred]
            for (rows, columns), part, spread in zip(spots, centred, spreads):
                inverse = lax.rsqrt(spread + EPS_NORM)
                unit = part * inverse
                n_ref[rows, columns] = (unit * c_ref[0, :, columns]).astype(BF)
                u_ref[rows, columns] = unit.astype(BF)
                i_ref[rows, columns] = inverse

        @pl.when(j == 2)
        def _():
            n_ref[...] = dot(h_ref[...], block[...]).astype(BF)

    first_two = lambda j: (0, jnp.minimum(j, 1))
    return call(
        kernel,
        (3,),
        [stream, ln_gain, gains] + blocks.arrays,
        [
            whole((tokens, D)),
            whole((1, D)),
            pl.BlockSpec((1, 1, D), lambda j: (jnp.minimum(j, 1), 0, 0)),
        ]
        + blocks.specs,
        [
            sds((tokens, D), BF),
            sds((tokens, 3 * D), BF),
            sds((tokens, 2 * D), BF),
            sds((tokens, 2 * D), F32),
        ],
        [
            whole((tokens, D)),
            pl.BlockSpec((tokens, D), lambda j: (0, j)),
            pl.BlockSpec((tokens, D), first_two),
            pl.BlockSpec((tokens, D), first_two),
        ],
        blocks.scratch,
        9.0,
        "qkv_in",
    )


def attend(qkv):
    tokens = qkv.shape[0]

    def kernel(z_ref, o_ref):
        low = half_masks(PAD)
        valid = lax.broadcasted_iota(jnp.int32, (PAD, PAD), 1) < SEQ
        raw = []
        for at in range(0, D, PAIR):
            keys = z_ref[:, D + at : D + at + PAIR]
            raw += [dot(query, keys, NT) for query in split_pair(z_ref[:, at : at + PAIR], low)]
        raised = [jnp.where(valid, jnp.exp2(part * EXP2_SCALE), 0.0) for part in raw]
        shares = [1.0 / jnp.sum(part, axis=1, keepdims=True) for part in raised]
        for pair, at in enumerate(range(0, D, PAIR)):
            values = z_ref[:, 2 * D + at : 2 * D + at + PAIR]
            sides = [dot(raised[n].astype(BF), values) * shares[n] for n in (2 * pair, 2 * pair + 1)]
            o_ref[:, at : at + PAIR] = jnp.where(low, sides[0], sides[1]).astype(BF)

    return call(
        kernel,
        (tokens // PAD,),
        [qkv],
        [pl.BlockSpec((PAD, 3 * D), lambda i: (i, 0))],
        [sds((tokens, D), BF)],
        [pl.BlockSpec((PAD, D), lambda i: (i, 0))],
        [],
        8.0,
        "attend",
    )[0]


def project(stream, attended, hidden, bias, blocks, last):
    tokens = stream.shape[0]

    def kernel(x_ref, o_ref, a_ref, b_ref, *refs):
        w_refs, (y_ref, total, x_held, x_sem, *fetch) = refs[: len(blocks.arrays)], refs[len(blocks.arrays) :]
        blocks.bind(w_refs, *fetch)
        j = pl.program_id(0)
        x_copy = pltpu.make_async_copy(x_ref, x_held, x_sem)
        block = blocks.step(j)

        @pl.when(j == 0)
        def _():
            x_copy.start()
            total[...] = dot(o_ref[...], block[...])

        @pl.when((j > 0) & (j < OUT_COUNT - 1))
        def _():
            total[...] += dot(a_ref[...], block[...])

        @pl.when(j == OUT_COUNT - 1)
        def _():
            x_copy.wait()
            for rows, columns in tiles(tokens, D):
                y_ref[rows, columns] = (
                    total[rows, columns]
                    + (x_held[rows, columns].astype(F32) + b_ref[:, columns])
                    + dot(a_ref[rows, :], block[:, columns])
                ).astype(y_ref.dtype)

    return call(
        kernel,
        (OUT_COUNT,),
        [stream, attended, hidden, bias] + blocks.arrays,
        [
            pl.BlockSpec(memory_space=pl.ANY),
            whole((tokens, D)),
            pl.BlockSpec((tokens, D), lambda j: (0, jnp.maximum(j - 1, 0))),
            whole((1, D)),
        ]
        + blocks.specs,
        [sds((tokens, D), BF if last else F32)],
        [whole((tokens, D))],
        [pltpu.VMEM((tokens, D), F32), pltpu.VMEM((tokens, D), stream.dtype), pltpu.SemaphoreType.DMA]
        + blocks.scratch,
        8.0,
        "project",
    )[0]


def mlp_back(grad, slope, blocks):
    tokens = grad.shape[0]

    def kernel(g_ref, s_ref, *refs):
        w_refs, refs = refs[: len(blocks.arrays)], refs[len(blocks.arrays) :]
        dy_ref, do_ref, du_ref, dbo_ref, dbu_ref, *fetch = refs
        blocks.bind(w_refs, *fetch)
        j = pl.program_id(0)

        @pl.when(j == 0)
        def _():
            dy = g_ref[...].astype(BF)
            dy_ref[...] = dy
            dbo_ref[...] = jnp.sum(dy.astype(F32), axis=0, keepdims=True)

        block = blocks.step(j)

        @pl.when(j == 0)
        def _():
            do_ref[...] = dot(dy_ref[...], block[...], NT).astype(BF)

        @pl.when(j > 0)
        def _():
            du = (dot(dy_ref[...], block[...], NT) * s_ref[...].astype(F32)).astype(BF)
            du_ref[...] = du
            dbu_ref[...] = jnp.sum(du.astype(F32), axis=0, keepdims=True)

    shifted = pl.BlockSpec((tokens, D), lambda j: (0, jnp.maximum(j - 1, 0)))
    return call(
        kernel,
        (OUT_COUNT,),
        [grad, slope] + blocks.arrays,
        [whole((tokens, D)), shifted] + blocks.specs,
        [
            sds((tokens, D), BF),
            sds((tokens, D), BF),
            sds((tokens, FF), BF),
            sds((1, D), F32),
            sds((1, FF), F32),
        ],
        [
            whole((tokens, D)),
            whole((tokens, D)),
            shifted,
            whole((1, D)),
            pl.BlockSpec((1, D), lambda j: (0, jnp.maximum(j - 1, 0))),
        ],
        blocks.scratch,
        9.0,
        "mlp_back",
    )


def attend_back(grad_o, qkv, unit, inverse, gains):
    tokens = grad_o.shape[0]

    def kernel(do_ref, z_ref, u_ref, i_ref, c_ref, dz_ref, dc_ref):
        low = half_masks(PAD)
        valid = lax.broadcasted_iota(jnp.int32, (PAD, PAD), 0) < SEQ
        top = lax.broadcasted_iota(jnp.int32, (PAIR, PAD), 0) < HEAD_DIM
        mixer = head_mixer()

        @pl.when(pl.program_id(0) == 0)
        def _():
            dc_ref[...] = jnp.zeros_like(dc_ref)

        def norm_back(grad, which, columns):
            at = slice(which * D + columns.start, which * D + columns.stop)
            hats = u_ref[:, at].astype(F32)
            dc_ref[which, :, columns] += jnp.sum(grad * hats, axis=0, keepdims=True)
            pull = grad * c_ref[which, :, columns]
            dz_ref[:, at] = (
                i_ref[:, at] * (pull - head_mean(pull, mixer) - hats * head_mean(pull * hats, mixer))
            ).astype(BF)

        for tile in range(0, D, 768):
            grads_q, grads_k = [], []
            pairs = range(tile, tile + 768, PAIR)
            raw, pulled, keys_t = [], [], []
            for at in pairs:
                query, key, value = (z_ref[:, side + at : side + at + PAIR] for side in (0, D, 2 * D))
                grad = do_ref[:, at : at + PAIR]
                keys_t.append(key.T)
                for query_t, grad_t in zip(split_rows(query.T, top), split_rows(grad.T, top)):
                    raw.append(dot(key, query_t))
                    pulled.append(dot(value, grad_t))
            probs, scores = [], []
            for part, pull in zip(raw, pulled):
                raised = jnp.exp2(part * EXP2_SCALE)
                raised = jnp.where(valid, raised, 0.0)
                share = raised * (1.0 / jnp.sum(raised, axis=0, keepdims=True))
                mixed = share * pull
                row_dot = jnp.sum(mixed, axis=0, keepdims=True)
                probs.append(share.astype(BF))
                scores.append((mixed - share * row_dot).astype(BF))
            for n, at in enumerate(pairs):
                query, grad = z_ref[:, at : at + PAIR], do_ref[:, at : at + PAIR]
                both_v = dot(jnp.concatenate(probs[2 * n : 2 * n + 2], axis=0), grad)
                both_k = dot(jnp.concatenate(scores[2 * n : 2 * n + 2], axis=0), query)
                turned = [
                    dot(keys_t[n][h * HEAD_DIM : (h + 1) * HEAD_DIM], scores[2 * n + h]) for h in (0, 1)
                ]
                grads_q.append((jnp.concatenate(turned, axis=0) * SCALE).astype(BF).T.astype(F32))
                grads_k.append((jnp.where(low, both_k[:PAD], both_k[PAD:]) * SCALE).astype(BF).astype(F32))
                dz_ref[:, 2 * D + at : 2 * D + at + PAIR] = jnp.where(low, both_v[:PAD], both_v[PAD:]).astype(BF)
            for k in range(0, 768, TILE):
                n = k // PAIR
                norm_back(jnp.concatenate(grads_q[n : n + 2], axis=1), 0, slice(tile + k, tile + k + TILE))
                norm_back(jnp.concatenate(grads_k[n : n + 2], axis=1), 1, slice(tile + k, tile + k + TILE))

    def per_image(columns):
        return pl.BlockSpec((PAD, columns), lambda i: (i, 0))

    return call(
        kernel,
        (tokens // PAD,),
        [grad_o, qkv, unit, inverse, gains],
        [per_image(D), per_image(3 * D), per_image(2 * D), per_image(2 * D), whole((2, 1, D))],
        [sds((tokens, 3 * D), BF), sds((2, 1, D), F32)],
        [per_image(3 * D), whole((2, 1, D))],
        [],
        14.0,
        "attend_back",
    )


def weight_grads(segments, cut, name):
    total = sum(count for _, _, count in segments)
    operands, specs, start = [], [], 0
    for left, right, count in segments:
        for side in (left, right):
            side, first, last = (*side, count - 1) if isinstance(side, tuple) else (side, 0, 0)
            tokens = side.shape[0]
            index = functools.partial(
                lambda at, first, last, j: (0, first + jnp.clip(j - at, 0, last)), start, first, last
            )
            operands.append(side)
            specs.append(pl.BlockSpec((tokens, D), index))
        start += count

    def kernel(*refs):
        ins, outs = refs[: len(operands)], refs[len(operands) :]
        j = pl.program_id(0)
        slot = lax.rem(j, 2)

        def leave(block, slot):
            *mine, theirs, held, sems = outs
            rows = D // 8
            copies = []
            for way in WAYS:
                for core, target in enumerate((mine[way].at[block], theirs.at[way, block])):
                    row = pl.multiple_of(piece_row(way, core, rows), 16)
                    copies.append(
                        pltpu.make_async_copy(held.at[slot, pl.ds(row, rows)], target, sems.at[slot, core, way])
                    )
            return copies

        if cut:

            @pl.when(j >= 2)
            def _():
                for copy in leave(j - 2, slot):
                    copy.wait()

        start = 0
        for at, (_, _, count) in enumerate(segments):

            def body(at=at):
                value = dot(ins[2 * at][...], ins[2 * at + 1][...], TN).astype(BF)
                if cut:
                    outs[5][slot] = value
                else:
                    outs[0][0] = value

            if count == total:
                body()
            else:
                pl.when((j >= start) & (j < start + count))(body)
            start += count
        if cut:
            for copy in leave(j, slot):
                copy.start()

            @pl.when(j == total - 1)
            def _():
                if total > 1:
                    for copy in leave(j - 1, 1 - slot):
                        copy.wait()
                for copy in leave(j, slot):
                    copy.wait()

    if cut:
        shapes = [pltpu.HBM((total, D // 8, D), BF)] * 4 + [pltpu.HBM((4, total, D // 8, D), BF)]
        out_specs = [pl.BlockSpec(memory_space=pl.ANY)] * 5
    else:
        shapes = [sds((total, D, D), BF)]
        out_specs = [pl.BlockSpec((1, D, D), lambda j: (j, 0, 0))]
    return list(call(
        kernel,
        (total,),
        operands,
        specs,
        shapes,
        out_specs,
        [pltpu.VMEM((2, D, D), BF), pltpu.SemaphoreType.DMA((2, 2, 4))] if cut else [],
        1.0 + 1.4 * total,
        name,
    ))


def stream_back(grad, stream, gain, grad_u, grad_qkv, blocks):
    tokens = grad.shape[0]

    def kernel(g_ref, x_ref, c_ref, du_ref, dz_ref, *refs):
        w_refs, refs = refs[: len(blocks.arrays)], refs[len(blocks.arrays) :]
        out_ref, dg_ref, total, g_held, x_held, sems, *fetch = refs
        blocks.bind(w_refs, *fetch)
        j = pl.program_id(0)
        late = [
            pltpu.make_async_copy(g_ref, g_held, sems.at[0]),
            pltpu.make_async_copy(x_ref, x_held, sems.at[1]),
        ]
        block = blocks.step(j)

        @pl.when(j == 0)
        def _():
            for copy in late:
                copy.start()
            total[...] = dot(du_ref[...], block[...], NT)

        @pl.when((j > 0) & (j < RATIO))
        def _():
            total[...] += dot(du_ref[...], block[...], NT)

        @pl.when(j >= RATIO)
        def _():
            total[...] += dot(dz_ref[...], block[...], NT)

        @pl.when(j == IN_COUNT - 1)
        def _():
            for copy in late:
                copy.wait()
            sums = 0.0
            for row in range(0, tokens, PAD // 2):
                rows = slice(row, row + PAD // 2)
                unit, inverse = row_parts(x_held[rows, :].astype(F32))
                grad_h = total[rows, :]
                sums = sums + jnp.sum(grad_h * unit, axis=0, keepdims=True)
                hat = grad_h * c_ref[...]
                out_ref[rows, :] = g_held[rows, :].astype(F32) + inverse * (
                    hat
                    - jnp.mean(hat, axis=-1, keepdims=True)
                    - unit * jnp.mean(hat * unit, axis=-1, keepdims=True)
                )
            dg_ref[...] = sums

    return call(
        kernel,
        (IN_COUNT,),
        [grad, stream, gain, grad_u, grad_qkv] + blocks.arrays,
        [
            pl.BlockSpec(memory_space=pl.ANY),
            pl.BlockSpec(memory_space=pl.ANY),
            whole((1, D)),
            pl.BlockSpec((tokens, D), lambda j: (0, jnp.minimum(j, RATIO - 1))),
            pl.BlockSpec((tokens, D), lambda j: (0, jnp.maximum(j - RATIO, 0))),
        ]
        + blocks.specs,
        [sds((tokens, D), F32), sds((1, D), F32)],
        [whole((tokens, D)), whole((1, D))],
        [
            pltpu.VMEM((tokens, D), F32),
            pltpu.VMEM((tokens, D), grad.dtype),
            pltpu.VMEM((tokens, D), stream.dtype),
            pltpu.SemaphoreType.DMA((2,)),
        ]
        + blocks.scratch,
        12.0,
        "stream_back",
    )


def shampoo(grad, full, right, left_root, left_stats, right_stats, weights, ema, first, earlier):
    count, rows, _ = grad.shape

    def kernel(g_ref, lr_ref, ls_ref, rs_ref, w_ref, e_ref, *refs):
        f_refs, refs = refs[: len(full.arrays)], refs[len(full.arrays) :]
        r_refs, refs = refs[: len(right.arrays)], refs[len(right.arrays) + len(earlier) :]
        go_ref, lo_ref, ro_ref, wo_ref, eo_ref, f_held, f_sems, r_held, r_sems = refs
        full.bind(f_refs, f_held, f_sems)
        right.bind(r_refs, r_held, r_sems)
        j = pl.program_id(0)
        at = lax.axis_index("dp") * rows
        block = full.step(j)[...]
        right_block = right.step(j)[...]
        go_ref[0] = g_ref[0]
        gram = dot(g_ref[0].astype(BF), block, NT)
        lo_ref[0] = STAT_DECAY * ls_ref[0] + (1.0 - STAT_DECAY) * gram
        pick = (
            lax.broadcasted_iota(jnp.int32, (rows, D), 1)
            == lax.broadcasted_iota(jnp.int32, (rows, D), 0) + at
        )
        columns = dot(jnp.where(pick, 1.0, 0.0).astype(BF), block, NT).astype(BF)
        ro_ref[0] = STAT_DECAY * rs_ref[0] + (1.0 - STAT_DECAY) * dot(columns, block)
        lifted = dot(lr_ref[0].astype(BF), block).astype(BF)
        precond = dot(lifted, right_block)
        renewed = w_ref[0] * (1.0 - RATE_MAT * DECAY_MAT) - RATE_MAT * precond
        wo_ref[0] = renewed
        eo_ref[0] = EMA_DECAY * e_ref[0] + (1.0 - EMA_DECAY) * renewed

    part = pl.BlockSpec((1, rows, D), lambda j: (j, 0, 0))
    own = pl.BlockSpec((1, rows, D), lambda j: (first + j, 0, 0))
    inputs = [grad, left_root, left_stats, right_stats, weights, ema] + full.arrays + right.arrays
    return call(
        kernel,
        (count,),
        inputs + list(earlier),
        [part] + [own] * 5 + full.specs + right.specs + [pl.BlockSpec(memory_space=pl.ANY)] * len(earlier),
        [sds(weights.shape, F32)] * 5,
        [own] * 5,
        full.scratch + right.scratch,
        2.0 + 3.0 * count,
        "shampoo",
        {len(inputs) + at: at for at in range(len(earlier))},
    )


def split_vector(row_vec):
    ends = (D, D + HEAD_DIM, D + 2 * HEAD_DIM, D + 2 * HEAD_DIM + FF)
    ln_gain, q_gain, k_gain, mlp_bias, out_bias = jnp.split(row_vec, ends)
    return (
        ln_gain[None],
        jnp.stack([jnp.tile(q_gain, HEADS)[None], jnp.tile(k_gain, HEADS)[None]]),
        mlp_bias[None],
        out_bias[None],
    )


def pad_tokens(array):
    return jnp.pad(array, ((0, 0), (0, PAD - SEQ), (0, 0))).reshape(-1, D)


def cut_tokens(array):
    return array.reshape(-1, PAD, D)[:, :SEQ]


QKV, MLP, OUT = 0, 3, IN_COUNT
SIZES = {QKV: 3, MLP: RATIO, OUT: OUT_COUNT}


class Collectives:
    cut = False

    def __init__(self, weights, right_root):
        rows = lax.all_gather(weights.astype(BF), "head", axis=0, tiled=True)
        self.blocks = lax.all_gather(rows, "dp", axis=1, tiled=True)
        self.right = lax.all_gather(right_root.astype(BF), "dp", axis=1, tiled=True)
        self.count = weights.shape[0]
        self.parts = {}

    def group(self, *runs):
        return Blocks(
            [
                [(None, [(self.blocks, depth * PER_LAYER + first + at)])]
                for depth, first, count in runs
                for at in range(count)
            ]
        )

    def next(self, array):
        return array

    def done(self, name, array):
        return array

    def add_grads(self, depth, first, pieces):
        self.parts[depth, first] = pieces[0]

    def finish(self, renew):
        partial = jnp.concatenate([self.parts[key] for key in sorted(self.parts)], axis=0)
        rows = lax.psum_scatter(partial, "dp", scatter_dimension=1, tiled=True)
        own = lax.psum_scatter(rows, "head", scatter_dimension=0, tiled=True)
        full = lax.all_gather(own, "dp", axis=1, tiled=True)
        full, right = (
            Blocks([[(None, [(array, at)])] for at in range(self.count)]) for array in (full, self.right)
        )
        return renew(own.astype(F32), full, right, 0, ())

    def vector_sum(self, vectors):
        return lambda: lax.psum(vectors, ("dp", "head"))


DP, LINE = 8, 4
HALF = 3
STEPS = {"core": (1, 1), "x": (2, 2), "y": (4, 4), "first": (2, 4), "second": (4, 2)}
ROUNDS = ((2, 0, 0, 0), (1, 2, 1, 1), (3, 3, 3, 2))


def swap(array, axis):
    return lax.ppermute(array, "dp", [(i, i ^ STEPS[axis][i % 2]) for i in range(DP)])


def hop(array, *pairs):
    return lax.ppermute(array, "head", pairs)


def along(axis):
    return functools.partial(swap, axis=axis)


def over(*pairs):
    return lambda array: hop(array, *pairs)


class PlaneGather:
    def __init__(self, own):
        self.own = own

    def steps(self):
        own = self.own
        first, second, core = along("first"), along("second"), along("core")
        one, two = yield [(own, first), (own, second)]
        three, *others = yield [(one, second), (own, core), (one, core)]
        more = yield [(two, core), (three, core)]
        self.chips = [own, one, two, three]
        self.others = others + more
        self.chips, self.others = (
            [pltpu.with_memory_space_constraint(array, pltpu.HBM) for array in arrays]
            for arrays in (self.chips, self.others)
        )
        yield []

    def pieces(self, at):
        return [(chip, at) for chip in self.chips + self.others]


STEPS_AFTER = {
    "qkv0": [["place4", "line1", "place3"]],
    "attend0": [["place3", "place4", "place5"], ["place3", "place5"], ["place3", "place6"]],
    "mlp0": [["place5", "place6", "place7"], ["place5"]],
    "project0": [["place6", "place7"], ["place6"]],
    "qkv1": [["place7", "right0"]],
    "attend1": [["place7"]],
    "mlp1": [["right0", "right1"]],
    "project1": [["out1", "right0", "right1"]],
    "mlp_back1": [["right0", "right1"]],
    "grad_mlp1": [["out1", "right1"]],
    "attend_back1": [["out1", "mlp1"]],
    "stream_back1": [["out1", "mlp1", "qkv1"]],
    "mlp_back0": [["mlp1"]],
    "grad_out0": [["out1", "mlp1", "qkv1"]],
    "grad_mlp0": [["out0", "qkv1"]],
    "attend_back0": [["mlp1", "qkv1"]],
    "grad_qkv0": [["out0", "mlp0", "qkv1"]],
    "stream_back0": [["out0", "qkv0"]],
}
FIRST_STEPS = [
    ["line0", "line1"],
    ["place0", "place1"],
    ["place0"],
    ["place1"],
    ["place0", "place1", "line0", "place2"],
    ["place0", "place1", "place2", "place4"],
    ["place2"],
    ["place2", "place4"],
]
LAST_STEPS = [
    ["mlp0"],
    ["qkv0", "sums"],
    ["mlp0", "sums"],
    ["qkv0", "out0", "sums"],
    ["mlp0"],
    ["qkv0"],
    ["out0", "mlp0", "full3"],
    ["qkv0", "full0"],
    ["full3", "sums"],
    ["full3", "full0", "sums"],
    ["full3", "full0", "sums"],
    ["full0"],
]


class Permutes:
    cut = True

    def __init__(self, weights, right_root):
        self.parts, self.chains, self.asked, self.sent = {}, {}, {}, {}
        own = weights.astype(BF)
        right_root = right_root.astype(BF)
        self.plan = [PlaneGather(own[:HALF]), PlaneGather(own[HALF:])] + [PlaneGather(None) for _ in range(6)]
        self.right = [PlaneGather(right_root[:HALF]), PlaneGather(right_root[HALF:])]
        for at, part in enumerate(self.plan):
            self.chains[f"place{at}"] = part.steps()
        for side in (0, 1):
            self.chains[f"line{side}"] = self.gather_line(side)
            self.chains[f"right{side}"] = self.right[side].steps()
        for group in FIRST_STEPS:
            self.step(group)

    def gather_line(self, side):
        (halves,) = yield [(self.plan[side].own, lambda array: lax.all_gather(array, "head"))]
        head = lax.axis_index("head")
        for at in (0, 1, 2):
            owner = functools.reduce(
                lambda value, z: jnp.where(head == z, ROUNDS[at][z], value), range(1, LINE), ROUNDS[at][0]
            )
            self.plan[2 + 2 * at + side].own = lax.dynamic_index_in_dim(halves, owner, 0, keepdims=False)
        yield []

    def send(self, array=None):
        names = [name for name in self.asked if name not in self.sent]
        asked = [entry for name in names for entry in self.asked[name]]
        operands = [operand for operand, _ in asked]
        if array is not None and operands:
            array, *operands = lax.optimization_barrier((array, *operands))
        for name in names:
            self.sent[name] = [how(operands.pop(0)) for _, how in self.asked[name]]
        return array

    def step(self, group, event=None):
        if any(name in self.asked and name not in self.sent for name in group):
            self.send()
        arrived = [array for name in group for array in self.sent.get(name, [])]
        if arrived:
            event, *arrived = (
                lax.optimization_barrier((event, *arrived))
                if event is not None
                else (None, *lax.optimization_barrier(tuple(arrived)))
            )
        for name in group:
            chain = self.chains[name]
            if name in self.sent:
                self.asked[name] = chain.send([arrived.pop(0) for _ in self.sent.pop(name)])
            else:
                self.asked[name] = next(chain)
        return event

    def done(self, name, array):
        for group in STEPS_AFTER.get(name, ()):
            array = self.step(group, array)
        return array

    def next(self, array):
        return self.send(array)

    def place(self, owner, side, head):
        if head == owner:
            return side
        return next(2 + 2 * at + side for at in (0, 1, 2) if ROUNDS[at][head] == owner)

    def group(self, *runs):
        steps = []
        for depth, first, count in runs:
            for block in range(first, first + count):
                owner, at = 2 * depth + block // (2 * HALF), block % (2 * HALF)
                side, at = at // HALF, at % HALF
                places = [self.place(owner, side, head) for head in range(LINE)]
                steps.append(
                    [
                        (
                            [head for head in range(LINE) if places[head] == place],
                            self.plan[place].pieces(at),
                        )
                        for place in sorted(set(places))
                    ]
                )
        return Blocks(steps)

    def add_grads(self, depth, first, pieces):
        name = {QKV: "qkv", MLP: "mlp"}.get(first, "out") + str(depth)
        self.chains[name] = self.reduce(depth, first, pieces[:4], pieces[4])
        self.step([name])

    def reduce(self, depth, first_block, mine, theirs):
        count = mine[0].shape[0]
        first, second = along("first"), along("second")
        (core,) = yield [(theirs, along("core"))]
        far, to_two = ((mine[way].astype(F32) + core[way].astype(F32)).astype(BF) for way in (3, 2))
        far, two = yield [(far, second), (to_two, second)]
        to_one = (mine[1].astype(F32) + core[1].astype(F32) + far.astype(F32)).astype(BF)
        (one,) = yield [(to_one, first)]
        total = mine[0].astype(F32) + core[0].astype(F32) + one.astype(F32) + two.astype(F32)
        total = total.astype(BF)
        split = min(max(2 * HALF - first_block, 0), count)
        runs = [(side, low, high) for side, low, high in ((0, 0, split), (1, split, count)) if low < high]
        parts = [total[low:high] for _, low, high in runs]
        outer, inner, far_in, far_out = (0, 1, 2, 3) if depth == 0 else (3, 2, 1, 0)
        owners = [2 * depth + side for side, _, _ in runs]
        arrived = yield [
            (part, over((far_out, far_in), (outer if owner == inner else inner, owner)))
            for part, owner in zip(parts, owners)
        ]
        parts = [(part.astype(F32) + other.astype(F32)).astype(BF) for part, other in zip(parts, arrived)]
        arrived = yield [(part, over((far_in, owner))) for part, owner in zip(parts, owners)]
        for (_, low, high), part, other in zip(runs, parts, arrived):
            part = part.astype(F32) + other.astype(F32)
            for at in range(low, high):
                self.parts[depth, first_block + at] = (part, at - low)
        yield []

    def own_blocks(self, low, high):
        head = lax.axis_index("head")
        own = None
        for owner in range(LINE):
            runs = []
            for at in range(low, high):
                part, block = self.parts[owner // 2, 2 * HALF * (owner % 2) + at]
                if runs and runs[-1][0] is part:
                    runs[-1][2] = block + 1
                else:
                    runs.append([part, block, block + 1])
            values = [part[start:stop] for part, start, stop in runs]
            value = values[0] if len(values) == 1 else jnp.concatenate(values, axis=0)
            own = value if own is None else jnp.where(head == owner, value, own)
        return own

    def finish(self, renew):
        self.full = {}
        for low in (HALF, 0):
            self.chains[f"full{low}"] = self.gather_own(low)
        for group in LAST_STEPS:
            self.step(group)
        results = ()
        for low in (HALF, 0):
            own, full = self.full[low]
            results = renew(
                own,
                Blocks([[(None, full.pieces(at))] for at in range(HALF)]),
                Blocks([[(None, self.right[low // HALF].pieces(at))] for at in range(HALF)]),
                low,
                results,
            )
        return results

    def gather_own(self, low):
        own = self.own_blocks(low, low + HALF)
        full = PlaneGather(own.astype(BF))
        self.full[low] = own, full
        yield from full.steps()

    def vector_sum(self, vectors):
        self.chains["sums"] = self.sum_vectors(vectors)
        return lambda: self.summed

    def sum_vectors(self, vectors):
        for axis in ("core", "x", "y"):
            (other,) = yield [(vectors, along(axis))]
            vectors = vectors + other
        for step in (1, 2):
            (other,) = yield [(vectors, over(*((i, i ^ step) for i in range(LINE))))]
            vectors = vectors + other
        self.summed = vectors
        yield []


def on_device(
    image_tokens,
    cotangent,
    weights,
    weights_ema,
    left_stats,
    right_stats,
    left_root,
    right_root,
    vectors,
    vec_first,
    vec_second,
):
    fits = lax.axis_size("dp") == DP and lax.axis_size("head") == LINE
    links = (Permutes if fits else Collectives)(weights, right_root)
    stream = pad_tokens(image_tokens)
    grad = pad_tokens(cotangent)
    saved = []
    top = LAYERS - 1
    for depth in range(LAYERS):
        ln_gain, gains, mlp_bias, out_bias = split_vector(vectors[depth])
        normed, qkv, unit, inverse = qkv_in(
            links.next(stream), ln_gain, gains, links.group((depth, QKV, 3))
        )
        qkv = links.done(f"qkv{depth}", qkv)
        attended = attend(links.next(qkv))
        attended = links.done(f"attend{depth}", attended)
        hidden, slope = mlp_in(links.next(normed), mlp_bias, links.group((depth, MLP, RATIO)))
        hidden = links.done(f"mlp{depth}", hidden)
        saved.append((stream, normed, hidden, slope, qkv, unit, inverse, attended))
        if depth == top:
            pieces = weight_grads(
                [(links.next(attended), grad, 1), ((hidden, 0), grad, RATIO)], links.cut, "grad_out"
            )
            pieces[0] = links.done(f"grad_out{depth}", pieces[0])
            links.add_grads(depth, OUT, pieces)
        stream = project(
            links.next(stream), attended, hidden, out_bias, links.group((depth, OUT, OUT_COUNT)), depth == top
        )
        stream = links.done(f"project{depth}", stream)
    block_out = cut_tokens(stream)
    vector_parts = [None] * LAYERS
    for depth in reversed(range(LAYERS)):
        ln_gain, gains, _, _ = split_vector(vectors[depth])
        stream, normed, hidden, slope, qkv, unit, inverse, attended = saved[depth]
        dy, do, du, dbo, dbu = mlp_back(links.next(grad), slope, links.group((depth, OUT, OUT_COUNT)))
        dy = links.done(f"mlp_back{depth}", dy)
        share = RATIO if depth == top else RATIO - 1
        if depth < top:
            segments = [(normed, (du, share), RATIO - share), (links.next(attended), dy, 1), ((hidden, 0), dy, RATIO)]
            pieces = weight_grads(segments, links.cut, "grad_out")
            pieces[0] = links.done(f"grad_out{depth}", pieces[0])
            links.add_grads(depth, MLP + share, pieces)
        pieces = weight_grads([(links.next(normed), (du, 0), share)], links.cut, "grad_mlp")
        pieces[0] = links.done(f"grad_mlp{depth}", pieces[0])
        links.add_grads(depth, MLP, pieces)
        dqkv, dgains = attend_back(links.next(do), qkv, unit, inverse, gains)
        dqkv = links.done(f"attend_back{depth}", dqkv)
        pieces = weight_grads([(links.next(normed), (dqkv, 0), 3)], links.cut, "grad_qkv")
        pieces[0] = links.done(f"grad_qkv{depth}", pieces[0])
        links.add_grads(depth, QKV, pieces)
        grad, dg = stream_back(
            links.next(grad), stream, ln_gain, du, dqkv, links.group((depth, MLP, RATIO), (depth, QKV, 3))
        )
        grad = links.done(f"stream_back{depth}", grad)
        vector_parts[depth] = jnp.concatenate(
            [
                dg[0],
                dgains.reshape(2, HEADS, HEAD_DIM).sum(1).reshape(-1),
                dbu[0],
                dbo[0],
            ]
        )
    grad_stream = cut_tokens(grad)
    vector_sum = links.vector_sum(jnp.stack(vector_parts))

    def renew(own, full, right, first, earlier):
        return shampoo(
            own, full, right, left_root, left_stats, right_stats, weights, weights_ema, first, earlier
        )

    weight_grad, left_new, right_new, weight_new, ema_new = links.finish(renew)
    vector_grad = vector_sum()
    first_new = BETA_ONE * vec_first + (1.0 - BETA_ONE) * vector_grad
    second_new = BETA_TWO * vec_second + (1.0 - BETA_TWO) * vector_grad * vector_grad
    first_hat = first_new / (1.0 - BETA_ONE**STEP)
    second_hat = second_new / (1.0 - BETA_TWO**STEP)
    vec_new = vectors - RATE_VEC * first_hat / (jnp.sqrt(second_hat) + ADAM_EPS)
    return (
        block_out,
        grad_stream,
        weight_grad,
        left_new,
        right_new,
        weight_new,
        ema_new,
        first_new,
        second_new,
        vec_new,
    )


def solution(mesh):
    tokens, blocks = P(("dp", "head"), None, None), P("head", "dp", None)
    return jax.shard_map(
        on_device,
        mesh=mesh,
        in_specs=(tokens, tokens) + (blocks,) * 6 + (P(),) * 3,
        out_specs=(tokens, tokens) + (blocks,) * 5 + (P(),) * 3,
        check_vma=False,
    )
```

```python
import functools
import math

import jax
import jax.numpy as jnp
from jax import lax
from jax.experimental import pallas as pl
from jax.experimental.pallas import tpu as pltpu
from jax.sharding import PartitionSpec as P

D = 768
HEADS = 12
HEAD_DIM = 64
FF = 3072
SEQ = 196
PAD = 208
LAYERS = 2
STEP = 10
RATIO = FF // D
IN_COUNT = 3 + RATIO
OUT_COUNT = 1 + RATIO
PER_LAYER = IN_COUNT + OUT_COUNT
PAIR = 2 * HEAD_DIM
TILE = 256

EPS_NORM = 1e-06
BETA_ONE = 0.9
BETA_TWO = 0.95
ADAM_EPS = 1e-08
RATE_VEC = 0.3
RATE_MAT = 0.003
DECAY_MAT = 0.1
STAT_DECAY = 0.5
EMA_DECAY = 0.8
SCALE = HEAD_DIM ** (-0.5)
EXP2_SCALE = SCALE * math.log2(math.e)

BF = jnp.bfloat16
F32 = jnp.float32
NN = (((1,), (0,)), ((), ()))
NT = (((1,), (1,)), ((), ()))
TN = (((0,), (0,)), ((), ()))


def dot(a, b, dims=NN):
    return lax.dot_general(a, b, dims, preferred_element_type=F32)


def call(kernel, grid, operands, in_specs, outs, out_specs, scratch, about_us, name, aliases=None):
    moved = sum(o.size * o.dtype.itemsize for o in operands) + sum(
        math.prod(o.shape) * o.dtype.itemsize for o in outs
    )
    return pl.pallas_call(
        kernel,
        grid=grid,
        in_specs=in_specs,
        out_specs=out_specs,
        out_shape=outs,
        scratch_shapes=scratch,
        compiler_params=pltpu.CompilerParams(vmem_limit_bytes=24 * 1024 * 1024),
        cost_estimate=pl.CostEstimate(flops=int(about_us * 1.1e9), bytes_accessed=moved, transcendentals=0),
        input_output_aliases=aliases or {},
        name=name,
    )(*operands)


def whole(shape):
    return pl.BlockSpec(shape, lambda *ids: (0,) * len(shape))


def sds(shape, dtype):
    return jax.ShapeDtypeStruct(shape, dtype)


WAYS = (0, 1, 2, 3)


class Blocks:
    def __init__(self, steps):
        self.steps = steps
        self.arrays = []
        for places in steps:
            for _, pieces in places:
                for array, _ in pieces:
                    if not any(array is other for other in self.arrays):
                        self.arrays.append(array)
        self.count = len(steps[0][0][1])
        self.specs = [pl.BlockSpec(memory_space=pltpu.HBM)] * len(self.arrays)
        self.scratch = [pltpu.VMEM((2, D, D), BF), pltpu.SemaphoreType.DMA((2, self.count))]

    def bind(self, refs, held, sems):
        self.refs, self.held, self.sems = refs, held, sems

    def copies(self, pieces, slot):
        made = []
        for at, (array, block) in enumerate(pieces):
            ref = next(ref for ref, other in zip(self.refs, self.arrays) if other is array)
            target = self.held.at[slot]
            if self.count > 1:
                rows = array.shape[-2]
                row = piece_row(at % 4, at // 4, rows)
                target = self.held.at[slot, pl.ds(pl.multiple_of(row, 16), rows)]
            made.append(pltpu.make_async_copy(ref.at[block], target, self.sems.at[slot, at]))
        return made

    def start(self, j, wanted):
        head = lax.axis_index("head")
        for step, places in enumerate(self.steps):
            for owners, pieces in places:
                here = wanted == step
                if owners is not None:
                    here = here & functools.reduce(lambda a, b: a | b, [head == owner for owner in owners])

                @pl.when(here)
                def _(step=step, pieces=pieces):
                    for copy in self.copies(pieces, step % 2):
                        copy.start()

    def step(self, j):
        @pl.when(j == 0)
        def _():
            self.start(j, j)

        @pl.when(j + 1 < len(self.steps))
        def _():
            self.start(j, j + 1)

        slot = lax.rem(j, 2)
        for copy in self.copies(self.steps[0][0][1], slot):
            copy.wait()
        return self.held.at[slot]


def piece_row(way, dc, rows):
    me = lax.axis_index("dp")
    core, x, y = lax.rem(me, 2), lax.rem(me // 2, 2), me // 4
    core = 1 - core if dc else core
    dx, dy = ((0, 0), (1 - core, core), (core, 1 - core), (1, 1))[way]
    return ((y + dy - 2 * y * dy) * 4 + (x + dx - 2 * x * dx) * 2 + core) * rows


def row_parts(values):
    average = jnp.mean(values, axis=-1, keepdims=True)
    centred = values - average
    inverse = lax.rsqrt(jnp.mean(centred * centred, axis=-1, keepdims=True) + EPS_NORM)
    return centred * inverse, inverse


def head_mixer():
    row = lax.broadcasted_iota(jnp.int32, (TILE, TILE), 0) // HEAD_DIM
    column = lax.broadcasted_iota(jnp.int32, (TILE, TILE), 1) // HEAD_DIM
    return jnp.where(row == column, 1.0 / HEAD_DIM, 0.0).astype(BF)


def head_mean(values, mixer):
    high = values.astype(BF)
    low = (values - high.astype(F32)).astype(BF)
    return dot(high, mixer) + dot(low, mixer)


def gelu_parts(z):
    decay = jnp.exp2(z * z * (-0.5 * math.log2(math.e)))
    t = 1.0 / (1.0 + (0.3275911 * math.sqrt(0.5)) * jnp.abs(z))
    poly = 0.5 * 1.061405429
    for factor in (-1.453152027, 1.421413741, -0.284496736, 0.254829592):
        poly = poly * t + 0.5 * factor
    tail = poly * t * decay
    share = jnp.where(z >= 0, 1.0 - tail, tail)
    return z * share, share + z * decay * (1.0 / math.sqrt(2.0 * math.pi))


def tiles(rows, columns):
    return [(slice(r, r + PAD), slice(c, c + TILE)) for r in range(0, rows, PAD) for c in range(0, columns, TILE)]


def mlp_in(normed, bias, blocks):
    tokens = normed.shape[0]

    def kernel(h_ref, b_ref, *refs):
        w_refs, (a_ref, s_ref, *fetch) = refs[: len(blocks.arrays)], refs[len(blocks.arrays) :]
        blocks.bind(w_refs, *fetch)
        block = blocks.step(pl.program_id(0))
        spots = tiles(tokens, D)
        wide = [dot(h_ref[rows, :], block[:, columns]) for rows, columns in spots]
        for (rows, columns), z in zip(spots, wide):
            act, slope = gelu_parts(z + b_ref[:, columns])
            a_ref[rows, columns] = act.astype(BF)
            s_ref[rows, columns] = slope.astype(BF)

    return call(
        kernel,
        (RATIO,),
        [normed, bias] + blocks.arrays,
        [whole((tokens, D)), pl.BlockSpec((1, D), lambda j: (0, j))] + blocks.specs,
        [sds((tokens, FF), BF), sds((tokens, FF), BF)],
        [pl.BlockSpec((tokens, D), lambda j: (0, j))] * 2,
        blocks.scratch,
        11.0,
        "mlp_in",
    )


def half_masks(rows):
    low = lax.broadcasted_iota(jnp.int32, (rows, PAIR), 1) < HEAD_DIM
    return low


def split_pair(values, low):
    zero = jnp.zeros_like(values)
    return jnp.where(low, values, zero), jnp.where(low, zero, values)


def split_rows(values, top):
    zero = jnp.zeros_like(values)
    return jnp.where(top, values, zero), jnp.where(top, zero, values)


def qkv_in(stream, ln_gain, gains, blocks):
    tokens = stream.shape[0]

    def kernel(x_ref, g_ref, c_ref, *refs):
        w_refs, (h_ref, n_ref, u_ref, i_ref, *fetch) = refs[: len(blocks.arrays)], refs[len(blocks.arrays) :]
        blocks.bind(w_refs, *fetch)
        j = pl.program_id(0)

        @pl.when(j == 0)
        def _():
            for row in range(0, tokens, PAD):
                rows = slice(row, row + PAD)
                unit, _ = row_parts(x_ref[rows, :].astype(F32))
                h_ref[rows, :] = (unit * g_ref[...]).astype(BF)

        block = blocks.step(j)

        @pl.when(j < 2)
        def _():
            mixer = head_mixer()
            spots = tiles(tokens, D)
            raws = [dot(h_ref[rows, :], block[:, columns]) for rows, columns in spots]
            centred = [raw - head_mean(raw, mixer) for raw in raws]
            spreads = [head_mean(part * part, mixer) for part in centred]
            for (rows, columns), part, spread in zip(spots, centred, spreads):
                inverse = lax.rsqrt(spread + EPS_NORM)
                unit = part * inverse
                n_ref[rows, columns] = (unit * c_ref[0, :, columns]).astype(BF)
                u_ref[rows, columns] = unit.astype(BF)
                i_ref[rows, columns] = inverse

        @pl.when(j == 2)
        def _():
            n_ref[...] = dot(h_ref[...], block[...]).astype(BF)

    first_two = lambda j: (0, jnp.minimum(j, 1))
    return call(
        kernel,
        (3,),
        [stream, ln_gain, gains] + blocks.arrays,
        [
            whole((tokens, D)),
            whole((1, D)),
            pl.BlockSpec((1, 1, D), lambda j: (jnp.minimum(j, 1), 0, 0)),
        ]
        + blocks.specs,
        [
            sds((tokens, D), BF),
            sds((tokens, 3 * D), BF),
            sds((tokens, 2 * D), BF),
            sds((tokens, 2 * D), F32),
        ],
        [
            whole((tokens, D)),
            pl.BlockSpec((tokens, D), lambda j: (0, j)),
            pl.BlockSpec((tokens, D), first_two),
            pl.BlockSpec((tokens, D), first_two),
        ],
        blocks.scratch,
        9.0,
        "qkv_in",
    )


def attend(qkv):
    tokens = qkv.shape[0]

    def kernel(z_ref, o_ref):
        low = half_masks(PAD)
        valid = lax.broadcasted_iota(jnp.int32, (PAD, PAD), 1) < SEQ
        raw = []
        for at in range(0, D, PAIR):
            keys = z_ref[:, D + at : D + at + PAIR]
            raw += [dot(query, keys, NT) for query in split_pair(z_ref[:, at : at + PAIR], low)]
        raised = [jnp.where(valid, jnp.exp2(part * EXP2_SCALE), 0.0) for part in raw]
        shares = [1.0 / jnp.sum(part, axis=1, keepdims=True) for part in raised]
        for pair, at in enumerate(range(0, D, PAIR)):
            values = z_ref[:, 2 * D + at : 2 * D + at + PAIR]
            sides = [dot(raised[n].astype(BF), values) * shares[n] for n in (2 * pair, 2 * pair + 1)]
            o_ref[:, at : at + PAIR] = jnp.where(low, sides[0], sides[1]).astype(BF)

    return call(
        kernel,
        (tokens // PAD,),
        [qkv],
        [pl.BlockSpec((PAD, 3 * D), lambda i: (i, 0))],
        [sds((tokens, D), BF)],
        [pl.BlockSpec((PAD, D), lambda i: (i, 0))],
        [],
        8.0,
        "attend",
    )[0]


def project(stream, attended, hidden, bias, blocks, last):
    tokens = stream.shape[0]

    def kernel(x_ref, o_ref, a_ref, b_ref, *refs):
        w_refs, (y_ref, total, x_held, x_sem, *fetch) = refs[: len(blocks.arrays)], refs[len(blocks.arrays) :]
        blocks.bind(w_refs, *fetch)
        j = pl.program_id(0)
        x_copy = pltpu.make_async_copy(x_ref, x_held, x_sem)
        block = blocks.step(j)

        @pl.when(j == 0)
        def _():
            x_copy.start()
            total[...] = dot(o_ref[...], block[...])

        @pl.when((j > 0) & (j < OUT_COUNT - 1))
        def _():
            total[...] += dot(a_ref[...], block[...])

        @pl.when(j == OUT_COUNT - 1)
        def _():
            x_copy.wait()
            for rows, columns in tiles(tokens, D):
                y_ref[rows, columns] = (
                    total[rows, columns]
                    + (x_held[rows, columns].astype(F32) + b_ref[:, columns])
                    + dot(a_ref[rows, :], block[:, columns])
                ).astype(y_ref.dtype)

    return call(
        kernel,
        (OUT_COUNT,),
        [stream, attended, hidden, bias] + blocks.arrays,
        [
            pl.BlockSpec(memory_space=pl.ANY),
            whole((tokens, D)),
            pl.BlockSpec((tokens, D), lambda j: (0, jnp.maximum(j - 1, 0))),
            whole((1, D)),
        ]
        + blocks.specs,
        [sds((tokens, D), BF if last else F32)],
        [whole((tokens, D))],
        [pltpu.VMEM((tokens, D), F32), pltpu.VMEM((tokens, D), stream.dtype), pltpu.SemaphoreType.DMA]
        + blocks.scratch,
        8.0,
        "project",
    )[0]


def mlp_back(grad, slope, blocks):
    tokens = grad.shape[0]

    def kernel(g_ref, s_ref, *refs):
        w_refs, refs = refs[: len(blocks.arrays)], refs[len(blocks.arrays) :]
        dy_ref, do_ref, du_ref, dbo_ref, dbu_ref, *fetch = refs
        blocks.bind(w_refs, *fetch)
        j = pl.program_id(0)

        @pl.when(j == 0)
        def _():
            dy = g_ref[...].astype(BF)
            dy_ref[...] = dy
            dbo_ref[...] = jnp.sum(dy.astype(F32), axis=0, keepdims=True)

        block = blocks.step(j)

        @pl.when(j == 0)
        def _():
            do_ref[...] = dot(dy_ref[...], block[...], NT).astype(BF)

        @pl.when(j > 0)
        def _():
            du = (dot(dy_ref[...], block[...], NT) * s_ref[...].astype(F32)).astype(BF)
            du_ref[...] = du
            dbu_ref[...] = jnp.sum(du.astype(F32), axis=0, keepdims=True)

    shifted = pl.BlockSpec((tokens, D), lambda j: (0, jnp.maximum(j - 1, 0)))
    return call(
        kernel,
        (OUT_COUNT,),
        [grad, slope] + blocks.arrays,
        [whole((tokens, D)), shifted] + blocks.specs,
        [
            sds((tokens, D), BF),
            sds((tokens, D), BF),
            sds((tokens, FF), BF),
            sds((1, D), F32),
            sds((1, FF), F32),
        ],
        [
            whole((tokens, D)),
            whole((tokens, D)),
            shifted,
            whole((1, D)),
            pl.BlockSpec((1, D), lambda j: (0, jnp.maximum(j - 1, 0))),
        ],
        blocks.scratch,
        9.0,
        "mlp_back",
    )


def attend_back(grad_o, qkv, unit, inverse, gains):
    tokens = grad_o.shape[0]

    def kernel(do_ref, z_ref, u_ref, i_ref, c_ref, dz_ref, dc_ref):
        low = half_masks(PAD)
        valid = lax.broadcasted_iota(jnp.int32, (PAD, PAD), 0) < SEQ
        top = lax.broadcasted_iota(jnp.int32, (PAIR, PAD), 0) < HEAD_DIM
        mixer = head_mixer()

        @pl.when(pl.program_id(0) == 0)
        def _():
            dc_ref[...] = jnp.zeros_like(dc_ref)

        def norm_back(grad, which, columns):
            at = slice(which * D + columns.start, which * D + columns.stop)
            hats = u_ref[:, at].astype(F32)
            dc_ref[which, :, columns] += jnp.sum(grad * hats, axis=0, keepdims=True)
            pull = grad * c_ref[which, :, columns]
            dz_ref[:, at] = (
                i_ref[:, at] * (pull - head_mean(pull, mixer) - hats * head_mean(pull * hats, mixer))
            ).astype(BF)

        for tile in range(0, D, 768):
            grads_q, grads_k = [], []
            pairs = range(tile, tile + 768, PAIR)
            raw, pulled, keys_t = [], [], []
            for at in pairs:
                query, key, value = (z_ref[:, side + at : side + at + PAIR] for side in (0, D, 2 * D))
                grad = do_ref[:, at : at + PAIR]
                keys_t.append(key.T)
                for query_t, grad_t in zip(split_rows(query.T, top), split_rows(grad.T, top)):
                    raw.append(dot(key, query_t))
                    pulled.append(dot(value, grad_t))
            probs, scores = [], []
            for part, pull in zip(raw, pulled):
                raised = jnp.exp2(part * EXP2_SCALE)
                raised = jnp.where(valid, raised, 0.0)
                share = raised * (1.0 / jnp.sum(raised, axis=0, keepdims=True))
                mixed = share * pull
                row_dot = jnp.sum(mixed, axis=0, keepdims=True)
                probs.append(share.astype(BF))
                scores.append((mixed - share * row_dot).astype(BF))
            for n, at in enumerate(pairs):
                query, grad = z_ref[:, at : at + PAIR], do_ref[:, at : at + PAIR]
                both_v = dot(jnp.concatenate(probs[2 * n : 2 * n + 2], axis=0), grad)
                both_k = dot(jnp.concatenate(scores[2 * n : 2 * n + 2], axis=0), query)
                turned = [
                    dot(keys_t[n][h * HEAD_DIM : (h + 1) * HEAD_DIM], scores[2 * n + h]) for h in (0, 1)
                ]
                grads_q.append((jnp.concatenate(turned, axis=0) * SCALE).astype(BF).T.astype(F32))
                grads_k.append((jnp.where(low, both_k[:PAD], both_k[PAD:]) * SCALE).astype(BF).astype(F32))
                dz_ref[:, 2 * D + at : 2 * D + at + PAIR] = jnp.where(low, both_v[:PAD], both_v[PAD:]).astype(BF)
            for k in range(0, 768, TILE):
                n = k // PAIR
                norm_back(jnp.concatenate(grads_q[n : n + 2], axis=1), 0, slice(tile + k, tile + k + TILE))
                norm_back(jnp.concatenate(grads_k[n : n + 2], axis=1), 1, slice(tile + k, tile + k + TILE))

    def per_image(columns):
        return pl.BlockSpec((PAD, columns), lambda i: (i, 0))

    return call(
        kernel,
        (tokens // PAD,),
        [grad_o, qkv, unit, inverse, gains],
        [per_image(D), per_image(3 * D), per_image(2 * D), per_image(2 * D), whole((2, 1, D))],
        [sds((tokens, 3 * D), BF), sds((2, 1, D), F32)],
        [per_image(3 * D), whole((2, 1, D))],
        [],
        14.0,
        "attend_back",
    )


def weight_grads(segments, cut, name):
    total = sum(count for _, _, count in segments)
    operands, specs, start = [], [], 0
    for left, right, count in segments:
        for side in (left, right):
            side, first, last = (*side, count - 1) if isinstance(side, tuple) else (side, 0, 0)
            tokens = side.shape[0]
            index = functools.partial(
                lambda at, first, last, j: (0, first + jnp.clip(j - at, 0, last)), start, first, last
            )
            operands.append(side)
            specs.append(pl.BlockSpec((tokens, D), index))
        start += count

    def kernel(*refs):
        ins, outs = refs[: len(operands)], refs[len(operands) :]
        j = pl.program_id(0)
        slot = lax.rem(j, 2)

        def leave(block, slot):
            *mine, theirs, held, sems = outs
            rows = D // 8
            copies = []
            for way in WAYS:
                for core, target in enumerate((mine[way].at[block], theirs.at[way, block])):
                    row = pl.multiple_of(piece_row(way, core, rows), 16)
                    copies.append(
                        pltpu.make_async_copy(held.at[slot, pl.ds(row, rows)], target, sems.at[slot, core, way])
                    )
            return copies

        if cut:

            @pl.when(j >= 2)
            def _():
                for copy in leave(j - 2, slot):
                    copy.wait()

        start = 0
        for at, (_, _, count) in enumerate(segments):

            def body(at=at):
                value = dot(ins[2 * at][...], ins[2 * at + 1][...], TN).astype(BF)
                if cut:
                    outs[5][slot] = value
                else:
                    outs[0][0] = value

            if count == total:
                body()
            else:
                pl.when((j >= start) & (j < start + count))(body)
            start += count
        if cut:
            for copy in leave(j, slot):
                copy.start()

            @pl.when(j == total - 1)
            def _():
                if total > 1:
                    for copy in leave(j - 1, 1 - slot):
                        copy.wait()
                for copy in leave(j, slot):
                    copy.wait()

    if cut:
        shapes = [pltpu.HBM((total, D // 8, D), BF)] * 4 + [pltpu.HBM((4, total, D // 8, D), BF)]
        out_specs = [pl.BlockSpec(memory_space=pl.ANY)] * 5
    else:
        shapes = [sds((total, D, D), BF)]
        out_specs = [pl.BlockSpec((1, D, D), lambda j: (j, 0, 0))]
    return list(call(
        kernel,
        (total,),
        operands,
        specs,
        shapes,
        out_specs,
        [pltpu.VMEM((2, D, D), BF), pltpu.SemaphoreType.DMA((2, 2, 4))] if cut else [],
        1.0 + 1.4 * total,
        name,
    ))


def stream_back(grad, stream, gain, grad_u, grad_qkv, blocks):
    tokens = grad.shape[0]

    def kernel(g_ref, x_ref, c_ref, du_ref, dz_ref, *refs):
        w_refs, refs = refs[: len(blocks.arrays)], refs[len(blocks.arrays) :]
        out_ref, dg_ref, total, g_held, x_held, sems, *fetch = refs
        blocks.bind(w_refs, *fetch)
        j = pl.program_id(0)
        late = [
            pltpu.make_async_copy(g_ref, g_held, sems.at[0]),
            pltpu.make_async_copy(x_ref, x_held, sems.at[1]),
        ]
        block = blocks.step(j)

        @pl.when(j == 0)
        def _():
            for copy in late:
                copy.start()
            total[...] = dot(du_ref[...], block[...], NT)

        @pl.when((j > 0) & (j < RATIO))
        def _():
            total[...] += dot(du_ref[...], block[...], NT)

        @pl.when(j >= RATIO)
        def _():
            total[...] += dot(dz_ref[...], block[...], NT)

        @pl.when(j == IN_COUNT - 1)
        def _():
            for copy in late:
                copy.wait()
            sums = 0.0
            for row in range(0, tokens, PAD // 2):
                rows = slice(row, row + PAD // 2)
                unit, inverse = row_parts(x_held[rows, :].astype(F32))
                grad_h = total[rows, :]
                sums = sums + jnp.sum(grad_h * unit, axis=0, keepdims=True)
                hat = grad_h * c_ref[...]
                out_ref[rows, :] = g_held[rows, :].astype(F32) + inverse * (
                    hat
                    - jnp.mean(hat, axis=-1, keepdims=True)
                    - unit * jnp.mean(hat * unit, axis=-1, keepdims=True)
                )
            dg_ref[...] = sums

    return call(
        kernel,
        (IN_COUNT,),
        [grad, stream, gain, grad_u, grad_qkv] + blocks.arrays,
        [
            pl.BlockSpec(memory_space=pl.ANY),
            pl.BlockSpec(memory_space=pl.ANY),
            whole((1, D)),
            pl.BlockSpec((tokens, D), lambda j: (0, jnp.minimum(j, RATIO - 1))),
            pl.BlockSpec((tokens, D), lambda j: (0, jnp.maximum(j - RATIO, 0))),
        ]
        + blocks.specs,
        [sds((tokens, D), F32), sds((1, D), F32)],
        [whole((tokens, D)), whole((1, D))],
        [
            pltpu.VMEM((tokens, D), F32),
            pltpu.VMEM((tokens, D), grad.dtype),
            pltpu.VMEM((tokens, D), stream.dtype),
            pltpu.SemaphoreType.DMA((2,)),
        ]
        + blocks.scratch,
        12.0,
        "stream_back",
    )


def shampoo(grad, full, right, left_root, left_stats, right_stats, weights, ema, first, earlier):
    count, rows, _ = grad.shape

    def kernel(g_ref, lr_ref, ls_ref, rs_ref, w_ref, e_ref, *refs):
        f_refs, refs = refs[: len(full.arrays)], refs[len(full.arrays) :]
        r_refs, refs = refs[: len(right.arrays)], refs[len(right.arrays) + len(earlier) :]
        go_ref, lo_ref, ro_ref, wo_ref, eo_ref, f_held, f_sems, r_held, r_sems = refs
        full.bind(f_refs, f_held, f_sems)
        right.bind(r_refs, r_held, r_sems)
        j = pl.program_id(0)
        at = lax.axis_index("dp") * rows
        block = full.step(j)[...]
        right_block = right.step(j)[...]
        go_ref[0] = g_ref[0]
        gram = dot(g_ref[0].astype(BF), block, NT)
        lo_ref[0] = STAT_DECAY * ls_ref[0] + (1.0 - STAT_DECAY) * gram
        pick = (
            lax.broadcasted_iota(jnp.int32, (rows, D), 1)
            == lax.broadcasted_iota(jnp.int32, (rows, D), 0) + at
        )
        columns = dot(jnp.where(pick, 1.0, 0.0).astype(BF), block, NT).astype(BF)
        ro_ref[0] = STAT_DECAY * rs_ref[0] + (1.0 - STAT_DECAY) * dot(columns, block)
        lifted = dot(lr_ref[0].astype(BF), block).astype(BF)
        precond = dot(lifted, right_block)
        renewed = w_ref[0] * (1.0 - RATE_MAT * DECAY_MAT) - RATE_MAT * precond
        wo_ref[0] = renewed
        eo_ref[0] = EMA_DECAY * e_ref[0] + (1.0 - EMA_DECAY) * renewed

    part = pl.BlockSpec((1, rows, D), lambda j: (j, 0, 0))
    own = pl.BlockSpec((1, rows, D), lambda j: (first + j, 0, 0))
    inputs = [grad, left_root, left_stats, right_stats, weights, ema] + full.arrays + right.arrays
    return list(call(
        kernel,
        (count,),
        inputs + list(earlier),
        [part] + [own] * 5 + full.specs + right.specs + [pl.BlockSpec(memory_space=pl.ANY)] * len(earlier),
        [sds(weights.shape, F32)] * 5,
        [own] * 5,
        full.scratch + right.scratch,
        2.0 + 3.0 * count,
        "shampoo",
        {len(inputs) + at: at for at in range(len(earlier))},
    ))


def split_vector(row_vec):
    ends = (D, D + HEAD_DIM, D + 2 * HEAD_DIM, D + 2 * HEAD_DIM + FF)
    ln_gain, q_gain, k_gain, mlp_bias, out_bias = jnp.split(row_vec, ends)
    return (
        ln_gain[None],
        jnp.stack([jnp.tile(q_gain, HEADS)[None], jnp.tile(k_gain, HEADS)[None]]),
        mlp_bias[None],
        out_bias[None],
    )


def pad_tokens(array):
    return jnp.pad(array, ((0, 0), (0, PAD - SEQ), (0, 0))).reshape(-1, D)


def cut_tokens(array):
    return array.reshape(-1, PAD, D)[:, :SEQ]


QKV, MLP, OUT = 0, 3, IN_COUNT
SIZES = {QKV: 3, MLP: RATIO, OUT: OUT_COUNT}


class Collectives:
    cut = False

    def __init__(self, weights, right_root):
        rows = lax.all_gather(weights.astype(BF), "head", axis=0, tiled=True)
        self.blocks = lax.all_gather(rows, "dp", axis=1, tiled=True)
        self.right = lax.all_gather(right_root.astype(BF), "dp", axis=1, tiled=True)
        self.count = weights.shape[0]
        self.parts = {}

    def group(self, *runs):
        return Blocks(
            [
                [(None, [(self.blocks, depth * PER_LAYER + first + at)])]
                for depth, first, count in runs
                for at in range(count)
            ]
        )

    def next(self, array):
        return array

    def done(self, name, array):
        return array

    def add_grads(self, depth, first, pieces):
        self.parts[depth, first] = pieces[0]

    def finish(self, renew):
        partial = jnp.concatenate([self.parts[key] for key in sorted(self.parts)], axis=0)
        rows = lax.psum_scatter(partial, "dp", scatter_dimension=1, tiled=True)
        own = lax.psum_scatter(rows, "head", scatter_dimension=0, tiled=True)
        full = lax.all_gather(own, "dp", axis=1, tiled=True)
        full, right = (
            Blocks([[(None, [(array, at)])] for at in range(self.count)]) for array in (full, self.right)
        )
        return renew(own.astype(F32), full, right, 0, ())

    def vector_sum(self, vectors):
        return lambda: lax.psum(vectors, ("dp", "head"))


DP, LINE = 8, 4
HALF = 3
STEPS = {"core": (1, 1), "x": (2, 2), "y": (4, 4), "first": (2, 4), "second": (4, 2)}
ROUNDS = ((2, 0, 0, 0), (1, 2, 1, 1), (3, 3, 3, 2))


def swap(array, axis):
    return lax.ppermute(array, "dp", [(i, i ^ STEPS[axis][i % 2]) for i in range(DP)])


def hop(array, *pairs):
    return lax.ppermute(array, "head", pairs)


def along(axis):
    return functools.partial(swap, axis=axis)


def over(*pairs):
    return lambda array: hop(array, *pairs)


class PlaneGather:
    def __init__(self, own):
        self.own = own

    def steps(self):
        own = self.own
        first, second, core = along("first"), along("second"), along("core")
        one, two = yield [(own, first), (own, second)]
        three, *others = yield [(one, second), (own, core), (one, core)]
        more = yield [(two, core), (three, core)]
        self.chips = [own, one, two, three]
        self.others = others + more
        self.chips, self.others = (
            [pltpu.with_memory_space_constraint(array, pltpu.HBM) for array in arrays]
            for arrays in (self.chips, self.others)
        )
        yield []

    def pieces(self, at):
        return [(chip, at) for chip in self.chips + self.others]


STEPS_AFTER = {
    "qkv0": [["place4", "line1", "place3", "place5"]],
    "attend0": [["place3", "place4"], ["place3", "place5", "place6"], ["place3"]],
    "mlp0": [["place5", "place6", "place7"], ["place5"]],
    "project0": [["place6", "place7"], ["place6"]],
    "qkv1": [["place7", "right0", "right1"]],
    "attend1": [["place7"]],
    "mlp1": [["right0", "right1"]],
    "project1": [["out1", "right0", "right1"]],
    "grad_mlp1": [["out1", "right1"]],
    "attend_back1": [["out1", "mlp1"]],
    "stream_back1": [["out1", "mlp1", "qkv1"]],
    "mlp_back0": [["mlp1"]],
    "grad_out0": [["out1", "mlp1", "qkv1"]],
    "grad_mlp0": [["out0", "qkv1"]],
    "attend_back0": [["mlp1", "qkv1", "mlp0"]],
    "grad_qkv0": [["out0", "qkv1"], ["out0", "mlp0"]],
    "stream_back0": [["out0", "mlp0", "qkv0"]],
}
FIRST_STEPS = [
    ["line0", "line1"],
    ["place0", "place1"],
    ["place0"],
    ["place1"],
    ["place0", "place1", "line0", "place2", "place4"],
    ["place0", "place1", "place2"],
    ["place2", "place4", "right0"],
    ["place2"],
]
LAST_STEPS = [
    ["sums"],
    ["out0", "mlp0", "qkv0", "sums"],
    ["mlp0", "full3", "qkv0", "sums"],
    ["full3", "qkv0", "sums"],
    ["qkv0", "full3", "full0", "sums"],
    ["full3", "full0", "sums"],
]


class Permutes:
    cut = True

    def __init__(self, weights, right_root):
        self.parts, self.chains, self.asked, self.sent = {}, {}, {}, {}
        own = weights.astype(BF)
        right_root = right_root.astype(BF)
        self.plan = [PlaneGather(own[:HALF]), PlaneGather(own[HALF:])] + [PlaneGather(None) for _ in range(6)]
        self.right = [PlaneGather(right_root[:HALF]), PlaneGather(right_root[HALF:])]
        for at, part in enumerate(self.plan):
            self.chains[f"place{at}"] = part.steps()
        for side in (0, 1):
            self.chains[f"line{side}"] = self.gather_line(side)
            self.chains[f"right{side}"] = self.right[side].steps()
        for group in FIRST_STEPS:
            self.step(group)

    def gather_line(self, side):
        (halves,) = yield [(self.plan[side].own, lambda array: lax.all_gather(array, "head"))]
        head = lax.axis_index("head")
        for at in (0, 1, 2):
            owner = functools.reduce(
                lambda value, z: jnp.where(head == z, ROUNDS[at][z], value), range(1, LINE), ROUNDS[at][0]
            )
            self.plan[2 + 2 * at + side].own = lax.dynamic_index_in_dim(halves, owner, 0, keepdims=False)
        yield []

    def send(self, array=None):
        names = [name for name in self.asked if name not in self.sent]
        asked = [entry for name in names for entry in self.asked[name]]
        operands = [operand for operand, _ in asked]
        if array is not None and operands:
            array, *operands = lax.optimization_barrier((array, *operands))
        for name in names:
            self.sent[name] = [how(operands.pop(0)) for _, how in self.asked[name]]
        return array

    def step(self, group, event=None):
        if any(name in self.asked and name not in self.sent for name in group):
            self.send()
        arrived = [array for name in group for array in self.sent.get(name, [])]
        if arrived:
            event, *arrived = (
                lax.optimization_barrier((event, *arrived))
                if event is not None
                else (None, *lax.optimization_barrier(tuple(arrived)))
            )
        for name in group:
            chain = self.chains[name]
            if name in self.sent:
                self.asked[name] = chain.send([arrived.pop(0) for _ in self.sent.pop(name)])
            else:
                self.asked[name] = next(chain)
        return event

    def done(self, name, array):
        for group in STEPS_AFTER.get(name, ()):
            array = self.step(group, array)
        return array

    def next(self, array):
        return self.send(array)

    def place(self, owner, side, head):
        if head == owner:
            return side
        return next(2 + 2 * at + side for at in (0, 1, 2) if ROUNDS[at][head] == owner)

    def group(self, *runs):
        steps = []
        for depth, first, count in runs:
            for block in range(first, first + count):
                owner, at = 2 * depth + block // (2 * HALF), block % (2 * HALF)
                side, at = at // HALF, at % HALF
                places = [self.place(owner, side, head) for head in range(LINE)]
                steps.append(
                    [
                        (
                            [head for head in range(LINE) if places[head] == place],
                            self.plan[place].pieces(at),
                        )
                        for place in sorted(set(places))
                    ]
                )
        return Blocks(steps)

    def add_grads(self, depth, first, pieces):
        name = {QKV: "qkv", MLP: "mlp"}.get(first, "out") + str(depth)
        self.chains[name] = self.reduce(depth, first, pieces[:4], pieces[4])
        self.step([name])

    def reduce(self, depth, first_block, mine, theirs):
        count = mine[0].shape[0]
        first, second = along("first"), along("second")
        (core,) = yield [(theirs, along("core"))]
        far, to_two = ((mine[way].astype(F32) + core[way].astype(F32)).astype(BF) for way in (3, 2))
        far, two = yield [(far, second), (to_two, second)]
        to_one = (mine[1].astype(F32) + core[1].astype(F32) + far.astype(F32)).astype(BF)
        (one,) = yield [(to_one, first)]
        total = mine[0].astype(F32) + core[0].astype(F32) + one.astype(F32) + two.astype(F32)
        total = total.astype(BF)
        split = min(max(2 * HALF - first_block, 0), count)
        runs = [(side, low, high) for side, low, high in ((0, 0, split), (1, split, count)) if low < high]
        parts = [total[low:high] for _, low, high in runs]
        outer, inner, far_in, far_out = (0, 1, 2, 3) if depth == 0 else (3, 2, 1, 0)
        owners = [2 * depth + side for side, _, _ in runs]
        arrived = yield [
            (part, over((far_out, far_in), (outer if owner == inner else inner, owner)))
            for part, owner in zip(parts, owners)
        ]
        parts = [(part.astype(F32) + other.astype(F32)).astype(BF) for part, other in zip(parts, arrived)]
        arrived = yield [(part, over((far_in, owner))) for part, owner in zip(parts, owners)]
        for (_, low, high), part, other in zip(runs, parts, arrived):
            part = part.astype(F32) + other.astype(F32)
            for at in range(low, high):
                self.parts[depth, first_block + at] = (part, at - low)
        yield []

    def own_blocks(self, low, high):
        head = lax.axis_index("head")
        own = None
        for owner in range(LINE):
            runs = []
            for at in range(low, high):
                part, block = self.parts[owner // 2, 2 * HALF * (owner % 2) + at]
                if runs and runs[-1][0] is part:
                    runs[-1][2] = block + 1
                else:
                    runs.append([part, block, block + 1])
            values = [part[start:stop] for part, start, stop in runs]
            value = values[0] if len(values) == 1 else jnp.concatenate(values, axis=0)
            own = value if own is None else jnp.where(head == owner, value, own)
        return own

    def finish(self, renew):
        self.full = {}
        for low in (HALF, 0):
            self.chains[f"full{low}"] = self.gather_own(low)
        for group in LAST_STEPS:
            self.step(group)
        results = ()
        for low in (HALF, 0):
            own, full = self.full[low]
            if low == 0:
                results[0] = self.step(["full0"], results[0])
                self.step(["full0"])
            results = renew(
                self.next(own),
                Blocks([[(None, full.pieces(at))] for at in range(HALF)]),
                Blocks([[(None, self.right[low // HALF].pieces(at))] for at in range(HALF)]),
                low,
                results,
            )
        return results

    def gather_own(self, low):
        own = self.own_blocks(low, low + HALF)
        full = PlaneGather(own.astype(BF))
        self.full[low] = own, full
        yield from full.steps()

    def vector_sum(self, vectors):
        self.chains["sums"] = self.sum_vectors(vectors)
        return lambda: self.summed

    def sum_vectors(self, vectors):
        for axis in ("core", "x", "y"):
            (other,) = yield [(vectors, along(axis))]
            vectors = vectors + other
        for step in (1, 2):
            (other,) = yield [(vectors, over(*((i, i ^ step) for i in range(LINE))))]
            vectors = vectors + other
        self.summed = vectors
        yield []


def on_device(
    image_tokens,
    cotangent,
    weights,
    weights_ema,
    left_stats,
    right_stats,
    left_root,
    right_root,
    vectors,
    vec_first,
    vec_second,
):
    fits = lax.axis_size("dp") == DP and lax.axis_size("head") == LINE
    links = (Permutes if fits else Collectives)(weights, right_root)
    stream = pad_tokens(image_tokens)
    grad = pad_tokens(cotangent)
    saved = []
    top = LAYERS - 1
    for depth in range(LAYERS):
        ln_gain, gains, mlp_bias, out_bias = split_vector(vectors[depth])
        normed, qkv, unit, inverse = qkv_in(
            links.next(stream), ln_gain, gains, links.group((depth, QKV, 3))
        )
        qkv = links.done(f"qkv{depth}", qkv)
        attended = attend(links.next(qkv))
        attended = links.done(f"attend{depth}", attended)
        hidden, slope = mlp_in(links.next(normed), mlp_bias, links.group((depth, MLP, RATIO)))
        hidden = links.done(f"mlp{depth}", hidden)
        saved.append((stream, normed, hidden, slope, qkv, unit, inverse, attended))
        if depth == top:
            pieces = weight_grads(
                [(links.next(attended), grad, 1), ((hidden, 0), grad, RATIO)], links.cut, "grad_out"
            )
            pieces[0] = links.done(f"grad_out{depth}", pieces[0])
            links.add_grads(depth, OUT, pieces)
        stream = project(
            links.next(stream), attended, hidden, out_bias, links.group((depth, OUT, OUT_COUNT)), depth == top
        )
        stream = links.done(f"project{depth}", stream)
    block_out = cut_tokens(stream)
    vector_parts = [None] * LAYERS
    for depth in reversed(range(LAYERS)):
        ln_gain, gains, _, _ = split_vector(vectors[depth])
        stream, normed, hidden, slope, qkv, unit, inverse, attended = saved[depth]
        dy, do, du, dbo, dbu = mlp_back(links.next(grad), slope, links.group((depth, OUT, OUT_COUNT)))
        dy = links.done(f"mlp_back{depth}", dy)
        share = RATIO if depth == top else RATIO - 1
        if depth < top:
            segments = [(normed, (du, share), RATIO - share), (links.next(attended), dy, 1), ((hidden, 0), dy, RATIO)]
            pieces = weight_grads(segments, links.cut, "grad_out")
            pieces[0] = links.done(f"grad_out{depth}", pieces[0])
            links.add_grads(depth, MLP + share, pieces)
        pieces = weight_grads([(links.next(normed), (du, 0), share)], links.cut, "grad_mlp")
        pieces[0] = links.done(f"grad_mlp{depth}", pieces[0])
        links.add_grads(depth, MLP, pieces)
        dqkv, dgains = attend_back(links.next(do), qkv, unit, inverse, gains)
        dqkv = links.done(f"attend_back{depth}", dqkv)
        pieces = weight_grads([(links.next(normed), (dqkv, 0), 3)], links.cut, "grad_qkv")
        pieces[0] = links.done(f"grad_qkv{depth}", pieces[0])
        links.add_grads(depth, QKV, pieces)
        grad, dg = stream_back(
            links.next(grad), stream, ln_gain, du, dqkv, links.group((depth, MLP, RATIO), (depth, QKV, 3))
        )
        grad = links.done(f"stream_back{depth}", grad)
        vector_parts[depth] = jnp.concatenate(
            [
                dg[0],
                dgains.reshape(2, HEADS, HEAD_DIM).sum(1).reshape(-1),
                dbu[0],
                dbo[0],
            ]
        )
    grad_stream = cut_tokens(grad)
    vector_sum = links.vector_sum(jnp.stack(vector_parts))

    def renew(own, full, right, first, earlier):
        return shampoo(
            own, full, right, left_root, left_stats, right_stats, weights, weights_ema, first, earlier
        )

    weight_grad, left_new, right_new, weight_new, ema_new = links.finish(renew)
    vector_grad = vector_sum()
    first_new = BETA_ONE * vec_first + (1.0 - BETA_ONE) * vector_grad
    second_new = BETA_TWO * vec_second + (1.0 - BETA_TWO) * vector_grad * vector_grad
    first_hat = first_new / (1.0 - BETA_ONE**STEP)
    second_hat = second_new / (1.0 - BETA_TWO**STEP)
    vec_new = vectors - RATE_VEC * first_hat / (jnp.sqrt(second_hat) + ADAM_EPS)
    return (
        block_out,
        grad_stream,
        weight_grad,
        left_new,
        right_new,
        weight_new,
        ema_new,
        first_new,
        second_new,
        vec_new,
    )


def solution(mesh):
    tokens, blocks = P(("dp", "head"), None, None), P("head", "dp", None)
    return jax.shard_map(
        on_device,
        mesh=mesh,
        in_specs=(tokens, tokens) + (blocks,) * 6 + (P(),) * 3,
        out_specs=(tokens, tokens) + (blocks,) * 5 + (P(),) * 3,
        check_vma=False,
    )
```

```python
import functools
import math

import jax
import jax.numpy as jnp
from jax import lax
from jax.experimental import pallas as pl
from jax.experimental.pallas import tpu as pltpu
from jax.sharding import PartitionSpec as P

D = 768
HEADS = 12
HEAD_DIM = 64
FF = 3072
SEQ = 196
PAD = 208
LAYERS = 2
STEP = 10
RATIO = FF // D
IN_COUNT = 3 + RATIO
OUT_COUNT = 1 + RATIO
PER_LAYER = IN_COUNT + OUT_COUNT
PAIR = 2 * HEAD_DIM
TILE = 256

EPS_NORM = 1e-06
BETA_ONE = 0.9
BETA_TWO = 0.95
ADAM_EPS = 1e-08
RATE_VEC = 0.3
RATE_MAT = 0.003
DECAY_MAT = 0.1
STAT_DECAY = 0.5
EMA_DECAY = 0.8
SCALE = HEAD_DIM ** (-0.5)
EXP2_SCALE = SCALE * math.log2(math.e)

BF = jnp.bfloat16
F32 = jnp.float32
NN = (((1,), (0,)), ((), ()))
NT = (((1,), (1,)), ((), ()))
TN = (((0,), (0,)), ((), ()))


def dot(a, b, dims=NN):
    return lax.dot_general(a, b, dims, preferred_element_type=F32)


def call(kernel, grid, operands, in_specs, outs, out_specs, scratch, about_us, name, aliases=None):
    moved = sum(o.size * o.dtype.itemsize for o in operands) + sum(
        math.prod(o.shape) * o.dtype.itemsize for o in outs
    )
    return pl.pallas_call(
        kernel,
        grid=grid,
        in_specs=in_specs,
        out_specs=out_specs,
        out_shape=outs,
        scratch_shapes=scratch,
        compiler_params=pltpu.CompilerParams(vmem_limit_bytes=24 * 1024 * 1024),
        cost_estimate=pl.CostEstimate(flops=int(about_us * 1.1e9), bytes_accessed=moved, transcendentals=0),
        input_output_aliases=aliases or {},
        name=name,
    )(*operands)


def whole(shape):
    return pl.BlockSpec(shape, lambda *ids: (0,) * len(shape))


def sds(shape, dtype):
    return jax.ShapeDtypeStruct(shape, dtype)


WAYS = (0, 1, 2, 3)


class Blocks:
    def __init__(self, steps):
        self.steps = steps
        self.arrays = []
        for places in steps:
            for _, pieces in places:
                for array, _ in pieces:
                    if not any(array is other for other in self.arrays):
                        self.arrays.append(array)
        self.count = len(steps[0][0][1])
        self.specs = [pl.BlockSpec(memory_space=pltpu.HBM)] * len(self.arrays)
        self.scratch = [pltpu.VMEM((2, D, D), BF), pltpu.SemaphoreType.DMA((2, self.count))]

    def bind(self, refs, held, sems):
        self.refs, self.held, self.sems = refs, held, sems

    def copies(self, pieces, slot):
        made = []
        for at, (array, block) in enumerate(pieces):
            ref = next(ref for ref, other in zip(self.refs, self.arrays) if other is array)
            target = self.held.at[slot]
            if self.count > 1:
                rows = array.shape[-2]
                row = piece_row(at % 4, at // 4, rows)
                target = self.held.at[slot, pl.ds(pl.multiple_of(row, 16), rows)]
            made.append(pltpu.make_async_copy(ref.at[block], target, self.sems.at[slot, at]))
        return made

    def start(self, j, wanted):
        head = lax.axis_index("head")
        for step, places in enumerate(self.steps):
            for owners, pieces in places:
                here = wanted == step
                if owners is not None:
                    here = here & functools.reduce(lambda a, b: a | b, [head == owner for owner in owners])

                @pl.when(here)
                def _(step=step, pieces=pieces):
                    for copy in self.copies(pieces, step % 2):
                        copy.start()

    def step(self, j):
        @pl.when(j == 0)
        def _():
            self.start(j, j)

        @pl.when(j + 1 < len(self.steps))
        def _():
            self.start(j, j + 1)

        slot = lax.rem(j, 2)
        for copy in self.copies(self.steps[0][0][1], slot):
            copy.wait()
        return self.held.at[slot]


def piece_row(way, dc, rows):
    me = lax.axis_index("dp")
    core, x, y = lax.rem(me, 2), lax.rem(me // 2, 2), me // 4
    core = 1 - core if dc else core
    dx, dy = ((0, 0), (1 - core, core), (core, 1 - core), (1, 1))[way]
    return ((y + dy - 2 * y * dy) * 4 + (x + dx - 2 * x * dx) * 2 + core) * rows


def row_parts(values):
    average = jnp.mean(values, axis=-1, keepdims=True)
    centred = values - average
    inverse = lax.rsqrt(jnp.mean(centred * centred, axis=-1, keepdims=True) + EPS_NORM)
    return centred * inverse, inverse


def head_mixer():
    row = lax.broadcasted_iota(jnp.int32, (TILE, TILE), 0) // HEAD_DIM
    column = lax.broadcasted_iota(jnp.int32, (TILE, TILE), 1) // HEAD_DIM
    return jnp.where(row == column, 1.0 / HEAD_DIM, 0.0).astype(BF)


def head_mean(values, mixer):
    high = values.astype(BF)
    low = (values - high.astype(F32)).astype(BF)
    return dot(high, mixer) + dot(low, mixer)


def gelu_parts(z):
    decay = jnp.exp2(z * z * (-0.5 * math.log2(math.e)))
    t = 1.0 / (1.0 + (0.3275911 * math.sqrt(0.5)) * jnp.abs(z))
    poly = 0.5 * 1.061405429
    for factor in (-1.453152027, 1.421413741, -0.284496736, 0.254829592):
        poly = poly * t + 0.5 * factor
    tail = poly * t * decay
    share = jnp.where(z >= 0, 1.0 - tail, tail)
    return z * share, share + z * decay * (1.0 / math.sqrt(2.0 * math.pi))


def tiles(rows, columns):
    return [(slice(r, r + PAD), slice(c, c + TILE)) for r in range(0, rows, PAD) for c in range(0, columns, TILE)]


def mlp_in(normed, bias, blocks):
    tokens = normed.shape[0]

    def kernel(h_ref, b_ref, *refs):
        w_refs, (a_ref, s_ref, *fetch) = refs[: len(blocks.arrays)], refs[len(blocks.arrays) :]
        blocks.bind(w_refs, *fetch)
        block = blocks.step(pl.program_id(0))
        spots = tiles(tokens, D)
        wide = [dot(h_ref[rows, :], block[:, columns]) for rows, columns in spots]
        for (rows, columns), z in zip(spots, wide):
            act, slope = gelu_parts(z + b_ref[:, columns])
            a_ref[rows, columns] = act.astype(BF)
            s_ref[rows, columns] = slope.astype(BF)

    return call(
        kernel,
        (RATIO,),
        [normed, bias] + blocks.arrays,
        [whole((tokens, D)), pl.BlockSpec((1, D), lambda j: (0, j))] + blocks.specs,
        [sds((tokens, FF), BF), sds((tokens, FF), BF)],
        [pl.BlockSpec((tokens, D), lambda j: (0, j))] * 2,
        blocks.scratch,
        11.0,
        "mlp_in",
    )


def half_masks(rows):
    low = lax.broadcasted_iota(jnp.int32, (rows, PAIR), 1) < HEAD_DIM
    return low


def split_pair(values, low):
    zero = jnp.zeros_like(values)
    return jnp.where(low, values, zero), jnp.where(low, zero, values)


def split_rows(values, top):
    zero = jnp.zeros_like(values)
    return jnp.where(top, values, zero), jnp.where(top, zero, values)


def qkv_in(stream, ln_gain, gains, blocks):
    tokens = stream.shape[0]

    def kernel(x_ref, g_ref, c_ref, *refs):
        w_refs, (h_ref, n_ref, u_ref, i_ref, *fetch) = refs[: len(blocks.arrays)], refs[len(blocks.arrays) :]
        blocks.bind(w_refs, *fetch)
        j = pl.program_id(0)

        @pl.when(j == 0)
        def _():
            for row in range(0, tokens, PAD):
                rows = slice(row, row + PAD)
                unit, _ = row_parts(x_ref[rows, :].astype(F32))
                h_ref[rows, :] = (unit * g_ref[...]).astype(BF)

        block = blocks.step(j)

        @pl.when(j < 2)
        def _():
            mixer = head_mixer()
            spots = tiles(tokens, D)
            raws = [dot(h_ref[rows, :], block[:, columns]) for rows, columns in spots]
            centred = [raw - head_mean(raw, mixer) for raw in raws]
            spreads = [head_mean(part * part, mixer) for part in centred]
            for (rows, columns), part, spread in zip(spots, centred, spreads):
                inverse = lax.rsqrt(spread + EPS_NORM)
                unit = part * inverse
                n_ref[rows, columns] = (unit * c_ref[0, :, columns]).astype(BF)
                u_ref[rows, columns] = unit.astype(BF)
                i_ref[rows, columns] = inverse

        @pl.when(j == 2)
        def _():
            n_ref[...] = dot(h_ref[...], block[...]).astype(BF)

    first_two = lambda j: (0, jnp.minimum(j, 1))
    return call(
        kernel,
        (3,),
        [stream, ln_gain, gains] + blocks.arrays,
        [
            whole((tokens, D)),
            whole((1, D)),
            pl.BlockSpec((1, 1, D), lambda j: (jnp.minimum(j, 1), 0, 0)),
        ]
        + blocks.specs,
        [
            sds((tokens, D), BF),
            sds((tokens, 3 * D), BF),
            sds((tokens, 2 * D), BF),
            sds((tokens, 2 * D), F32),
        ],
        [
            whole((tokens, D)),
            pl.BlockSpec((tokens, D), lambda j: (0, j)),
            pl.BlockSpec((tokens, D), first_two),
            pl.BlockSpec((tokens, D), first_two),
        ],
        blocks.scratch,
        9.0,
        "qkv_in",
    )


def attend(qkv):
    tokens = qkv.shape[0]

    def kernel(z_ref, o_ref):
        low = half_masks(PAD)
        valid = lax.broadcasted_iota(jnp.int32, (PAD, PAD), 1) < SEQ
        raw = []
        for at in range(0, D, PAIR):
            keys = z_ref[:, D + at : D + at + PAIR]
            raw += [dot(query, keys, NT) for query in split_pair(z_ref[:, at : at + PAIR], low)]
        raised = [jnp.where(valid, jnp.exp2(part * EXP2_SCALE), 0.0) for part in raw]
        shares = [1.0 / jnp.sum(part, axis=1, keepdims=True) for part in raised]
        for pair, at in enumerate(range(0, D, PAIR)):
            values = z_ref[:, 2 * D + at : 2 * D + at + PAIR]
            sides = [dot(raised[n].astype(BF), values) * shares[n] for n in (2 * pair, 2 * pair + 1)]
            o_ref[:, at : at + PAIR] = jnp.where(low, sides[0], sides[1]).astype(BF)

    return call(
        kernel,
        (tokens // PAD,),
        [qkv],
        [pl.BlockSpec((PAD, 3 * D), lambda i: (i, 0))],
        [sds((tokens, D), BF)],
        [pl.BlockSpec((PAD, D), lambda i: (i, 0))],
        [],
        8.0,
        "attend",
    )[0]


def project(stream, attended, hidden, bias, blocks, last):
    tokens = stream.shape[0]

    def kernel(x_ref, o_ref, a_ref, b_ref, *refs):
        w_refs, (y_ref, total, x_held, x_sem, *fetch) = refs[: len(blocks.arrays)], refs[len(blocks.arrays) :]
        blocks.bind(w_refs, *fetch)
        j = pl.program_id(0)
        x_copy = pltpu.make_async_copy(x_ref, x_held, x_sem)
        block = blocks.step(j)

        @pl.when(j == 0)
        def _():
            x_copy.start()
            total[...] = dot(o_ref[...], block[...])

        @pl.when((j > 0) & (j < OUT_COUNT - 1))
        def _():
            total[...] += dot(a_ref[...], block[...])

        @pl.when(j == OUT_COUNT - 1)
        def _():
            x_copy.wait()
            for rows, columns in tiles(tokens, D):
                y_ref[rows, columns] = (
                    total[rows, columns]
                    + (x_held[rows, columns].astype(F32) + b_ref[:, columns])
                    + dot(a_ref[rows, :], block[:, columns])
                ).astype(y_ref.dtype)

    return call(
        kernel,
        (OUT_COUNT,),
        [stream, attended, hidden, bias] + blocks.arrays,
        [
            pl.BlockSpec(memory_space=pl.ANY),
            whole((tokens, D)),
            pl.BlockSpec((tokens, D), lambda j: (0, jnp.maximum(j - 1, 0))),
            whole((1, D)),
        ]
        + blocks.specs,
        [sds((tokens, D), BF if last else F32)],
        [whole((tokens, D))],
        [pltpu.VMEM((tokens, D), F32), pltpu.VMEM((tokens, D), stream.dtype), pltpu.SemaphoreType.DMA]
        + blocks.scratch,
        8.0,
        "project",
    )[0]


def mlp_back(grad, slope, blocks):
    tokens = grad.shape[0]

    def kernel(g_ref, s_ref, *refs):
        w_refs, refs = refs[: len(blocks.arrays)], refs[len(blocks.arrays) :]
        dy_ref, do_ref, du_ref, dbo_ref, dbu_ref, *fetch = refs
        blocks.bind(w_refs, *fetch)
        j = pl.program_id(0)

        @pl.when(j == 0)
        def _():
            dy = g_ref[...].astype(BF)
            dy_ref[...] = dy
            dbo_ref[...] = jnp.sum(dy.astype(F32), axis=0, keepdims=True)

        block = blocks.step(j)

        @pl.when(j == 0)
        def _():
            do_ref[...] = dot(dy_ref[...], block[...], NT).astype(BF)

        @pl.when(j > 0)
        def _():
            du = (dot(dy_ref[...], block[...], NT) * s_ref[...].astype(F32)).astype(BF)
            du_ref[...] = du
            dbu_ref[...] = jnp.sum(du.astype(F32), axis=0, keepdims=True)

    shifted = pl.BlockSpec((tokens, D), lambda j: (0, jnp.maximum(j - 1, 0)))
    return call(
        kernel,
        (OUT_COUNT,),
        [grad, slope] + blocks.arrays,
        [whole((tokens, D)), shifted] + blocks.specs,
        [
            sds((tokens, D), BF),
            sds((tokens, D), BF),
            sds((tokens, FF), BF),
            sds((1, D), F32),
            sds((1, FF), F32),
        ],
        [
            whole((tokens, D)),
            whole((tokens, D)),
            shifted,
            whole((1, D)),
            pl.BlockSpec((1, D), lambda j: (0, jnp.maximum(j - 1, 0))),
        ],
        blocks.scratch,
        9.0,
        "mlp_back",
    )


def attend_back(grad_o, qkv, unit, inverse, gains):
    tokens = grad_o.shape[0]

    def kernel(do_ref, z_ref, u_ref, i_ref, c_ref, dz_ref, dc_ref):
        low = half_masks(PAD)
        valid = lax.broadcasted_iota(jnp.int32, (PAD, PAD), 0) < SEQ
        top = lax.broadcasted_iota(jnp.int32, (PAIR, PAD), 0) < HEAD_DIM
        mixer = head_mixer()

        @pl.when(pl.program_id(0) == 0)
        def _():
            dc_ref[...] = jnp.zeros_like(dc_ref)

        def norm_back(grad, which, columns):
            at = slice(which * D + columns.start, which * D + columns.stop)
            hats = u_ref[:, at].astype(F32)
            dc_ref[which, :, columns] += jnp.sum(grad * hats, axis=0, keepdims=True)
            pull = grad * c_ref[which, :, columns]
            dz_ref[:, at] = (
                i_ref[:, at] * (pull - head_mean(pull, mixer) - hats * head_mean(pull * hats, mixer))
            ).astype(BF)

        for tile in range(0, D, 768):
            grads_q, grads_k = [], []
            pairs = range(tile, tile + 768, PAIR)
            raw, pulled, keys_t = [], [], []
            for at in pairs:
                query, key, value = (z_ref[:, side + at : side + at + PAIR] for side in (0, D, 2 * D))
                grad = do_ref[:, at : at + PAIR]
                keys_t.append(key.T)
                for query_t, grad_t in zip(split_rows(query.T, top), split_rows(grad.T, top)):
                    raw.append(dot(key, query_t))
                    pulled.append(dot(value, grad_t))
            probs, scores = [], []
            for part, pull in zip(raw, pulled):
                raised = jnp.exp2(part * EXP2_SCALE)
                raised = jnp.where(valid, raised, 0.0)
                share = raised * (1.0 / jnp.sum(raised, axis=0, keepdims=True))
                mixed = share * pull
                row_dot = jnp.sum(mixed, axis=0, keepdims=True)
                probs.append(share.astype(BF))
                scores.append((mixed - share * row_dot).astype(BF))
            for n, at in enumerate(pairs):
                query, grad = z_ref[:, at : at + PAIR], do_ref[:, at : at + PAIR]
                both_v = dot(jnp.concatenate(probs[2 * n : 2 * n + 2], axis=0), grad)
                both_k = dot(jnp.concatenate(scores[2 * n : 2 * n + 2], axis=0), query)
                turned = [
                    dot(keys_t[n][h * HEAD_DIM : (h + 1) * HEAD_DIM], scores[2 * n + h]) for h in (0, 1)
                ]
                grads_q.append((jnp.concatenate(turned, axis=0) * SCALE).astype(BF).T.astype(F32))
                grads_k.append((jnp.where(low, both_k[:PAD], both_k[PAD:]) * SCALE).astype(BF).astype(F32))
                dz_ref[:, 2 * D + at : 2 * D + at + PAIR] = jnp.where(low, both_v[:PAD], both_v[PAD:]).astype(BF)
            for k in range(0, 768, TILE):
                n = k // PAIR
                norm_back(jnp.concatenate(grads_q[n : n + 2], axis=1), 0, slice(tile + k, tile + k + TILE))
                norm_back(jnp.concatenate(grads_k[n : n + 2], axis=1), 1, slice(tile + k, tile + k + TILE))

    def per_image(columns):
        return pl.BlockSpec((PAD, columns), lambda i: (i, 0))

    return call(
        kernel,
        (tokens // PAD,),
        [grad_o, qkv, unit, inverse, gains],
        [per_image(D), per_image(3 * D), per_image(2 * D), per_image(2 * D), whole((2, 1, D))],
        [sds((tokens, 3 * D), BF), sds((2, 1, D), F32)],
        [per_image(3 * D), whole((2, 1, D))],
        [],
        14.0,
        "attend_back",
    )


def weight_grads(segments, cut, name):
    total = sum(count for _, _, count in segments)
    operands, specs, start = [], [], 0
    for left, right, count in segments:
        for side in (left, right):
            side, first, last = (*side, count - 1) if isinstance(side, tuple) else (side, 0, 0)
            tokens = side.shape[0]
            index = functools.partial(
                lambda at, first, last, j: (0, first + jnp.clip(j - at, 0, last)), start, first, last
            )
            operands.append(side)
            specs.append(pl.BlockSpec((tokens, D), index))
        start += count

    def kernel(*refs):
        ins, outs = refs[: len(operands)], refs[len(operands) :]
        j = pl.program_id(0)
        slot = lax.rem(j, 2)

        def leave(block, slot):
            *mine, theirs, held, sems = outs
            rows = D // 8
            copies = []
            for way in WAYS:
                for core, target in enumerate((mine[way].at[block], theirs.at[way, block])):
                    row = pl.multiple_of(piece_row(way, core, rows), 16)
                    copies.append(
                        pltpu.make_async_copy(held.at[slot, pl.ds(row, rows)], target, sems.at[slot, core, way])
                    )
            return copies

        if cut:

            @pl.when(j >= 2)
            def _():
                for copy in leave(j - 2, slot):
                    copy.wait()

        start = 0
        for at, (_, _, count) in enumerate(segments):

            def body(at=at):
                value = dot(ins[2 * at][...], ins[2 * at + 1][...], TN).astype(BF)
                if cut:
                    outs[5][slot] = value
                else:
                    outs[0][0] = value

            if count == total:
                body()
            else:
                pl.when((j >= start) & (j < start + count))(body)
            start += count
        if cut:
            for copy in leave(j, slot):
                copy.start()

            @pl.when(j == total - 1)
            def _():
                if total > 1:
                    for copy in leave(j - 1, 1 - slot):
                        copy.wait()
                for copy in leave(j, slot):
                    copy.wait()

    if cut:
        shapes = [pltpu.HBM((total, D // 8, D), BF)] * 4 + [pltpu.HBM((4, total, D // 8, D), BF)]
        out_specs = [pl.BlockSpec(memory_space=pl.ANY)] * 5
    else:
        shapes = [sds((total, D, D), BF)]
        out_specs = [pl.BlockSpec((1, D, D), lambda j: (j, 0, 0))]
    return list(call(
        kernel,
        (total,),
        operands,
        specs,
        shapes,
        out_specs,
        [pltpu.VMEM((2, D, D), BF), pltpu.SemaphoreType.DMA((2, 2, 4))] if cut else [],
        1.0 + 1.4 * total,
        name,
    ))


def stream_back(grad, stream, gain, grad_u, grad_qkv, blocks):
    tokens = grad.shape[0]

    def kernel(g_ref, x_ref, c_ref, du_ref, dz_ref, *refs):
        w_refs, refs = refs[: len(blocks.arrays)], refs[len(blocks.arrays) :]
        out_ref, dg_ref, total, g_held, x_held, sems, *fetch = refs
        blocks.bind(w_refs, *fetch)
        j = pl.program_id(0)
        late = [
            pltpu.make_async_copy(g_ref, g_held, sems.at[0]),
            pltpu.make_async_copy(x_ref, x_held, sems.at[1]),
        ]
        block = blocks.step(j)

        @pl.when(j == 0)
        def _():
            for copy in late:
                copy.start()
            total[...] = dot(du_ref[...], block[...], NT)

        @pl.when((j > 0) & (j < RATIO))
        def _():
            total[...] += dot(du_ref[...], block[...], NT)

        @pl.when(j >= RATIO)
        def _():
            total[...] += dot(dz_ref[...], block[...], NT)

        @pl.when(j == IN_COUNT - 1)
        def _():
            for copy in late:
                copy.wait()
            sums = 0.0
            for row in range(0, tokens, PAD // 2):
                rows = slice(row, row + PAD // 2)
                unit, inverse = row_parts(x_held[rows, :].astype(F32))
                grad_h = total[rows, :]
                sums = sums + jnp.sum(grad_h * unit, axis=0, keepdims=True)
                hat = grad_h * c_ref[...]
                out_ref[rows, :] = g_held[rows, :].astype(F32) + inverse * (
                    hat
                    - jnp.mean(hat, axis=-1, keepdims=True)
                    - unit * jnp.mean(hat * unit, axis=-1, keepdims=True)
                )
            dg_ref[...] = sums

    return call(
        kernel,
        (IN_COUNT,),
        [grad, stream, gain, grad_u, grad_qkv] + blocks.arrays,
        [
            pl.BlockSpec(memory_space=pl.ANY),
            pl.BlockSpec(memory_space=pl.ANY),
            whole((1, D)),
            pl.BlockSpec((tokens, D), lambda j: (0, jnp.minimum(j, RATIO - 1))),
            pl.BlockSpec((tokens, D), lambda j: (0, jnp.maximum(j - RATIO, 0))),
        ]
        + blocks.specs,
        [sds((tokens, D), F32), sds((1, D), F32)],
        [whole((tokens, D)), whole((1, D))],
        [
            pltpu.VMEM((tokens, D), F32),
            pltpu.VMEM((tokens, D), grad.dtype),
            pltpu.VMEM((tokens, D), stream.dtype),
            pltpu.SemaphoreType.DMA((2,)),
        ]
        + blocks.scratch,
        12.0,
        "stream_back",
    )


def shampoo(grad, full, right, left_root, left_stats, right_stats, weights, ema, first, earlier):
    count, rows, _ = grad.shape

    def products(one, two, block):
        if rows % 16:
            return dot(one, block), dot(two, block)
        both = dot(jnp.concatenate([one, two], axis=0), block)
        return both[:rows], both[rows:]

    def kernel(g_ref, lr_ref, ls_ref, rs_ref, w_ref, e_ref, *refs):
        f_refs, refs = refs[: len(full.arrays)], refs[len(full.arrays) :]
        r_refs, refs = refs[: len(right.arrays)], refs[len(right.arrays) + len(earlier) :]
        go_ref, lo_ref, ro_ref, wo_ref, eo_ref, f_held, f_sems, r_held, r_sems = refs
        full.bind(f_refs, f_held, f_sems)
        right.bind(r_refs, r_held, r_sems)
        j = pl.program_id(0)
        at = lax.axis_index("dp") * rows
        block = full.step(j)[...]
        right_block = right.step(j)[...]
        go_ref[0] = g_ref[0]
        pick = (
            lax.broadcasted_iota(jnp.int32, (rows, D), 1)
            == lax.broadcasted_iota(jnp.int32, (rows, D), 0) + at
        )
        grads, picked, root = (
            part.astype(BF) for part in (g_ref[0], jnp.where(pick, 1.0, 0.0), lr_ref[0])
        )
        turned = block.T
        gram, columns = products(grads, picked, turned)
        own_columns, lifted = products(columns.astype(BF), root, block)
        lo_ref[0] = STAT_DECAY * ls_ref[0] + (1.0 - STAT_DECAY) * gram
        ro_ref[0] = STAT_DECAY * rs_ref[0] + (1.0 - STAT_DECAY) * own_columns
        precond = dot(lifted.astype(BF), right_block)
        renewed = w_ref[0] * (1.0 - RATE_MAT * DECAY_MAT) - RATE_MAT * precond
        wo_ref[0] = renewed
        eo_ref[0] = EMA_DECAY * e_ref[0] + (1.0 - EMA_DECAY) * renewed

    part = pl.BlockSpec((1, rows, D), lambda j: (j, 0, 0))
    own = pl.BlockSpec((1, rows, D), lambda j: (first + j, 0, 0))
    inputs = [grad, left_root, left_stats, right_stats, weights, ema] + full.arrays + right.arrays
    return list(call(
        kernel,
        (count,),
        inputs + list(earlier),
        [part] + [own] * 5 + full.specs + right.specs + [pl.BlockSpec(memory_space=pl.ANY)] * len(earlier),
        [sds(weights.shape, F32)] * 5,
        [own] * 5,
        full.scratch + right.scratch,
        2.0 + 3.0 * count,
        "shampoo",
        {len(inputs) + at: at for at in range(len(earlier))},
    ))


def split_vector(row_vec):
    ends = (D, D + HEAD_DIM, D + 2 * HEAD_DIM, D + 2 * HEAD_DIM + FF)
    ln_gain, q_gain, k_gain, mlp_bias, out_bias = jnp.split(row_vec, ends)
    return (
        ln_gain[None],
        jnp.stack([jnp.tile(q_gain, HEADS)[None], jnp.tile(k_gain, HEADS)[None]]),
        mlp_bias[None],
        out_bias[None],
    )


def pad_tokens(array):
    return jnp.pad(array, ((0, 0), (0, PAD - SEQ), (0, 0))).reshape(-1, D)


def cut_tokens(array):
    return array.reshape(-1, PAD, D)[:, :SEQ]


QKV, MLP, OUT = 0, 3, IN_COUNT
SIZES = {QKV: 3, MLP: RATIO, OUT: OUT_COUNT}


class Collectives:
    cut = False

    def __init__(self, weights, right_root):
        rows = lax.all_gather(weights.astype(BF), "head", axis=0, tiled=True)
        self.blocks = lax.all_gather(rows, "dp", axis=1, tiled=True)
        self.right = lax.all_gather(right_root.astype(BF), "dp", axis=1, tiled=True)
        self.count = weights.shape[0]
        self.parts = {}

    def group(self, *runs):
        return Blocks(
            [
                [(None, [(self.blocks, depth * PER_LAYER + first + at)])]
                for depth, first, count in runs
                for at in range(count)
            ]
        )

    def next(self, array):
        return array

    def done(self, name, array):
        return array

    def add_grads(self, depth, first, pieces):
        self.parts[depth, first] = pieces[0]

    def finish(self, renew):
        partial = jnp.concatenate([self.parts[key] for key in sorted(self.parts)], axis=0)
        rows = lax.psum_scatter(partial, "dp", scatter_dimension=1, tiled=True)
        own = lax.psum_scatter(rows, "head", scatter_dimension=0, tiled=True)
        full = lax.all_gather(own, "dp", axis=1, tiled=True)
        full, right = (
            Blocks([[(None, [(array, at)])] for at in range(self.count)]) for array in (full, self.right)
        )
        return renew(own.astype(F32), full, right, 0, ())

    def vector_sum(self, vectors):
        return lambda: lax.psum(vectors, ("dp", "head"))


DP, LINE = 8, 4
HALF = 3
STEPS = {"core": (1, 1), "x": (2, 2), "y": (4, 4), "first": (2, 4), "second": (4, 2)}
ROUNDS = ((2, 0, 0, 0), (1, 2, 1, 1), (3, 3, 3, 2))


def swap(array, axis):
    return lax.ppermute(array, "dp", [(i, i ^ STEPS[axis][i % 2]) for i in range(DP)])


def hop(array, *pairs):
    return lax.ppermute(array, "head", pairs)


def along(axis):
    return functools.partial(swap, axis=axis)


def over(*pairs):
    return lambda array: hop(array, *pairs)


class PlaneGather:
    def __init__(self, own):
        self.own = own

    def steps(self):
        own = self.own
        first, second, core = along("first"), along("second"), along("core")
        one, two = yield [(own, first), (own, second)]
        three, *others = yield [(one, second), (own, core), (one, core)]
        more = yield [(two, core), (three, core)]
        self.chips = [own, one, two, three]
        self.others = others + more
        self.chips, self.others = (
            [pltpu.with_memory_space_constraint(array, pltpu.HBM) for array in arrays]
            for arrays in (self.chips, self.others)
        )
        yield []

    def pieces(self, at):
        return [(chip, at) for chip in self.chips + self.others]


STEPS_AFTER = {
    "qkv0": [["place4", "line1", "place3", "place5"]],
    "attend0": [["place3", "place4"], ["place3", "place5", "place6"], ["place3"]],
    "mlp0": [["place5", "place6", "place7"], ["place5"]],
    "project0": [["place6", "place7"], ["place6"]],
    "qkv1": [["place7", "right0"]],
    "attend1": [["place7", "right1"]],
    "mlp1": [["right0"]],
    "project1": [["out1", "right0", "right1"]],
    "grad_mlp1": [["out1", "right1"]],
    "attend_back1": [["out1", "mlp1", "right1"]],
    "stream_back1": [["out1", "mlp1", "qkv1"]],
    "mlp_back0": [["mlp1"]],
    "grad_out0": [["out1", "mlp1", "qkv1"]],
    "grad_mlp0": [["out0", "qkv1"]],
    "attend_back0": [["mlp1", "qkv1", "mlp0"]],
    "grad_qkv0": [["out0", "qkv1"], ["out0", "mlp0"]],
    "stream_back0": [["out0", "mlp0", "qkv0"]],
}
FIRST_STEPS = [
    ["line0", "line1"],
    ["place0", "place1"],
    ["place0"],
    ["place1"],
    ["place0", "place1", "line0", "place2", "place4"],
    ["place0", "place1", "place2"],
    ["place2", "place4", "right0"],
    ["place2"],
]
LAST_STEPS = [
    ["sums"],
    ["out0", "mlp0", "qkv0", "sums"],
    ["mlp0", "full3", "qkv0", "sums"],
    ["full3", "qkv0", "sums"],
    ["qkv0", "full3", "full0", "sums"],
    ["full3", "full0", "sums"],
]


class Permutes:
    cut = True

    def __init__(self, weights, right_root):
        self.parts, self.chains, self.asked, self.sent = {}, {}, {}, {}
        own = weights.astype(BF)
        right_root = right_root.astype(BF)
        self.plan = [PlaneGather(own[:HALF]), PlaneGather(own[HALF:])] + [PlaneGather(None) for _ in range(6)]
        self.right = [PlaneGather(right_root[:HALF]), PlaneGather(right_root[HALF:])]
        for at, part in enumerate(self.plan):
            self.chains[f"place{at}"] = part.steps()
        for side in (0, 1):
            self.chains[f"line{side}"] = self.gather_line(side)
            self.chains[f"right{side}"] = self.right[side].steps()
        for group in FIRST_STEPS:
            self.step(group)

    def gather_line(self, side):
        (halves,) = yield [(self.plan[side].own, lambda array: lax.all_gather(array, "head"))]
        head = lax.axis_index("head")
        for at in (0, 1, 2):
            owner = functools.reduce(
                lambda value, z: jnp.where(head == z, ROUNDS[at][z], value), range(1, LINE), ROUNDS[at][0]
            )
            self.plan[2 + 2 * at + side].own = lax.dynamic_index_in_dim(halves, owner, 0, keepdims=False)
        yield []

    def send(self, array=None):
        names = [name for name in self.asked if name not in self.sent]
        asked = [entry for name in names for entry in self.asked[name]]
        operands = [operand for operand, _ in asked]
        if array is not None and operands:
            array, *operands = lax.optimization_barrier((array, *operands))
        for name in names:
            self.sent[name] = [how(operands.pop(0)) for _, how in self.asked[name]]
        return array

    def step(self, group, event=None):
        if any(name in self.asked and name not in self.sent for name in group):
            self.send()
        arrived = [array for name in group for array in self.sent.get(name, [])]
        if arrived:
            event, *arrived = (
                lax.optimization_barrier((event, *arrived))
                if event is not None
                else (None, *lax.optimization_barrier(tuple(arrived)))
            )
        for name in group:
            chain = self.chains[name]
            if name in self.sent:
                self.asked[name] = chain.send([arrived.pop(0) for _ in self.sent.pop(name)])
            else:
                self.asked[name] = next(chain)
        return event

    def done(self, name, array):
        for group in STEPS_AFTER.get(name, ()):
            array = self.step(group, array)
        return array

    def next(self, array):
        return self.send(array)

    def place(self, owner, side, head):
        if head == owner:
            return side
        return next(2 + 2 * at + side for at in (0, 1, 2) if ROUNDS[at][head] == owner)

    def group(self, *runs):
        steps = []
        for depth, first, count in runs:
            for block in range(first, first + count):
                owner, at = 2 * depth + block // (2 * HALF), block % (2 * HALF)
                side, at = at // HALF, at % HALF
                places = [self.place(owner, side, head) for head in range(LINE)]
                steps.append(
                    [
                        (
                            [head for head in range(LINE) if places[head] == place],
                            self.plan[place].pieces(at),
                        )
                        for place in sorted(set(places))
                    ]
                )
        return Blocks(steps)

    def add_grads(self, depth, first, pieces):
        name = {QKV: "qkv", MLP: "mlp"}.get(first, "out") + str(depth)
        self.chains[name] = self.reduce(depth, first, pieces[:4], pieces[4])
        self.step([name])

    def reduce(self, depth, first_block, mine, theirs):
        count = mine[0].shape[0]
        first, second = along("first"), along("second")
        (core,) = yield [(theirs, along("core"))]
        far, to_two = ((mine[way].astype(F32) + core[way].astype(F32)).astype(BF) for way in (3, 2))
        far, two = yield [(far, second), (to_two, second)]
        to_one = (mine[1].astype(F32) + core[1].astype(F32) + far.astype(F32)).astype(BF)
        (one,) = yield [(to_one, first)]
        total = mine[0].astype(F32) + core[0].astype(F32) + one.astype(F32) + two.astype(F32)
        total = total.astype(BF)
        split = min(max(2 * HALF - first_block, 0), count)
        runs = [(side, low, high) for side, low, high in ((0, 0, split), (1, split, count)) if low < high]
        parts = [total[low:high] for _, low, high in runs]
        outer, inner, far_in, far_out = (0, 1, 2, 3) if depth == 0 else (3, 2, 1, 0)
        owners = [2 * depth + side for side, _, _ in runs]
        arrived = yield [
            (part, over((far_out, far_in), (outer if owner == inner else inner, owner)))
            for part, owner in zip(parts, owners)
        ]
        parts = [(part.astype(F32) + other.astype(F32)).astype(BF) for part, other in zip(parts, arrived)]
        arrived = yield [(part, over((far_in, owner))) for part, owner in zip(parts, owners)]
        for (_, low, high), part, other in zip(runs, parts, arrived):
            part = part.astype(F32) + other.astype(F32)
            for at in range(low, high):
                self.parts[depth, first_block + at] = (part, at - low)
        yield []

    def own_blocks(self, low, high):
        head = lax.axis_index("head")
        own = None
        for owner in range(LINE):
            runs = []
            for at in range(low, high):
                part, block = self.parts[owner // 2, 2 * HALF * (owner % 2) + at]
                if runs and runs[-1][0] is part:
                    runs[-1][2] = block + 1
                else:
                    runs.append([part, block, block + 1])
            values = [part[start:stop] for part, start, stop in runs]
            value = values[0] if len(values) == 1 else jnp.concatenate(values, axis=0)
            own = value if own is None else jnp.where(head == owner, value, own)
        return own

    def finish(self, renew):
        self.full = {}
        for low in (HALF, 0):
            self.chains[f"full{low}"] = self.gather_own(low)
        for group in LAST_STEPS:
            self.step(group)
        results = ()
        for low in (HALF, 0):
            own, full = self.full[low]
            if low == 0:
                results[0] = self.step(["full0"], results[0])
                self.step(["full0"])
            results = renew(
                self.next(own),
                Blocks([[(None, full.pieces(at))] for at in range(HALF)]),
                Blocks([[(None, self.right[low // HALF].pieces(at))] for at in range(HALF)]),
                low,
                results,
            )
        return results

    def gather_own(self, low):
        own = self.own_blocks(low, low + HALF)
        full = PlaneGather(own.astype(BF))
        self.full[low] = own, full
        yield from full.steps()

    def vector_sum(self, vectors):
        self.chains["sums"] = self.sum_vectors(vectors)
        return lambda: self.summed

    def sum_vectors(self, vectors):
        for axis in ("core", "x", "y"):
            (other,) = yield [(vectors, along(axis))]
            vectors = vectors + other
        for step in (1, 2):
            (other,) = yield [(vectors, over(*((i, i ^ step) for i in range(LINE))))]
            vectors = vectors + other
        self.summed = vectors
        yield []


def on_device(
    image_tokens,
    cotangent,
    weights,
    weights_ema,
    left_stats,
    right_stats,
    left_root,
    right_root,
    vectors,
    vec_first,
    vec_second,
):
    fits = lax.axis_size("dp") == DP and lax.axis_size("head") == LINE
    links = (Permutes if fits else Collectives)(weights, right_root)
    stream = pad_tokens(image_tokens)
    grad = pad_tokens(cotangent)
    saved = []
    top = LAYERS - 1
    for depth in range(LAYERS):
        ln_gain, gains, mlp_bias, out_bias = split_vector(vectors[depth])
        normed, qkv, unit, inverse = qkv_in(
            links.next(stream), ln_gain, gains, links.group((depth, QKV, 3))
        )
        qkv = links.done(f"qkv{depth}", qkv)
        attended = attend(links.next(qkv))
        attended = links.done(f"attend{depth}", attended)
        hidden, slope = mlp_in(links.next(normed), mlp_bias, links.group((depth, MLP, RATIO)))
        hidden = links.done(f"mlp{depth}", hidden)
        saved.append((stream, normed, hidden, slope, qkv, unit, inverse, attended))
        if depth == top:
            pieces = weight_grads(
                [(links.next(attended), grad, 1), ((hidden, 0), grad, RATIO)], links.cut, "grad_out"
            )
            pieces[0] = links.done(f"grad_out{depth}", pieces[0])
            links.add_grads(depth, OUT, pieces)
        stream = project(
            links.next(stream), attended, hidden, out_bias, links.group((depth, OUT, OUT_COUNT)), depth == top
        )
        stream = links.done(f"project{depth}", stream)
    block_out = cut_tokens(stream)
    vector_parts = [None] * LAYERS
    for depth in reversed(range(LAYERS)):
        ln_gain, gains, _, _ = split_vector(vectors[depth])
        stream, normed, hidden, slope, qkv, unit, inverse, attended = saved[depth]
        dy, do, du, dbo, dbu = mlp_back(links.next(grad), slope, links.group((depth, OUT, OUT_COUNT)))
        dy = links.done(f"mlp_back{depth}", dy)
        share = RATIO if depth == top else RATIO - 1
        if depth < top:
            segments = [(normed, (du, share), RATIO - share), (links.next(attended), dy, 1), ((hidden, 0), dy, RATIO)]
            pieces = weight_grads(segments, links.cut, "grad_out")
            pieces[0] = links.done(f"grad_out{depth}", pieces[0])
            links.add_grads(depth, MLP + share, pieces)
        pieces = weight_grads([(links.next(normed), (du, 0), share)], links.cut, "grad_mlp")
        pieces[0] = links.done(f"grad_mlp{depth}", pieces[0])
        links.add_grads(depth, MLP, pieces)
        dqkv, dgains = attend_back(links.next(do), qkv, unit, inverse, gains)
        dqkv = links.done(f"attend_back{depth}", dqkv)
        pieces = weight_grads([(links.next(normed), (dqkv, 0), 3)], links.cut, "grad_qkv")
        pieces[0] = links.done(f"grad_qkv{depth}", pieces[0])
        links.add_grads(depth, QKV, pieces)
        grad, dg = stream_back(
            links.next(grad), stream, ln_gain, du, dqkv, links.group((depth, MLP, RATIO), (depth, QKV, 3))
        )
        grad = links.done(f"stream_back{depth}", grad)
        vector_parts[depth] = jnp.concatenate(
            [
                dg[0],
                dgains.reshape(2, HEADS, HEAD_DIM).sum(1).reshape(-1),
                dbu[0],
                dbo[0],
            ]
        )
    grad_stream = cut_tokens(grad)
    vector_sum = links.vector_sum(jnp.stack(vector_parts))

    def renew(own, full, right, first, earlier):
        return shampoo(
            own, full, right, left_root, left_stats, right_stats, weights, weights_ema, first, earlier
        )

    weight_grad, left_new, right_new, weight_new, ema_new = links.finish(renew)
    vector_grad = vector_sum()
    first_new = BETA_ONE * vec_first + (1.0 - BETA_ONE) * vector_grad
    second_new = BETA_TWO * vec_second + (1.0 - BETA_TWO) * vector_grad * vector_grad
    first_hat = first_new / (1.0 - BETA_ONE**STEP)
    second_hat = second_new / (1.0 - BETA_TWO**STEP)
    vec_new = vectors - RATE_VEC * first_hat / (jnp.sqrt(second_hat) + ADAM_EPS)
    return (
        block_out,
        grad_stream,
        weight_grad,
        left_new,
        right_new,
        weight_new,
        ema_new,
        first_new,
        second_new,
        vec_new,
    )


def solution(mesh):
    tokens, blocks = P(("dp", "head"), None, None), P("head", "dp", None)
    return jax.shard_map(
        on_device,
        mesh=mesh,
        in_specs=(tokens, tokens) + (blocks,) * 6 + (P(),) * 3,
        out_specs=(tokens, tokens) + (blocks,) * 5 + (P(),) * 3,
        check_vma=False,
    )
```

```python
import functools
import math

import jax
import jax.numpy as jnp
from jax import lax
from jax.experimental import pallas as pl
from jax.experimental.pallas import tpu as pltpu
from jax.sharding import PartitionSpec as P

D = 768
HEADS = 12
HEAD_DIM = 64
FF = 3072
SEQ = 196
PAD = 208
LAYERS = 2
STEP = 10
RATIO = FF // D
IN_COUNT = 3 + RATIO
OUT_COUNT = 1 + RATIO
PER_LAYER = IN_COUNT + OUT_COUNT
PAIR = 2 * HEAD_DIM
TILE = 256

EPS_NORM = 1e-06
BETA_ONE = 0.9
BETA_TWO = 0.95
ADAM_EPS = 1e-08
RATE_VEC = 0.3
RATE_MAT = 0.003
DECAY_MAT = 0.1
STAT_DECAY = 0.5
EMA_DECAY = 0.8
SCALE = HEAD_DIM ** (-0.5)
EXP2_SCALE = SCALE * math.log2(math.e)

BF = jnp.bfloat16
F32 = jnp.float32
NN = (((1,), (0,)), ((), ()))
NT = (((1,), (1,)), ((), ()))
TN = (((0,), (0,)), ((), ()))


def dot(a, b, dims=NN):
    return lax.dot_general(a, b, dims, preferred_element_type=F32)


def call(kernel, grid, operands, in_specs, outs, out_specs, scratch, about_us, name, aliases=None):
    moved = sum(o.size * o.dtype.itemsize for o in operands) + sum(
        math.prod(o.shape) * o.dtype.itemsize for o in outs
    )
    return pl.pallas_call(
        kernel,
        grid=grid,
        in_specs=in_specs,
        out_specs=out_specs,
        out_shape=outs,
        scratch_shapes=scratch,
        compiler_params=pltpu.CompilerParams(vmem_limit_bytes=24 * 1024 * 1024),
        cost_estimate=pl.CostEstimate(flops=int(about_us * 1.1e9), bytes_accessed=moved, transcendentals=0),
        input_output_aliases=aliases or {},
        name=name,
    )(*operands)


def whole(shape):
    return pl.BlockSpec(shape, lambda *ids: (0,) * len(shape))


def sds(shape, dtype):
    return jax.ShapeDtypeStruct(shape, dtype)


WAYS = (0, 1, 2, 3)


class Blocks:
    def __init__(self, steps):
        self.steps = steps
        self.arrays = []
        for places in steps:
            for _, pieces in places:
                for array, _ in pieces:
                    if not any(array is other for other in self.arrays):
                        self.arrays.append(array)
        self.count = len(steps[0][0][1])
        self.specs = [pl.BlockSpec(memory_space=pltpu.HBM)] * len(self.arrays)
        self.scratch = [pltpu.VMEM((2, D, D), BF), pltpu.SemaphoreType.DMA((2, self.count))]

    def bind(self, refs, held, sems):
        self.refs, self.held, self.sems = refs, held, sems

    def copies(self, pieces, slot):
        made = []
        for at, (array, block) in enumerate(pieces):
            ref = next(ref for ref, other in zip(self.refs, self.arrays) if other is array)
            target = self.held.at[slot]
            if self.count > 1:
                rows = array.shape[-2]
                row = piece_row(at % 4, at // 4, rows)
                target = self.held.at[slot, pl.ds(pl.multiple_of(row, 16), rows)]
            made.append(pltpu.make_async_copy(ref.at[block], target, self.sems.at[slot, at]))
        return made

    def start(self, j, wanted):
        head = lax.axis_index("head")
        for step, places in enumerate(self.steps):
            for owners, pieces in places:
                here = wanted == step
                if owners is not None:
                    here = here & functools.reduce(lambda a, b: a | b, [head == owner for owner in owners])

                @pl.when(here)
                def _(step=step, pieces=pieces):
                    for copy in self.copies(pieces, step % 2):
                        copy.start()

    def step(self, j):
        @pl.when(j == 0)
        def _():
            self.start(j, j)

        @pl.when(j + 1 < len(self.steps))
        def _():
            self.start(j, j + 1)

        slot = lax.rem(j, 2)
        for copy in self.copies(self.steps[0][0][1], slot):
            copy.wait()
        return self.held.at[slot]


def piece_row(way, dc, rows):
    me = lax.axis_index("dp")
    core, x, y = lax.rem(me, 2), lax.rem(me // 2, 2), me // 4
    core = 1 - core if dc else core
    dx, dy = ((0, 0), (1 - core, core), (core, 1 - core), (1, 1))[way]
    return ((y + dy - 2 * y * dy) * 4 + (x + dx - 2 * x * dx) * 2 + core) * rows


def row_parts(values):
    average = jnp.mean(values, axis=-1, keepdims=True)
    centred = values - average
    inverse = lax.rsqrt(jnp.mean(centred * centred, axis=-1, keepdims=True) + EPS_NORM)
    return centred * inverse, inverse


def head_mixer():
    row = lax.broadcasted_iota(jnp.int32, (TILE, TILE), 0) // HEAD_DIM
    column = lax.broadcasted_iota(jnp.int32, (TILE, TILE), 1) // HEAD_DIM
    return jnp.where(row == column, 1.0 / HEAD_DIM, 0.0).astype(BF)


def head_mean(values, mixer):
    high = values.astype(BF)
    low = (values - high.astype(F32)).astype(BF)
    return dot(high, mixer) + dot(low, mixer)


def gelu_parts(z):
    decay = jnp.exp2(z * z * (-0.5 * math.log2(math.e)))
    t = 1.0 / (1.0 + (0.3275911 * math.sqrt(0.5)) * jnp.abs(z))
    poly = 0.5 * 1.061405429
    for factor in (-1.453152027, 1.421413741, -0.284496736, 0.254829592):
        poly = poly * t + 0.5 * factor
    tail = poly * t * decay
    share = jnp.where(z >= 0, 1.0 - tail, tail)
    return z * share, share + z * decay * (1.0 / math.sqrt(2.0 * math.pi))


def tiles(rows, columns):
    return [(slice(r, r + PAD), slice(c, c + TILE)) for r in range(0, rows, PAD) for c in range(0, columns, TILE)]


def mlp_in(normed, bias, blocks):
    tokens = normed.shape[0]

    def kernel(h_ref, b_ref, *refs):
        w_refs, (a_ref, s_ref, *fetch) = refs[: len(blocks.arrays)], refs[len(blocks.arrays) :]
        blocks.bind(w_refs, *fetch)
        block = blocks.step(pl.program_id(0))
        spots = tiles(tokens, D)
        wide = [dot(h_ref[rows, :], block[:, columns]) for rows, columns in spots]
        for (rows, columns), z in zip(spots, wide):
            act, slope = gelu_parts(z + b_ref[:, columns])
            a_ref[rows, columns] = act.astype(BF)
            s_ref[rows, columns] = slope.astype(BF)

    return call(
        kernel,
        (RATIO,),
        [normed, bias] + blocks.arrays,
        [whole((tokens, D)), pl.BlockSpec((1, D), lambda j: (0, j))] + blocks.specs,
        [sds((tokens, FF), BF), sds((tokens, FF), BF)],
        [pl.BlockSpec((tokens, D), lambda j: (0, j))] * 2,
        blocks.scratch,
        11.0,
        "mlp_in",
    )


def half_masks(rows):
    low = lax.broadcasted_iota(jnp.int32, (rows, PAIR), 1) < HEAD_DIM
    return low


def split_pair(values, low):
    zero = jnp.zeros_like(values)
    return jnp.where(low, values, zero), jnp.where(low, zero, values)


def split_rows(values, top):
    zero = jnp.zeros_like(values)
    return jnp.where(top, values, zero), jnp.where(top, zero, values)


def qkv_in(stream, ln_gain, gains, blocks):
    tokens = stream.shape[0]

    def kernel(x_ref, g_ref, c_ref, *refs):
        w_refs, (h_ref, n_ref, u_ref, i_ref, *fetch) = refs[: len(blocks.arrays)], refs[len(blocks.arrays) :]
        blocks.bind(w_refs, *fetch)
        j = pl.program_id(0)

        @pl.when(j == 0)
        def _():
            for row in range(0, tokens, PAD):
                rows = slice(row, row + PAD)
                unit, _ = row_parts(x_ref[rows, :].astype(F32))
                h_ref[rows, :] = (unit * g_ref[...]).astype(BF)

        block = blocks.step(j)

        @pl.when(j < 2)
        def _():
            mixer = head_mixer()
            spots = tiles(tokens, D)
            raws = [dot(h_ref[rows, :], block[:, columns]) for rows, columns in spots]
            centred = [raw - head_mean(raw, mixer) for raw in raws]
            spreads = [head_mean(part * part, mixer) for part in centred]
            for (rows, columns), part, spread in zip(spots, centred, spreads):
                inverse = lax.rsqrt(spread + EPS_NORM)
                unit = part * inverse
                n_ref[rows, columns] = (unit * c_ref[0, :, columns]).astype(BF)
                u_ref[rows, columns] = unit.astype(BF)
                i_ref[rows, columns] = inverse

        @pl.when(j == 2)
        def _():
            n_ref[...] = dot(h_ref[...], block[...]).astype(BF)

    first_two = lambda j: (0, jnp.minimum(j, 1))
    return call(
        kernel,
        (3,),
        [stream, ln_gain, gains] + blocks.arrays,
        [
            whole((tokens, D)),
            whole((1, D)),
            pl.BlockSpec((1, 1, D), lambda j: (jnp.minimum(j, 1), 0, 0)),
        ]
        + blocks.specs,
        [
            sds((tokens, D), BF),
            sds((tokens, 3 * D), BF),
            sds((tokens, 2 * D), BF),
            sds((tokens, 2 * D), F32),
        ],
        [
            whole((tokens, D)),
            pl.BlockSpec((tokens, D), lambda j: (0, j)),
            pl.BlockSpec((tokens, D), first_two),
            pl.BlockSpec((tokens, D), first_two),
        ],
        blocks.scratch,
        9.0,
        "qkv_in",
    )


def attend(qkv):
    tokens = qkv.shape[0]

    def kernel(z_ref, o_ref):
        low = half_masks(PAD)
        valid = lax.broadcasted_iota(jnp.int32, (PAD, PAD), 1) < SEQ
        raw = []
        for at in range(0, D, PAIR):
            keys = z_ref[:, D + at : D + at + PAIR]
            raw += [dot(query, keys, NT) for query in split_pair(z_ref[:, at : at + PAIR], low)]
        raised = [jnp.where(valid, jnp.exp2(part * EXP2_SCALE), 0.0) for part in raw]
        shares = [1.0 / jnp.sum(part, axis=1, keepdims=True) for part in raised]
        for pair, at in enumerate(range(0, D, PAIR)):
            values = z_ref[:, 2 * D + at : 2 * D + at + PAIR]
            sides = [dot(raised[n].astype(BF), values) * shares[n] for n in (2 * pair, 2 * pair + 1)]
            o_ref[:, at : at + PAIR] = jnp.where(low, sides[0], sides[1]).astype(BF)

    return call(
        kernel,
        (tokens // PAD,),
        [qkv],
        [pl.BlockSpec((PAD, 3 * D), lambda i: (i, 0))],
        [sds((tokens, D), BF)],
        [pl.BlockSpec((PAD, D), lambda i: (i, 0))],
        [],
        8.0,
        "attend",
    )[0]


def project(stream, attended, hidden, bias, blocks, last):
    tokens = stream.shape[0]

    def kernel(x_ref, o_ref, a_ref, b_ref, *refs):
        w_refs, (y_ref, total, x_held, x_sem, *fetch) = refs[: len(blocks.arrays)], refs[len(blocks.arrays) :]
        blocks.bind(w_refs, *fetch)
        j = pl.program_id(0)
        x_copy = pltpu.make_async_copy(x_ref, x_held, x_sem)
        block = blocks.step(j)

        @pl.when(j == 0)
        def _():
            x_copy.start()
            total[...] = dot(o_ref[...], block[...])

        @pl.when((j > 0) & (j < OUT_COUNT - 1))
        def _():
            total[...] += dot(a_ref[...], block[...])

        @pl.when(j == OUT_COUNT - 1)
        def _():
            x_copy.wait()
            for rows, columns in tiles(tokens, D):
                y_ref[rows, columns] = (
                    total[rows, columns]
                    + (x_held[rows, columns].astype(F32) + b_ref[:, columns])
                    + dot(a_ref[rows, :], block[:, columns])
                ).astype(y_ref.dtype)

    return call(
        kernel,
        (OUT_COUNT,),
        [stream, attended, hidden, bias] + blocks.arrays,
        [
            pl.BlockSpec(memory_space=pl.ANY),
            whole((tokens, D)),
            pl.BlockSpec((tokens, D), lambda j: (0, jnp.maximum(j - 1, 0))),
            whole((1, D)),
        ]
        + blocks.specs,
        [sds((tokens, D), BF if last else F32)],
        [whole((tokens, D))],
        [pltpu.VMEM((tokens, D), F32), pltpu.VMEM((tokens, D), stream.dtype), pltpu.SemaphoreType.DMA]
        + blocks.scratch,
        8.0,
        "project",
    )[0]


def mlp_back(grad, slope, blocks):
    tokens = grad.shape[0]

    def kernel(g_ref, s_ref, *refs):
        w_refs, refs = refs[: len(blocks.arrays)], refs[len(blocks.arrays) :]
        dy_ref, do_ref, du_ref, dbo_ref, dbu_ref, *fetch = refs
        blocks.bind(w_refs, *fetch)
        j = pl.program_id(0)

        @pl.when(j == 0)
        def _():
            dy = g_ref[...].astype(BF)
            dy_ref[...] = dy
            dbo_ref[...] = jnp.sum(dy.astype(F32), axis=0, keepdims=True)

        block = blocks.step(j)

        @pl.when(j == 0)
        def _():
            do_ref[...] = dot(dy_ref[...], block[...], NT).astype(BF)

        @pl.when(j > 0)
        def _():
            du = (dot(dy_ref[...], block[...], NT) * s_ref[...].astype(F32)).astype(BF)
            du_ref[...] = du
            dbu_ref[...] = jnp.sum(du.astype(F32), axis=0, keepdims=True)

    shifted = pl.BlockSpec((tokens, D), lambda j: (0, jnp.maximum(j - 1, 0)))
    return call(
        kernel,
        (OUT_COUNT,),
        [grad, slope] + blocks.arrays,
        [whole((tokens, D)), shifted] + blocks.specs,
        [
            sds((tokens, D), BF),
            sds((tokens, D), BF),
            sds((tokens, FF), BF),
            sds((1, D), F32),
            sds((1, FF), F32),
        ],
        [
            whole((tokens, D)),
            whole((tokens, D)),
            shifted,
            whole((1, D)),
            pl.BlockSpec((1, D), lambda j: (0, jnp.maximum(j - 1, 0))),
        ],
        blocks.scratch,
        9.0,
        "mlp_back",
    )


def attend_back(grad_o, qkv, unit, inverse, gains):
    tokens = grad_o.shape[0]

    def kernel(do_ref, z_ref, u_ref, i_ref, c_ref, dz_ref, dc_ref):
        low = half_masks(PAD)
        valid = lax.broadcasted_iota(jnp.int32, (PAD, PAD), 0) < SEQ
        top = lax.broadcasted_iota(jnp.int32, (PAIR, PAD), 0) < HEAD_DIM
        mixer = head_mixer()

        @pl.when(pl.program_id(0) == 0)
        def _():
            dc_ref[...] = jnp.zeros_like(dc_ref)

        def norm_back(grad, which, columns):
            at = slice(which * D + columns.start, which * D + columns.stop)
            hats = u_ref[:, at].astype(F32)
            dc_ref[which, :, columns] += jnp.sum(grad * hats, axis=0, keepdims=True)
            pull = grad * c_ref[which, :, columns]
            dz_ref[:, at] = (
                i_ref[:, at] * (pull - head_mean(pull, mixer) - hats * head_mean(pull * hats, mixer))
            ).astype(BF)

        for tile in range(0, D, 768):
            grads_q, grads_k = [], []
            pairs = range(tile, tile + 768, PAIR)
            raw, pulled, keys_t = [], [], []
            for at in pairs:
                query, key, value = (z_ref[:, side + at : side + at + PAIR] for side in (0, D, 2 * D))
                grad = do_ref[:, at : at + PAIR]
                keys_t.append(key.T)
                for query_t, grad_t in zip(split_rows(query.T, top), split_rows(grad.T, top)):
                    raw.append(dot(key, query_t))
                    pulled.append(dot(value, grad_t))
            probs, scores = [], []
            for part, pull in zip(raw, pulled):
                raised = jnp.exp2(part * EXP2_SCALE)
                raised = jnp.where(valid, raised, 0.0)
                share = raised * (1.0 / jnp.sum(raised, axis=0, keepdims=True))
                mixed = share * pull
                row_dot = jnp.sum(mixed, axis=0, keepdims=True)
                probs.append(share.astype(BF))
                scores.append((mixed - share * row_dot).astype(BF))
            for n, at in enumerate(pairs):
                query, grad = z_ref[:, at : at + PAIR], do_ref[:, at : at + PAIR]
                both_v = dot(jnp.concatenate(probs[2 * n : 2 * n + 2], axis=0), grad)
                both_k = dot(jnp.concatenate(scores[2 * n : 2 * n + 2], axis=0), query)
                turned = [
                    dot(keys_t[n][h * HEAD_DIM : (h + 1) * HEAD_DIM], scores[2 * n + h]) for h in (0, 1)
                ]
                grads_q.append((jnp.concatenate(turned, axis=0) * SCALE).astype(BF).T.astype(F32))
                grads_k.append((jnp.where(low, both_k[:PAD], both_k[PAD:]) * SCALE).astype(BF).astype(F32))
                dz_ref[:, 2 * D + at : 2 * D + at + PAIR] = jnp.where(low, both_v[:PAD], both_v[PAD:]).astype(BF)
            for k in range(0, 768, TILE):
                n = k // PAIR
                norm_back(jnp.concatenate(grads_q[n : n + 2], axis=1), 0, slice(tile + k, tile + k + TILE))
                norm_back(jnp.concatenate(grads_k[n : n + 2], axis=1), 1, slice(tile + k, tile + k + TILE))

    def per_image(columns):
        return pl.BlockSpec((PAD, columns), lambda i: (i, 0))

    return call(
        kernel,
        (tokens // PAD,),
        [grad_o, qkv, unit, inverse, gains],
        [per_image(D), per_image(3 * D), per_image(2 * D), per_image(2 * D), whole((2, 1, D))],
        [sds((tokens, 3 * D), BF), sds((2, 1, D), F32)],
        [per_image(3 * D), whole((2, 1, D))],
        [],
        14.0,
        "attend_back",
    )


def weight_grads(segments, cut, name):
    total = sum(count for _, _, count in segments)
    operands, specs, start = [], [], 0
    for left, right, count in segments:
        for side in (left, right):
            side, first, last = (*side, count - 1) if isinstance(side, tuple) else (side, 0, 0)
            tokens = side.shape[0]
            index = functools.partial(
                lambda at, first, last, j: (0, first + jnp.clip(j - at, 0, last)), start, first, last
            )
            operands.append(side)
            specs.append(pl.BlockSpec((tokens, D), index))
        start += count

    def kernel(*refs):
        ins, outs = refs[: len(operands)], refs[len(operands) :]
        j = pl.program_id(0)
        slot = lax.rem(j, 2)

        def leave(block, slot):
            *mine, theirs, held, sems = outs
            rows = D // 8
            copies = []
            for way in WAYS:
                for core, target in enumerate((mine[way].at[block], theirs.at[way, block])):
                    row = pl.multiple_of(piece_row(way, core, rows), 16)
                    copies.append(
                        pltpu.make_async_copy(held.at[slot, pl.ds(row, rows)], target, sems.at[slot, core, way])
                    )
            return copies

        if cut:

            @pl.when(j >= 2)
            def _():
                for copy in leave(j - 2, slot):
                    copy.wait()

        start = 0
        for at, (_, _, count) in enumerate(segments):

            def body(at=at):
                value = dot(ins[2 * at][...], ins[2 * at + 1][...], TN).astype(BF)
                if cut:
                    outs[5][slot] = value
                else:
                    outs[0][0] = value

            if count == total:
                body()
            else:
                pl.when((j >= start) & (j < start + count))(body)
            start += count
        if cut:
            for copy in leave(j, slot):
                copy.start()

            @pl.when(j == total - 1)
            def _():
                if total > 1:
                    for copy in leave(j - 1, 1 - slot):
                        copy.wait()
                for copy in leave(j, slot):
                    copy.wait()

    if cut:
        shapes = [pltpu.HBM((total, D // 8, D), BF)] * 4 + [pltpu.HBM((4, total, D // 8, D), BF)]
        out_specs = [pl.BlockSpec(memory_space=pl.ANY)] * 5
    else:
        shapes = [sds((total, D, D), BF)]
        out_specs = [pl.BlockSpec((1, D, D), lambda j: (j, 0, 0))]
    return list(call(
        kernel,
        (total,),
        operands,
        specs,
        shapes,
        out_specs,
        [pltpu.VMEM((2, D, D), BF), pltpu.SemaphoreType.DMA((2, 2, 4))] if cut else [],
        1.0 + 1.4 * total,
        name,
    ))


def stream_back(grad, stream, gain, grad_u, grad_qkv, blocks):
    tokens = grad.shape[0]

    def kernel(g_ref, x_ref, c_ref, du_ref, dz_ref, *refs):
        w_refs, refs = refs[: len(blocks.arrays)], refs[len(blocks.arrays) :]
        out_ref, dg_ref, total, g_held, x_held, sems, *fetch = refs
        blocks.bind(w_refs, *fetch)
        j = pl.program_id(0)
        late = [
            pltpu.make_async_copy(g_ref, g_held, sems.at[0]),
            pltpu.make_async_copy(x_ref, x_held, sems.at[1]),
        ]
        block = blocks.step(j)

        @pl.when(j == 0)
        def _():
            for copy in late:
                copy.start()
            total[...] = dot(du_ref[...], block[...], NT)

        @pl.when((j > 0) & (j < RATIO))
        def _():
            total[...] += dot(du_ref[...], block[...], NT)

        @pl.when(j >= RATIO)
        def _():
            total[...] += dot(dz_ref[...], block[...], NT)

        @pl.when(j == IN_COUNT - 1)
        def _():
            for copy in late:
                copy.wait()
            sums = 0.0
            for row in range(0, tokens, PAD // 2):
                rows = slice(row, row + PAD // 2)
                unit, inverse = row_parts(x_held[rows, :].astype(F32))
                grad_h = total[rows, :]
                sums = sums + jnp.sum(grad_h * unit, axis=0, keepdims=True)
                hat = grad_h * c_ref[...]
                out_ref[rows, :] = g_held[rows, :].astype(F32) + inverse * (
                    hat
                    - jnp.mean(hat, axis=-1, keepdims=True)
                    - unit * jnp.mean(hat * unit, axis=-1, keepdims=True)
                )
            dg_ref[...] = sums

    return call(
        kernel,
        (IN_COUNT,),
        [grad, stream, gain, grad_u, grad_qkv] + blocks.arrays,
        [
            pl.BlockSpec(memory_space=pl.ANY),
            pl.BlockSpec(memory_space=pl.ANY),
            whole((1, D)),
            pl.BlockSpec((tokens, D), lambda j: (0, jnp.minimum(j, RATIO - 1))),
            pl.BlockSpec((tokens, D), lambda j: (0, jnp.maximum(j - RATIO, 0))),
        ]
        + blocks.specs,
        [sds((tokens, D), F32), sds((1, D), F32)],
        [whole((tokens, D)), whole((1, D))],
        [
            pltpu.VMEM((tokens, D), F32),
            pltpu.VMEM((tokens, D), grad.dtype),
            pltpu.VMEM((tokens, D), stream.dtype),
            pltpu.SemaphoreType.DMA((2,)),
        ]
        + blocks.scratch,
        12.0,
        "stream_back",
    )


def shampoo(grad, full, right, left_root, left_stats, right_stats, weights, ema, first, earlier):
    count, rows, _ = grad.shape

    def products(one, two, block):
        if rows % 16:
            return dot(one, block), dot(two, block)
        both = dot(jnp.concatenate([one, two], axis=0), block)
        return both[:rows], both[rows:]

    def kernel(g_ref, lr_ref, ls_ref, rs_ref, w_ref, e_ref, *refs):
        f_refs, refs = refs[: len(full.arrays)], refs[len(full.arrays) :]
        r_refs, refs = refs[: len(right.arrays)], refs[len(right.arrays) + len(earlier) :]
        go_ref, lo_ref, ro_ref, wo_ref, eo_ref, f_held, f_sems, r_held, r_sems = refs
        full.bind(f_refs, f_held, f_sems)
        right.bind(r_refs, r_held, r_sems)
        j = pl.program_id(0)
        at = lax.axis_index("dp") * rows
        block = full.step(j)[...]
        right_block = right.step(j)[...]
        go_ref[0] = g_ref[0]
        pick = (
            lax.broadcasted_iota(jnp.int32, (rows, D), 1)
            == lax.broadcasted_iota(jnp.int32, (rows, D), 0) + at
        )
        grads, picked, root = (
            part.astype(BF) for part in (g_ref[0], jnp.where(pick, 1.0, 0.0), lr_ref[0])
        )
        turned = block.T
        gram, columns = products(grads, picked, turned)
        own_columns, lifted = products(columns.astype(BF), root, block)
        lo_ref[0] = STAT_DECAY * ls_ref[0] + (1.0 - STAT_DECAY) * gram
        ro_ref[0] = STAT_DECAY * rs_ref[0] + (1.0 - STAT_DECAY) * own_columns
        precond = dot(lifted.astype(BF), right_block)
        renewed = w_ref[0] * (1.0 - RATE_MAT * DECAY_MAT) - RATE_MAT * precond
        wo_ref[0] = renewed
        eo_ref[0] = EMA_DECAY * e_ref[0] + (1.0 - EMA_DECAY) * renewed

    part = pl.BlockSpec((1, rows, D), lambda j: (j, 0, 0))
    own = pl.BlockSpec((1, rows, D), lambda j: (first + j, 0, 0))
    inputs = [grad, left_root, left_stats, right_stats, weights, ema] + full.arrays + right.arrays
    return list(call(
        kernel,
        (count,),
        inputs + list(earlier),
        [part] + [own] * 5 + full.specs + right.specs + [pl.BlockSpec(memory_space=pl.ANY)] * len(earlier),
        [sds(weights.shape, F32)] * 5,
        [own] * 5,
        full.scratch + right.scratch,
        2.0 + 3.0 * count,
        "shampoo",
        {len(inputs) + at: at for at in range(len(earlier))},
    ))


def split_vector(row_vec):
    ends = (D, D + HEAD_DIM, D + 2 * HEAD_DIM, D + 2 * HEAD_DIM + FF)
    ln_gain, q_gain, k_gain, mlp_bias, out_bias = jnp.split(row_vec, ends)
    return (
        ln_gain[None],
        jnp.stack([jnp.tile(q_gain, HEADS)[None], jnp.tile(k_gain, HEADS)[None]]),
        mlp_bias[None],
        out_bias[None],
    )


def pad_tokens(array):
    return jnp.pad(array, ((0, 0), (0, PAD - SEQ), (0, 0))).reshape(-1, D)


def cut_tokens(array):
    return array.reshape(-1, PAD, D)[:, :SEQ]


QKV, MLP, OUT = 0, 3, IN_COUNT
SIZES = {QKV: 3, MLP: RATIO, OUT: OUT_COUNT}


class Collectives:
    cut = False

    def __init__(self, weights, right_root):
        rows = lax.all_gather(weights.astype(BF), "head", axis=0, tiled=True)
        self.blocks = lax.all_gather(rows, "dp", axis=1, tiled=True)
        self.right = lax.all_gather(right_root.astype(BF), "dp", axis=1, tiled=True)
        self.count = weights.shape[0]
        self.parts = {}

    def group(self, *runs):
        return Blocks(
            [
                [(None, [(self.blocks, depth * PER_LAYER + first + at)])]
                for depth, first, count in runs
                for at in range(count)
            ]
        )

    def next(self, array):
        return array

    def done(self, name, array):
        return array

    def add_grads(self, depth, first, pieces):
        self.parts[depth, first] = pieces[0]

    def finish(self, renew):
        partial = jnp.concatenate([self.parts[key] for key in sorted(self.parts)], axis=0)
        rows = lax.psum_scatter(partial, "dp", scatter_dimension=1, tiled=True)
        own = lax.psum_scatter(rows, "head", scatter_dimension=0, tiled=True)
        full = lax.all_gather(own, "dp", axis=1, tiled=True)
        full, right = (
            Blocks([[(None, [(array, at)])] for at in range(self.count)]) for array in (full, self.right)
        )
        return renew(own.astype(F32), full, right, 0, ())

    def vector_sum(self, vectors):
        return lambda: lax.psum(vectors, ("dp", "head"))


DP, LINE = 8, 4
HALF = 3
STEPS = {"core": (1, 1), "x": (2, 2), "y": (4, 4), "first": (2, 4), "second": (4, 2)}
ROUNDS = ((2, 0, 0, 0), (1, 2, 1, 1), (3, 3, 3, 2))


def swap(array, axis):
    return lax.ppermute(array, "dp", [(i, i ^ STEPS[axis][i % 2]) for i in range(DP)])


def hop(array, *pairs):
    return lax.ppermute(array, "head", pairs)


def along(axis):
    return functools.partial(swap, axis=axis)


def over(*pairs):
    return lambda array: hop(array, *pairs)


class PlaneGather:
    def __init__(self, own):
        self.own = own

    def steps(self):
        own = self.own
        first, second, core = along("first"), along("second"), along("core")
        one, two = yield [(own, first), (own, second)]
        three, *others = yield [(one, second), (own, core), (one, core)]
        more = yield [(two, core), (three, core)]
        self.chips = [own, one, two, three]
        self.others = others + more
        self.chips, self.others = (
            [pltpu.with_memory_space_constraint(array, pltpu.HBM) for array in arrays]
            for arrays in (self.chips, self.others)
        )
        yield []

    def pieces(self, at):
        return [(chip, at) for chip in self.chips + self.others]


STEPS_AFTER = {
    "qkv0": [["place4", "line1", "place3", "place5"]],
    "attend0": [["place3", "place4"], ["place3", "place5", "place6"], ["place3"]],
    "mlp0": [["place5", "place6", "place7"], ["place5"]],
    "project0": [["place6", "place7"], ["place6"]],
    "qkv1": [["place7", "right0"]],
    "attend1": [["place7", "right1"]],
    "mlp1": [["right0"]],
    "project1": [["out1", "right0", "right1"]],
    "grad_mlp1": [["out1", "right1"]],
    "attend_back1": [["out1", "mlp1", "right1"]],
    "stream_back1": [["out1", "mlp1", "qkv1"]],
    "mlp_back0": [["mlp1"]],
    "grad_out0": [["out1", "mlp1", "qkv1"]],
    "grad_mlp0": [["out0", "qkv1"]],
    "attend_back0": [["mlp1", "qkv1", "mlp0"]],
    "grad_qkv0": [["out0", "qkv1"], ["out0", "mlp0"]],
    "stream_back0": [["out0", "mlp0", "qkv0"]],
}
FIRST_STEPS = [
    ["line0", "line1"],
    ["place0", "place1"],
    ["place0"],
    ["place1"],
    ["place0", "place1", "line0", "place2", "place4"],
    ["place0", "place1", "place2"],
    ["place2", "place4", "right0"],
    ["place2"],
]
LAST_STEPS = [
    ["sums"],
    ["out0", "mlp0", "qkv0", "sums"],
    ["mlp0", "full3", "qkv0", "sums"],
    ["full3", "qkv0", "sums"],
    ["qkv0", "full3", "full0", "sums"],
    ["full3", "full0", "sums"],
]


class Permutes:
    cut = True

    def __init__(self, weights, right_root):
        self.parts, self.chains, self.asked, self.sent = {}, {}, {}, {}
        own, right_root = ([part[:HALF].astype(BF), part[HALF:].astype(BF)] for part in (weights, right_root))
        self.plan = [PlaneGather(own[0]), PlaneGather(own[1])] + [PlaneGather(None) for _ in range(6)]
        self.right = [PlaneGather(right_root[0]), PlaneGather(right_root[1])]
        for at, part in enumerate(self.plan):
            self.chains[f"place{at}"] = part.steps()
        for side in (0, 1):
            self.chains[f"line{side}"] = self.gather_line(side)
            self.chains[f"right{side}"] = self.right[side].steps()
        for group in FIRST_STEPS:
            self.step(group)

    def gather_line(self, side):
        (halves,) = yield [(self.plan[side].own, lambda array: lax.all_gather(array, "head"))]
        head = lax.axis_index("head")
        for at in (0, 1, 2):
            owner = functools.reduce(
                lambda value, z: jnp.where(head == z, ROUNDS[at][z], value), range(1, LINE), ROUNDS[at][0]
            )
            self.plan[2 + 2 * at + side].own = lax.dynamic_index_in_dim(halves, owner, 0, keepdims=False)
        yield []

    def send(self, array=None):
        names = [name for name in self.asked if name not in self.sent]
        asked = [entry for name in names for entry in self.asked[name]]
        operands = [operand for operand, _ in asked]
        if array is not None and operands:
            array, *operands = lax.optimization_barrier((array, *operands))
        for name in names:
            self.sent[name] = [how(operands.pop(0)) for _, how in self.asked[name]]
        return array

    def step(self, group, event=None):
        if any(name in self.asked and name not in self.sent for name in group):
            self.send()
        arrived = [array for name in group for array in self.sent.get(name, [])]
        if arrived:
            event, *arrived = (
                lax.optimization_barrier((event, *arrived))
                if event is not None
                else (None, *lax.optimization_barrier(tuple(arrived)))
            )
        for name in group:
            chain = self.chains[name]
            if name in self.sent:
                self.asked[name] = chain.send([arrived.pop(0) for _ in self.sent.pop(name)])
            else:
                self.asked[name] = next(chain)
        return event

    def done(self, name, array):
        for group in STEPS_AFTER.get(name, ()):
            array = self.step(group, array)
        return array

    def next(self, array):
        return self.send(array)

    def place(self, owner, side, head):
        if head == owner:
            return side
        return next(2 + 2 * at + side for at in (0, 1, 2) if ROUNDS[at][head] == owner)

    def group(self, *runs):
        steps = []
        for depth, first, count in runs:
            for block in range(first, first + count):
                owner, at = 2 * depth + block // (2 * HALF), block % (2 * HALF)
                side, at = at // HALF, at % HALF
                places = [self.place(owner, side, head) for head in range(LINE)]
                steps.append(
                    [
                        (
                            [head for head in range(LINE) if places[head] == place],
                            self.plan[place].pieces(at),
                        )
                        for place in sorted(set(places))
                    ]
                )
        return Blocks(steps)

    def add_grads(self, depth, first, pieces):
        name = {QKV: "qkv", MLP: "mlp"}.get(first, "out") + str(depth)
        self.chains[name] = self.reduce(depth, first, pieces[:4], pieces[4])
        self.step([name])

    def reduce(self, depth, first_block, mine, theirs):
        count = mine[0].shape[0]
        first, second = along("first"), along("second")
        (core,) = yield [(theirs, along("core"))]
        far, to_two = ((mine[way].astype(F32) + core[way].astype(F32)).astype(BF) for way in (3, 2))
        far, two = yield [(far, second), (to_two, second)]
        to_one = (mine[1].astype(F32) + core[1].astype(F32) + far.astype(F32)).astype(BF)
        (one,) = yield [(to_one, first)]
        total = mine[0].astype(F32) + core[0].astype(F32) + one.astype(F32) + two.astype(F32)
        total = total.astype(BF)
        split = min(max(2 * HALF - first_block, 0), count)
        runs = [(side, low, high) for side, low, high in ((0, 0, split), (1, split, count)) if low < high]
        parts = [total[low:high] for _, low, high in runs]
        outer, inner, far_in, far_out = (0, 1, 2, 3) if depth == 0 else (3, 2, 1, 0)
        owners = [2 * depth + side for side, _, _ in runs]
        arrived = yield [
            (part, over((far_out, far_in), (outer if owner == inner else inner, owner)))
            for part, owner in zip(parts, owners)
        ]
        parts = [(part.astype(F32) + other.astype(F32)).astype(BF) for part, other in zip(parts, arrived)]
        arrived = yield [(part, over((far_in, owner))) for part, owner in zip(parts, owners)]
        for (_, low, high), part, other in zip(runs, parts, arrived):
            part = part.astype(F32) + other.astype(F32)
            for at in range(low, high):
                self.parts[depth, first_block + at] = (part, at - low)
        yield []

    def own_blocks(self, low, high):
        head = lax.axis_index("head")
        own = None
        for owner in range(LINE):
            runs = []
            for at in range(low, high):
                part, block = self.parts[owner // 2, 2 * HALF * (owner % 2) + at]
                if runs and runs[-1][0] is part:
                    runs[-1][2] = block + 1
                else:
                    runs.append([part, block, block + 1])
            values = [part[start:stop] for part, start, stop in runs]
            value = values[0] if len(values) == 1 else jnp.concatenate(values, axis=0)
            own = value if own is None else jnp.where(head == owner, value, own)
        return own

    def finish(self, renew):
        self.full = {}
        for low in (HALF, 0):
            self.chains[f"full{low}"] = self.gather_own(low)
        for group in LAST_STEPS:
            self.step(group)
        results = ()
        for low in (HALF, 0):
            own, full = self.full[low]
            if low == 0:
                results[0] = self.step(["full0"], results[0])
                self.step(["full0"])
            results = renew(
                self.next(own),
                Blocks([[(None, full.pieces(at))] for at in range(HALF)]),
                Blocks([[(None, self.right[low // HALF].pieces(at))] for at in range(HALF)]),
                low,
                results,
            )
        return results

    def gather_own(self, low):
        own = self.own_blocks(low, low + HALF)
        full = PlaneGather(own.astype(BF))
        self.full[low] = own, full
        yield from full.steps()

    def vector_sum(self, vectors):
        self.chains["sums"] = self.sum_vectors(vectors)
        return lambda: self.summed

    def sum_vectors(self, vectors):
        for axis in ("core", "x", "y"):
            (other,) = yield [(vectors, along(axis))]
            vectors = vectors + other
        for step in (1, 2):
            (other,) = yield [(vectors, over(*((i, i ^ step) for i in range(LINE))))]
            vectors = vectors + other
        self.summed = vectors
        yield []


def on_device(
    image_tokens,
    cotangent,
    weights,
    weights_ema,
    left_stats,
    right_stats,
    left_root,
    right_root,
    vectors,
    vec_first,
    vec_second,
):
    fits = lax.axis_size("dp") == DP and lax.axis_size("head") == LINE
    links = (Permutes if fits else Collectives)(weights, right_root)
    stream = pad_tokens(image_tokens)
    grad = pad_tokens(cotangent)
    saved = []
    top = LAYERS - 1
    for depth in range(LAYERS):
        ln_gain, gains, mlp_bias, out_bias = split_vector(vectors[depth])
        normed, qkv, unit, inverse = qkv_in(
            links.next(stream), ln_gain, gains, links.group((depth, QKV, 3))
        )
        qkv = links.done(f"qkv{depth}", qkv)
        attended = attend(links.next(qkv))
        attended = links.done(f"attend{depth}", attended)
        hidden, slope = mlp_in(links.next(normed), mlp_bias, links.group((depth, MLP, RATIO)))
        hidden = links.done(f"mlp{depth}", hidden)
        saved.append((stream, normed, hidden, slope, qkv, unit, inverse, attended))
        if depth == top:
            pieces = weight_grads(
                [(links.next(attended), grad, 1), ((hidden, 0), grad, RATIO)], links.cut, "grad_out"
            )
            pieces[0] = links.done(f"grad_out{depth}", pieces[0])
            links.add_grads(depth, OUT, pieces)
        stream = project(
            links.next(stream), attended, hidden, out_bias, links.group((depth, OUT, OUT_COUNT)), depth == top
        )
        stream = links.done(f"project{depth}", stream)
    block_out = cut_tokens(stream)
    vector_parts = [None] * LAYERS
    for depth in reversed(range(LAYERS)):
        ln_gain, gains, _, _ = split_vector(vectors[depth])
        stream, normed, hidden, slope, qkv, unit, inverse, attended = saved[depth]
        dy, do, du, dbo, dbu = mlp_back(links.next(grad), slope, links.group((depth, OUT, OUT_COUNT)))
        dy = links.done(f"mlp_back{depth}", dy)
        share = RATIO if depth == top else RATIO - 1
        if depth < top:
            segments = [(normed, (du, share), RATIO - share), (links.next(attended), dy, 1), ((hidden, 0), dy, RATIO)]
            pieces = weight_grads(segments, links.cut, "grad_out")
            pieces[0] = links.done(f"grad_out{depth}", pieces[0])
            links.add_grads(depth, MLP + share, pieces)
        pieces = weight_grads([(links.next(normed), (du, 0), share)], links.cut, "grad_mlp")
        pieces[0] = links.done(f"grad_mlp{depth}", pieces[0])
        links.add_grads(depth, MLP, pieces)
        dqkv, dgains = attend_back(links.next(do), qkv, unit, inverse, gains)
        dqkv = links.done(f"attend_back{depth}", dqkv)
        pieces = weight_grads([(links.next(normed), (dqkv, 0), 3)], links.cut, "grad_qkv")
        pieces[0] = links.done(f"grad_qkv{depth}", pieces[0])
        links.add_grads(depth, QKV, pieces)
        grad, dg = stream_back(
            links.next(grad), stream, ln_gain, du, dqkv, links.group((depth, MLP, RATIO), (depth, QKV, 3))
        )
        grad = links.done(f"stream_back{depth}", grad)
        vector_parts[depth] = jnp.concatenate(
            [
                dg[0],
                dgains.reshape(2, HEADS, HEAD_DIM).sum(1).reshape(-1),
                dbu[0],
                dbo[0],
            ]
        )
    grad_stream = cut_tokens(grad)
    vector_sum = links.vector_sum(jnp.stack(vector_parts))

    def renew(own, full, right, first, earlier):
        return shampoo(
            own, full, right, left_root, left_stats, right_stats, weights, weights_ema, first, earlier
        )

    weight_grad, left_new, right_new, weight_new, ema_new = links.finish(renew)
    vector_grad = vector_sum()
    first_new = BETA_ONE * vec_first + (1.0 - BETA_ONE) * vector_grad
    second_new = BETA_TWO * vec_second + (1.0 - BETA_TWO) * vector_grad * vector_grad
    first_hat = first_new / (1.0 - BETA_ONE**STEP)
    second_hat = second_new / (1.0 - BETA_TWO**STEP)
    vec_new = vectors - RATE_VEC * first_hat / (jnp.sqrt(second_hat) + ADAM_EPS)
    return (
        block_out,
        grad_stream,
        weight_grad,
        left_new,
        right_new,
        weight_new,
        ema_new,
        first_new,
        second_new,
        vec_new,
    )


def solution(mesh):
    tokens, blocks = P(("dp", "head"), None, None), P("head", "dp", None)
    return jax.shard_map(
        on_device,
        mesh=mesh,
        in_specs=(tokens, tokens) + (blocks,) * 6 + (P(),) * 3,
        out_specs=(tokens, tokens) + (blocks,) * 5 + (P(),) * 3,
        check_vma=False,
    )
```
